256 devices in a mesh: box: 8 (over z_lo, core), row: 32 (over z_hi, y, x).
Axes of the slice: x: 4, y: 4, z: 8 (z_hi: 2, z_lo: 4; z = z_hi * 4 + z_lo), core: 2. Of those that a mesh axis runs over, the one named last changes fastest.
Arguments:
- dtn: float32 [16, 6, 384, 2304], P('box', None, 'row'), may hold values from -2 to 8, as said below
- interface_perm: int32 [8, 384], P('box'), may hold values from 0 to 383, each once within a row
Outputs:
- solution_first: float32 [8, 384, 3840], P('box', 'row')
- solution_second: float32 [8, 384, 6144], P('box', 'row')
- merged_map: float32 [8, 8, 384, 6144], P('box', None, 'row')
The draws below stay inside these ranges and needn't reach their ends.
Inputs may be any that keep to these rules, and one draw needn't show every extreme that they name: `dtn`: each box's map, read as a (2304) x (2304) matrix, is symmetric and positive definite.
All inputs are finite; a program needn't handle non-finite values.
Results may differ from the reference program's by a relative error of at most 0.00012.
Values sent between devices are 32-bit elements; how exact they have to be, the bound alone decides.
No kernel may reach another device: no remote copies, remote signals or barrier semaphores. Data moves between devices by JAX's collectives and lax.ppermute only.
A program may use at most 192 MiB of HBM per device.

```python
import jax
import jax.numpy as jnp
from jax import lax

F = 384
NBOX = 16
NPAIR = 8


def one_map(key):
    order = 6 * F
    key_noise, key_scale = jax.random.split(key, 2)
    base_noise = jax.random.normal(key_noise, (order, order), jnp.float32)
    row_scale = 1.0 + 0.0 * jax.random.uniform(key_scale, (order,), jnp.float32)
    gram_matrix = jnp.dot(base_noise, base_noise.T, precision=lax.Precision.HIGHEST) / order
    gram_matrix = (gram_matrix + gram_matrix.T) * 0.5
    shifted = gram_matrix + 0.1 * jnp.eye(order, dtype=jnp.float32)
    scaled = row_scale[:, None] * shifted * row_scale[None, :]
    return scaled.reshape(6, F, order)


def draw_dtn(key, part):
    keys = jax.random.split(jax.random.fold_in(key, 11), NBOX)
    return jax.lax.map(one_map, keys)


def setup_inputs(seed: int = 0) -> dict:
    seeds = jax.random.split(jax.random.key(seed), 3)
    return {
        "dtn": draw_dtn(jax.random.fold_in(seeds[2], 71), 0),
        "interface_perm": jax.vmap(lambda own: jax.random.permutation(own, F))(jax.random.split(seeds[1], NPAIR)).reshape((NPAIR, F)).astype(jnp.int32),
    }


def face_index(faces, width):
    return jnp.concatenate([jnp.arange(width, dtype=jnp.int32) + f * width for f in faces])

def pick(matrix, rows, cols):
    return jnp.take(jnp.take(matrix, rows, axis=0), cols, axis=1)

def merge(left, right, left_s, left_o, right_s, right_o):
    couple = pick(left, left_s, left_s) + pick(right, right_s, right_s)
    coupled = jnp.concatenate([pick(left, left_s, left_o), pick(right, right_s, right_o)], axis=1)
    factor = jnp.linalg.cholesky(couple)
    solution = -jax.scipy.linalg.cho_solve((factor, True), coupled)
    n_left = left_o.shape[0]
    n_right = right_o.shape[0]
    top = jnp.concatenate([pick(left, left_o, left_o), jnp.zeros((n_left, n_right), jnp.float32)], axis=1)
    bottom = jnp.concatenate([jnp.zeros((n_right, n_left), jnp.float32), pick(right, right_o, right_o)], axis=1)
    lift = jnp.concatenate([pick(left, left_o, left_s), pick(right, right_o, right_s)], axis=0)
    merged = jnp.concatenate([top, bottom], axis=0) + jnp.dot(lift, solution, precision=lax.Precision.HIGHEST)
    return (solution, merged)

def reference(dtn, interface_perm):
    size = 6 * F
    firsts = []
    merged_one = []
    for p in range(NPAIR):
        first = dtn[2 * p].reshape(size, size)
        second = dtn[2 * p + 1].reshape(size, size)
        order = jnp.concatenate([interface_perm[p].astype(jnp.int32), jnp.arange(F, size, dtype=jnp.int32)])
        second = pick(second, order, order)
        solution, merged = merge(first, second, face_index([1], F), face_index([0, 2, 3, 4, 5], F), face_index([0], F), face_index([1, 2, 3, 4, 5], F))
        firsts.append(solution)
        merged_one.append(merged)
    seconds = []
    maps = []
    for c in range(NPAIR // 2):
        solution, merged = merge(merged_one[2 * c], merged_one[2 * c + 1], face_index([2, 7], F), face_index([0, 1, 3, 4, 5, 6, 8, 9], F), face_index([1, 6], F), face_index([0, 2, 3, 4, 5, 7, 8, 9], F))
        for h in range(2):
            seconds.append(solution[h * F:(h + 1) * F])
            maps.append(merged[h * 8 * F:(h + 1) * 8 * F].reshape(8, F, 16 * F))
    return (jnp.stack(firsts), jnp.stack(seconds), jnp.stack(maps))
```

```python
import functools

import jax
import jax.numpy as jnp
import numpy as np
from jax import lax
from jax.experimental import pallas as pl
from jax.experimental.pallas import tpu as pltpu
from jax.sharding import PartitionSpec as P

F = 384
N = 12
ROWS = 32
PLANE = 16
BF = jnp.bfloat16
F32 = jnp.float32
LIMIT = pltpu.CompilerParams(vmem_limit_bytes=56 * 1024 * 1024)
VMEM = pl.BlockSpec(memory_space=pltpu.VMEM)
SMEM = pl.BlockSpec(memory_space=pltpu.SMEM)


def call(kernel, outs, operands, smem=(), scratch=(), flops=10**9):
    return pl.pallas_call(
        kernel,
        out_shape=[jax.ShapeDtypeStruct(s, d) for s, d in outs],
        in_specs=[SMEM if i in smem else VMEM for i in range(len(operands))],
        out_specs=[VMEM] * len(outs),
        scratch_shapes=list(scratch),
        compiler_params=LIMIT,
        cost_estimate=pl.CostEstimate(flops=flops, bytes_accessed=10**6, transcendentals=0),
    )(*operands)


def dot(a, b):
    return jnp.dot(a, b, preferred_element_type=F32)


def dot_full(a, b):
    return jnp.dot(a, b, preferred_element_type=F32, precision=lax.Precision.HIGHEST)


def dot_full_t(a, b):
    return lax.dot_general(
        a, b, (((1,), (1,)), ((), ())), preferred_element_type=F32, precision=lax.Precision.HIGHEST
    )


def split(x, parts):
    out = []
    for _ in range(parts):
        top = x.astype(BF)
        out.append(top)
        x = x - top.astype(F32)
    return out


def iota(shape, dim):
    return lax.broadcasted_iota(jnp.int32, shape, dim)


def pack_kernel(sc, dtn, k1s, k2s, gs, x1, x2, dl):
    even = sc[0] == 0
    for b in range(2):
        i1 = 1 - b
        outer = (b, 2, 4, 5)
        cols_one = slice(i1 * F, (i1 + 1) * F)

        def second(rows):
            return jnp.where(even, rows[:, 3 * F : 4 * F], rows[:, 2 * F : 3 * F])

        def others(rows):
            return [
                rows[:, b * F : (b + 1) * F],
                jnp.where(even, rows[:, 2 * F : 3 * F], rows[:, 3 * F : 4 * F]),
                rows[:, 4 * F : 6 * F],
            ]

        row_one = dtn[b, i1]
        row_two = jnp.where(even, dtn[b, 3], dtn[b, 2])
        k1s[b * N : (b + 1) * N] = row_one[:, cols_one]
        k2s[2 * b * N : (2 * b + 1) * N] = row_two[:, cols_one]
        k2s[(2 * b + 1) * N : (2 * b + 2) * N] = second(row_two)
        for f, rows in enumerate((row_one, row_two)):
            at = 0
            for piece in others(rows):
                gs[b, f * N : (f + 1) * N, at : at + piece.shape[1]] = piece
                at += piece.shape[1]
        for k, face in enumerate(outer):
            rows = jnp.where(even, dtn[b, 2], dtn[b, 3]) if face == 2 else dtn[b, face]
            start = (4 * b + k) * N
            x1[start : start + N] = rows[:, cols_one]
            x2[start : start + N] = second(rows)
            at = 0
            for piece in others(rows):
                dl[b, k * N : (k + 1) * N, at : at + piece.shape[1]] = piece
                at += piece.shape[1]


def natural(dst, src, offset, base=0):
    for z in range(2):
        for q in range(PLANE):
            r = z * PLANE + q
            dst[base + r * N : base + (r + 1) * N] = src[q, z, offset : offset + N]


def scaled(k_ref, n):
    total = jnp.zeros((1, n), F32)
    cols = []
    for t in range(n // 128):
        rows = slice(t * 128, (t + 1) * 128)
        eye = iota((128, n), 0) + t * 128 == iota((128, n), 1)
        diag = jnp.where(eye, k_ref[rows], 0.0)
        total = total + jnp.sum(diag, axis=0, keepdims=True)
        cols.append(lax.rsqrt(jnp.sum(diag, axis=1, keepdims=True)))
    row = lax.rsqrt(total)
    norm = jnp.float32(0.0)
    peak = jnp.float32(0.0)
    for t in range(n // 128):
        rows = slice(t * 128, (t + 1) * 128)
        part = k_ref[rows] * cols[t] * row
        k_ref[rows] = part
        norm = norm + jnp.sum(part * part)
        peak = jnp.maximum(peak, jnp.max(jnp.sum(jnp.abs(part), axis=1, keepdims=True)))
    return row, cols, norm, peak


def solve_right(k_ref, v_ref, u_ref, x_ref, r_ref, xf_ref, rf_ref, n, norm, peak):
    tile = 256 if n % 256 == 0 else 128
    count = n // tile
    m = v_ref.shape[0]
    mtile = 128
    alpha = n / norm

    def eye(t, width):
        return (iota((width, n), 0) + t * width == iota((width, n), 1)).astype(F32)

    for t in range(count):
        rows = slice(t * tile, (t + 1) * tile)
        e = eye(t, tile)
        first = e - alpha * k_ref[rows]
        r_ref[0, rows] = first.astype(BF)
        x_ref[rows] = (alpha * (e + first)).astype(BF)

    def square(src, dst):
        def step(t, acc):
            rows = pl.ds(pl.multiple_of(t * tile, tile), tile)
            new = dot(r_ref[src, rows], r_ref[src])
            r_ref[dst, rows] = new.astype(BF)
            return acc + jnp.sum(new * new)

        return lax.fori_loop(0, count, step, jnp.float32(0.0))

    def advance(src):
        def step(t, carry):
            rows = pl.ds(pl.multiple_of(t * tile, tile), tile)
            old = x_ref[rows]
            x_ref[rows] = (old.astype(F32) + dot(old, r_ref[src])).astype(BF)
            return carry

        lax.fori_loop(0, count, step, 0)

    size = square(0, 1)

    def more(state):
        k, size = state
        return (size > 0.003 * n) & (k < 12)

    def iterate(state):
        k, _ = state
        src = (k + 1) % 2
        advance(src)
        return k + 1, square(src, k % 2)

    k, _ = lax.while_loop(more, iterate, (jnp.int32(0), size))
    advance((k + 1) % 2)

    def start(t, acc):
        rows = pl.ds(pl.multiple_of(t * mtile, mtile), mtile)
        v = v_ref[rows]
        u_ref[rows] = dot(v.astype(BF), x_ref[...])
        return acc + jnp.sum(v * v)

    scale = lax.fori_loop(0, m // mtile, start, jnp.float32(0.0))

    def refine(full):
        def step(t, acc):
            rows = pl.ds(pl.multiple_of(t * mtile, mtile), mtile)
            u = u_ref[rows]
            left = v_ref[rows] - dot_full(u, k_ref[...])
            if full:
                u_ref[rows] = u + dot_full(left, xf_ref[...])
            else:
                u_ref[rows] = u + dot(left.astype(BF), x_ref[...])
            return acc + jnp.sum(left * left)

        return lax.fori_loop(0, m // mtile, step, jnp.float32(0.0))

    def unfinished(state):
        k, left = state
        return (left > 1e-7 * scale) & (left < 0.1 * scale) & (k < 12)

    done, left = lax.while_loop(
        unfinished, lambda s: (s[0] + 1, refine(False)), (jnp.int32(1), refine(False))
    )

    @pl.when(jnp.logical_not(left <= 1e-7 * scale))
    def _():
        def rows_of(t):
            return pl.ds(pl.multiple_of(t * 128, 128), 128)

        def begin(t, carry):
            xf_ref[rows_of(t)] = eye(t, 128) / peak
            return carry

        lax.fori_loop(0, n // 128, begin, 0)

        def newton(state):
            k, _ = state

            def residual(t, acc):
                rows = rows_of(t)
                new = eye(t, 128) - dot_full(xf_ref[rows], k_ref[...])
                rf_ref[rows] = new
                return acc + jnp.sum(new * new)

            size = lax.fori_loop(0, n // 128, residual, jnp.float32(0.0))
            for t in range(n // 128):
                r_t = slice(t * 128, (t + 1) * 128)
                rf_ref[n + t * 128 : n + (t + 1) * 128] = xf_ref[r_t]

            def update(t, carry):
                rows = rows_of(t)
                xf_ref[rows] = xf_ref[rows] + dot_full(rf_ref[rows], rf_ref[n : 2 * n])
                return carry

            lax.fori_loop(0, n // 128, update, 0)
            return k + 1, size

        lax.while_loop(
            lambda s: (s[1] > 1e-5) & (s[0] < 80), newton, (jnp.int32(0), jnp.float32(1.0) * n)
        )

        def again(t, carry):
            rows = pl.ds(pl.multiple_of(t * mtile, mtile), mtile)
            u_ref[rows] = dot_full(v_ref[rows], xf_ref[...])
            return carry

        lax.fori_loop(0, m // mtile, again, 0)
        refine(True)
        refine(True)


def solve_scratch(n, m):
    return [
        pltpu.VMEM((n, n), F32),
        pltpu.VMEM((m, n), F32),
        pltpu.VMEM((m, n), F32),
        pltpu.VMEM((n, n), BF),
        pltpu.VMEM((2, n, n), BF),
        pltpu.VMEM((n, n), F32),
        pltpu.VMEM((2 * n, n), F32),
    ]


def permute_cols(x, perm_row):
    hot = (iota((F, F), 0) == perm_row).astype(BF)
    return sum(dot(part, hot) for part in split(x, 3))


def level_one_kernel(sc, kg, perm_col, perm_row, x1, inv, y1, f1, k, v, u, x, r, xf, rf):
    natural(v, kg, N)
    hot = (perm_col[...] == iota((F, F), 1)).astype(BF)
    turned = sum(dot(hot, part) for part in split(v[...], 3))
    u[...] = permute_cols(turned, perm_row[...])
    natural(k, kg, 0)
    k[...] = k[...] + u[...]
    row, cols, norm, peak = scaled(k, F)
    v[...] = (iota((F, F), 0) == iota((F, F), 1)).astype(F32)
    solve_right(k, v, u, x, r, xf, rf, F, norm, peak)
    for t in range(F // 128):
        rows = slice(t * 128, (t + 1) * 128)
        inv[rows] = u[rows] * cols[t] * row
    y1[:48] = dot_full(x1[:48], inv[...])
    y1[48:] = dot_full(permute_cols(x1[48:], perm_row[...]), inv[...])
    lane = iota((16, F), 1)
    sub = iota((16, F), 0)
    pick = ((lane == sub + sc[1] * N) & (sub < N)).astype(F32)
    f1[...] = dot_full(pick, inv[...])


def level_two_kernel(kg, perm_row, inv, x2, y1, f1, pv, wt, sf2, st):
    natural(st, kg, 0)
    natural(st, kg, 2 * N, F)
    st[F:] = permute_cols(st[F:], perm_row[...])
    natural(wt, kg, N)
    natural(wt, kg, 3 * N, F)
    for t in range(6):
        rows = slice(t * 128, (t + 1) * 128)
        base = wt[rows]
        w = dot_full(st[rows], inv[...])
        wt[rows] = w
        part = -dot_full_t(w, st[...])
        own = slice(0, F) if t < 3 else slice(F, 2 * F)
        other = slice(F, 2 * F) if t < 3 else slice(0, F)
        pv[rows, own] = part[:, own] + base
        pv[rows, other] = part[:, other]
    part = -dot_full_t(y1[...], st[...])
    pv[768:816, :F] = part[:48, :F] + x2[:48]
    pv[768:816, F:] = part[:48, F:]
    pv[816:864, :F] = part[48:, :F]
    pv[816:864, F:] = part[48:, F:] + x2[48:]
    sf2[...] = -dot_full_t(f1[...], st[...])


def couple_kernel(sc, pv, other, wt, y1, f1, key, target, ch, cl, k, v, u, x, r, xf, rf):
    n = 2 * F
    for t in range(6):
        rows = slice(t * 128, (t + 1) * 128)
        k[rows] = pv[rows] + other[rows]
    row, _, norm, peak = scaled(k, n)
    lane = iota((16, n), 1)
    sub = iota((16, n), 0)
    for h, source in enumerate((pv, other)):
        half = sc[0] if h == 0 else 1 - sc[0]
        pick = ((lane == half * F + sc[1] * N + sub) & (sub < N)).astype(F32)
        base = h * 128
        v[base : base + 96] = source[n : n + 96] * row
        v[base + 96 : base + 112] = pick * row
        v[base + 112 : base + 128] = jnp.zeros((16, n), F32)
    solve_right(k, v, u, x, r, xf, rf, n, norm, peak)
    for t in range(2):
        rows = slice(t * 128, (t + 1) * 128)
        u2 = u[rows] * row
        u[rows] = -u2
        k[rows, :F] = dot_full(u2, wt[...])
    k[:96, :F] = k[:96, :F] - y1[...]
    k[108:120, :F] = k[108:120, :F] - f1[:N]
    lanes = target[...]
    for b in range(2):
        keys = iota((n, 1), 0) if b == 0 else key[...]
        hot = (keys == lanes).astype(BF)
        for t in range(2):
            rows = slice(t * 128, (t + 1) * 128)
            coef = jnp.concatenate([k[rows, :F], u[rows, b * F : (b + 1) * F]], axis=1)
            high, low = split(coef, 2)
            ch[b, rows] = dot(high, hot).astype(BF)
            cl[b, rows] = dot(low, hot).astype(BF)


WIDE = 512


def product_kernel(ch, cl, g, dl, own, part):
    block = g[...].reshape(2 * F, WIDE)
    high, low = split(block, 2)
    acc = dot(ch[0], high) + (dot(ch[0], low) + dot(cl[0], high))
    own[...] = acc[:128]
    part[...] = acc[128:240]
    for b in range(2):
        @pl.when(pl.program_id(0) == b)
        def _():
            own[48 * b : 48 * (b + 1)] = acc[48 * b : 48 * (b + 1)] + dl[0]


def product(ch, cl, g, dl):
    steps = 4 * F // WIDE
    coef = pl.BlockSpec((1, 256, 2 * F), lambda b, j: (b, 0, 0))
    return pl.pallas_call(
        product_kernel,
        grid=(2, steps),
        in_specs=[
            coef,
            coef,
            pl.BlockSpec((ROWS, 1, 2 * N, WIDE), lambda b, j: (0, b, 0, j)),
            pl.BlockSpec((1, 4 * N, WIDE), lambda b, j: (b, 0, j)),
        ],
        out_specs=[
            pl.BlockSpec((128, WIDE), lambda b, j: (0, b * steps + j)),
            pl.BlockSpec((112, WIDE), lambda b, j: (0, b * steps + j)),
        ],
        out_shape=[
            jax.ShapeDtypeStruct((128, 8 * F), F32),
            jax.ShapeDtypeStruct((112, 8 * F), F32),
        ],
        compiler_params=LIMIT,
        cost_estimate=pl.CostEstimate(flops=4 * 10**9, bytes_accessed=10**7, transcendentals=0),
    )(ch, cl, g, dl)


def finish_kernel(sc, own, other, sf2, sf, ss, mm):
    wide = 8 * F
    for h in range(2):
        @pl.when(sc[0] == h)
        def _():
            near = slice(h * wide, (h + 1) * wide)
            far = slice((1 - h) * wide, (2 - h) * wide)
            for s in range(8):
                mm[0, s, :, near] = own[s * N : (s + 1) * N]
                mm[0, s, :, far] = other[s * N : (s + 1) * N]
            ss[0, :, near] = own[96:108]
            ss[0, :, far] = other[96:108]
            for b in range(2):
                at = 5 * b * F
                left = 4 * b * F
                sf[0, :, at : at + F] = own[108:120, left : left + F]
                outer, inner = (at + F, at + 2 * F) if h == 0 else (at + 2 * F, at + F)
                sf[0, :, outer : outer + F] = own[108:120, left + F : left + 2 * F]
                sf[0, :, inner : inner + F] = sf2[:N, b * F : (b + 1) * F]
                sf[0, :, at + 3 * F : at + 5 * F] = own[108:120, left + 2 * F : left + 4 * F]


def swap(x, axis, bit):
    return lax.ppermute(x, axis, [(i, i ^ bit) for i in range(lax.axis_size(axis))])


GROUPS = [list(range(z * PLANE, (z + 1) * PLANE)) for z in range(2)]


def both_planes(x):
    other = swap(x, "row", PLANE)
    low = lax.axis_index("row") < PLANE
    return jnp.stack([jnp.where(low, x, other), jnp.where(low, other, x)])


def gather_plane(x):
    spread = jnp.broadcast_to(x[None], (PLANE,) + x.shape)
    return lax.all_to_all(spread, "row", 0, 0, axis_index_groups=GROUPS)


def body(dtn, interface_perm):
    half = lax.axis_index("box") % 2
    row = lax.axis_index("row")
    sc = jnp.stack([half, row]).astype(jnp.int32)
    perm_row = interface_perm
    perm_col = interface_perm.reshape(F, 1)
    k1s, k2s, gs, x1, x2, dl = call(
        pack_kernel,
        [
            ((2 * N, F), F32),
            ((4 * N, F), F32),
            ((2, 2 * N, 4 * F), F32),
            ((8 * N, F), F32),
            ((8 * N, F), F32),
            ((2, 4 * N, 4 * F), F32),
        ],
        (sc, dtn),
        smem=(0,),
    )
    k1g = gather_plane(both_planes(k1s))
    k2g = gather_plane(both_planes(k2s))
    g = lax.all_gather(both_planes(gs), "row", axis_index_groups=GROUPS)
    g = g.reshape(ROWS, 2, 2 * N, 4 * F)
    inv, y1, f1 = call(
        level_one_kernel,
        [((F, F), F32), ((8 * N, F), F32), ((16, F), F32)],
        (sc, k1g, perm_col, perm_row, x1),
        smem=(0,),
        scratch=solve_scratch(F, F),
        flops=10 * 10**9,
    )
    pv, wt, sf2 = call(
        level_two_kernel,
        [((864, 2 * F), F32), ((2 * F, F), F32), ((16, 2 * F), F32)],
        (k2g, perm_row, inv, x2, y1, f1),
        scratch=[pltpu.VMEM((2 * F, F), F32)],
        flops=5 * 10**9,
    )
    other = swap(pv, "box", 1)
    natural_row = np.arange(F).reshape(2, PLANE, N).transpose(1, 0, 2)
    target = np.stack([natural_row, natural_row + F], axis=2).reshape(1, 2 * F)
    key = jnp.concatenate([perm_col, F + iota((F, 1), 0)], axis=0)
    ch, cl = call(
        couple_kernel,
        [((2, 256, 2 * F), BF), ((2, 256, 2 * F), BF)],
        (sc, pv, other, wt, y1, f1, key, jnp.asarray(target, jnp.int32)),
        smem=(0,),
        scratch=solve_scratch(2 * F, 256),
        flops=20 * 10**9,
    )
    own, part = product(ch, cl, g, dl)
    arrived = swap(part, "box", 1)
    return tuple(
        call(
            finish_kernel,
            [((1, N, 10 * F), F32), ((1, N, 16 * F), F32), ((1, 8, N, 16 * F), F32)],
            (sc, own, arrived, sf2),
            smem=(0,),
        )
    )


def solution(mesh):
    return jax.shard_map(
        body,
        mesh=mesh,
        in_specs=(P("box", None, "row", None), P("box", None)),
        out_specs=(P("box", "row", None), P("box", "row", None), P("box", None, "row", None)),
        check_vma=False,
    )
```

```python
import functools

import jax
import jax.numpy as jnp
import numpy as np
from jax import lax
from jax.experimental import pallas as pl
from jax.experimental.pallas import tpu as pltpu
from jax.sharding import PartitionSpec as P

F = 384
N = 12
ROWS = 32
PLANE = 16
BF = jnp.bfloat16
F32 = jnp.float32
LIMIT = pltpu.CompilerParams(vmem_limit_bytes=56 * 1024 * 1024)
VMEM = pl.BlockSpec(memory_space=pltpu.VMEM)
SMEM = pl.BlockSpec(memory_space=pltpu.SMEM)


def call(kernel, outs, operands, smem=(), scratch=(), flops=10**9):
    return pl.pallas_call(
        kernel,
        out_shape=[jax.ShapeDtypeStruct(s, d) for s, d in outs],
        in_specs=[SMEM if i in smem else VMEM for i in range(len(operands))],
        out_specs=[VMEM] * len(outs),
        scratch_shapes=list(scratch),
        compiler_params=LIMIT,
        cost_estimate=pl.CostEstimate(flops=flops, bytes_accessed=10**6, transcendentals=0),
    )(*operands)


def dot(a, b):
    return jnp.dot(a, b, preferred_element_type=F32)


def dot_full(a, b):
    return jnp.dot(a, b, preferred_element_type=F32, precision=lax.Precision.HIGHEST)


def dot_t(a, b):
    return lax.dot_general(a, b, (((1,), (1,)), ((), ())), preferred_element_type=F32)


def dot_three(a, b, kernel=dot):
    (ah, al), (bh, bl) = a, b
    return kernel(ah, bh) + (kernel(ah, bl) + kernel(al, bh))


def split(x, parts):
    out = []
    for _ in range(parts):
        top = x.astype(BF)
        out.append(top)
        x = x - top.astype(F32)
    return out


def iota(shape, dim):
    return lax.broadcasted_iota(jnp.int32, shape, dim)


def pack_kernel(sc, dtn, ks, gs, x1, x2, dl):
    even = sc[0] == 0
    empty = jnp.zeros((4, 4 * F), F32)
    for i in range(N):
        one, two, block = [], [], []
        for b in range(2):
            i1 = 1 - b
            def second(rows):
                return jnp.where(even, rows[:, 3 * F : 4 * F], rows[:, 2 * F : 3 * F])

            def others(rows):
                mid = jnp.where(even, rows[:, 2 * F : 3 * F], rows[:, 3 * F : 4 * F])
                return jnp.concatenate([rows[:, b * F : (b + 1) * F], mid, rows[:, 4 * F :]], axis=1)

            face = [dtn[f, i, b : b + 1] for f in range(6)]
            row_one = face[i1]
            row_two = jnp.where(even, face[3], face[2])
            middle = jnp.where(even, face[2], face[3])
            outer = jnp.concatenate([face[b], middle, face[4], face[5]], axis=0)
            cols = slice(i1 * F, (i1 + 1) * F)
            ks[b * N + i : b * N + i + 1] = row_one[:, cols]
            at = 2 * (b + 1) * N + i
            ks[at : at + 1] = row_two[:, cols]
            ks[at + N : at + N + 1] = second(row_two)
            gs[b, i : i + 1] = others(row_one)
            gs[b, N + i : N + i + 1] = others(row_two)
            one.append(outer[:, cols])
            two.append(second(outer))
            block.append(others(outer))
        rows = slice(8 * i, 8 * i + 8)
        x1[rows] = jnp.concatenate(one, axis=0)
        x2[rows] = jnp.concatenate(two, axis=0)
        dl[rows, : 4 * F] = jnp.concatenate([block[0], empty], axis=0)
        dl[rows, 4 * F :] = jnp.concatenate([empty, block[1]], axis=0)


def natural(dst, src, offset, base=0):
    for z in range(2):
        for q in range(PLANE):
            r = z * PLANE + q
            dst[base + r * N : base + (r + 1) * N] = src[q, z, offset : offset + N]


def scaled(k_ref, n):
    total = jnp.zeros((1, n), F32)
    cols = []
    for t in range(n // 128):
        rows = slice(t * 128, (t + 1) * 128)
        eye = iota((128, n), 0) + t * 128 == iota((128, n), 1)
        diag = jnp.where(eye, k_ref[rows], 0.0)
        total = total + jnp.sum(diag, axis=0, keepdims=True)
        cols.append(lax.rsqrt(jnp.sum(diag, axis=1, keepdims=True)))
    row = lax.rsqrt(total)
    norm = jnp.float32(0.0)
    peak = jnp.float32(0.0)
    for t in range(n // 128):
        rows = slice(t * 128, (t + 1) * 128)
        part = k_ref[rows] * cols[t] * row
        k_ref[rows] = part
        norm = norm + jnp.sum(part * part)
        peak = jnp.maximum(peak, jnp.max(jnp.sum(jnp.abs(part), axis=1, keepdims=True)))
    return row, cols, norm, peak


TILE = 384
MTILE = 384


def solve_right(k_ref, v_ref, u_ref, x_ref, r_ref, xf_ref, rf_ref, kh_ref, kl_ref, n, norm, peak):
    tile = TILE
    count = n // tile
    m = v_ref.shape[0]
    mtile = min(m, MTILE)
    alpha = n / norm

    def eye(t, width):
        return (iota((width, n), 0) + t * width == iota((width, n), 1)).astype(F32)

    for t in range(count):
        rows = slice(t * tile, (t + 1) * tile)
        e = eye(t, tile)
        kh_ref[rows], kl_ref[rows] = split(k_ref[rows], 2)
        first = e - alpha * k_ref[rows]
        r_ref[0, rows] = first.astype(BF)
        x_ref[rows] = (alpha * (e + first)).astype(BF)

    def square(src, dst):
        def step(t, acc):
            rows = pl.ds(pl.multiple_of(t * tile, tile), tile)
            new = dot(r_ref[src, rows], r_ref[src])
            r_ref[dst, rows] = new.astype(BF)
            return acc + jnp.sum(new * new)

        return lax.fori_loop(0, count, step, jnp.float32(0.0))

    def advance(src):
        def step(t, carry):
            rows = pl.ds(pl.multiple_of(t * tile, tile), tile)
            old = x_ref[rows]
            x_ref[rows] = (old.astype(F32) + dot(old, r_ref[src])).astype(BF)
            return carry

        lax.fori_loop(0, count, step, 0)

    size = square(0, 1)

    def more(state):
        k, size = state
        return (size > 0.003 * n) & (k < 12)

    def iterate(state):
        k, _ = state
        src = (k + 1) % 2
        advance(src)
        return k + 1, square(src, k % 2)

    k, _ = lax.while_loop(more, iterate, (jnp.int32(0), size))
    advance((k + 1) % 2)

    def start(t, acc):
        rows = pl.ds(pl.multiple_of(t * mtile, mtile), mtile)
        v = v_ref[rows]
        u_ref[rows] = dot(v.astype(BF), x_ref[...])
        return acc + jnp.sum(v * v)

    scale = lax.fori_loop(0, m // mtile, start, jnp.float32(0.0))

    def refine(full):
        def step(t, acc):
            rows = pl.ds(pl.multiple_of(t * mtile, mtile), mtile)
            u = u_ref[rows]
            if full:
                left = v_ref[rows] - dot_full(u, k_ref[...])
                u_ref[rows] = u + dot_full(left, xf_ref[...])
            else:
                left = v_ref[rows] - dot_three(split(u, 2), (kh_ref[...], kl_ref[...]))
                u_ref[rows] = u + dot(left.astype(BF), x_ref[...])
            return acc + jnp.sum(left * left)

        return lax.fori_loop(0, m // mtile, step, jnp.float32(0.0))

    def unfinished(state):
        k, left = state
        return (left > 1e-7 * scale) & (left < 0.1 * scale) & (k < 12)

    done, left = lax.while_loop(
        unfinished, lambda s: (s[0] + 1, refine(False)), (jnp.int32(1), refine(False))
    )

    @pl.when(jnp.logical_not(left <= 1e-7 * scale))
    def _():
        def rows_of(t):
            return pl.ds(pl.multiple_of(t * 128, 128), 128)

        def begin(t, carry):
            xf_ref[rows_of(t)] = eye(t, 128) / peak
            return carry

        lax.fori_loop(0, n // 128, begin, 0)

        def newton(state):
            k, _ = state

            def residual(t, acc):
                rows = rows_of(t)
                new = eye(t, 128) - dot_full(xf_ref[rows], k_ref[...])
                rf_ref[rows] = new
                return acc + jnp.sum(new * new)

            size = lax.fori_loop(0, n // 128, residual, jnp.float32(0.0))
            for t in range(n // 128):
                r_t = slice(t * 128, (t + 1) * 128)
                rf_ref[n + t * 128 : n + (t + 1) * 128] = xf_ref[r_t]

            def update(t, carry):
                rows = rows_of(t)
                xf_ref[rows] = xf_ref[rows] + dot_full(rf_ref[rows], rf_ref[n : 2 * n])
                return carry

            lax.fori_loop(0, n // 128, update, 0)
            return k + 1, size

        lax.while_loop(
            lambda s: (s[1] > 1e-5) & (s[0] < 80), newton, (jnp.int32(0), jnp.float32(1.0) * n)
        )

        def again(t, carry):
            rows = pl.ds(pl.multiple_of(t * mtile, mtile), mtile)
            u_ref[rows] = dot_full(v_ref[rows], xf_ref[...])
            return carry

        lax.fori_loop(0, m // mtile, again, 0)
        refine(True)
        refine(True)


def solve_scratch(n, m):
    return [
        pltpu.VMEM((n, n), F32),
        pltpu.VMEM((m, n), F32),
        pltpu.VMEM((m, n), F32),
        pltpu.VMEM((n, n), BF),
        pltpu.VMEM((2, n, n), BF),
        pltpu.VMEM((n, n), F32),
        pltpu.VMEM((2 * n, n), F32),
        pltpu.VMEM((n, n), BF),
        pltpu.VMEM((n, n), BF),
    ]


def column(row):
    eye = iota((F, F), 0) == iota((F, F), 1)
    spread = jnp.where(eye, row.astype(F32), 0.0)
    return jnp.sum(spread, axis=1, keepdims=True).astype(jnp.int32)


def permute_cols(x, perm_row):
    hot = (iota((F, F), 0) == perm_row).astype(BF)
    return sum(dot(part, hot) for part in split(x, 3))


def from_second(rows):
    return (iota((rows, 1), 0) & 7) >= 4


def level_one_kernel(sc, kg, perm_row, x1, inv, y1, f1, k, v, u, x, r, xf, rf, kh, kl):
    natural(v, kg, N)
    hot = (column(perm_row[...]) == iota((F, F), 1)).astype(BF)
    turned = sum(dot(hot, part) for part in split(v[...], 3))
    u[...] = permute_cols(turned, perm_row[...])
    natural(k, kg, 0)
    k[...] = k[...] + u[...]
    row, cols, norm, peak = scaled(k, F)
    v[...] = (iota((F, F), 0) == iota((F, F), 1)).astype(F32)
    solve_right(k, v, u, x, r, xf, rf, kh, kl, F, norm, peak)
    for t in range(F // 128):
        rows = slice(t * 128, (t + 1) * 128)
        inv[rows] = u[rows] * cols[t] * row
    inverse = split(inv[...], 2)
    points = x1[...]
    points = jnp.where(from_second(8 * N), permute_cols(points, perm_row[...]), points)
    y1[...] = dot_three(split(points, 2), inverse)
    lane = iota((16, F), 1)
    sub = iota((16, F), 0)
    pick = ((lane == sub + sc[1] * N) & (sub < N)).astype(BF)
    f1[...] = sum(dot(pick, part) for part in split(inv[...], 3))


def level_two_kernel(kg, perm_row, inv, x2, y1, f1, pv, wt, sf2, st):
    natural(st, kg, 0)
    natural(st, kg, 2 * N, F)
    st[F:] = permute_cols(st[F:], perm_row[...])
    natural(wt, kg, N)
    natural(wt, kg, 3 * N, F)
    inverse = split(inv[...], 2)
    second = split(st[...], 2)
    for t in range(2):
        rows = slice(t * F, (t + 1) * F)
        other = slice((1 - t) * F, (2 - t) * F)
        base = wt[rows]
        w = dot_three([part[rows] for part in second], inverse)
        wt[rows] = w
        part = dot_three(split(w, 2), second, dot_t)
        pv[rows, rows] = base - part[:, rows]
        pv[rows, other] = -part[:, other]
    part = dot_three(split(y1[...], 2), second, dot_t)
    late = from_second(8 * N)
    n = 2 * F
    pv[n : n + 96, :F] = jnp.where(late, 0.0, x2[...]) - part[:, :F]
    pv[n : n + 96, F:] = jnp.where(late, x2[...], 0.0) - part[:, F:]
    sf2[...] = -dot_three(split(f1[...], 2), second, dot_t)


def couple_kernel(sc, pv, other, wt, y1, f1, perm_row, target, ch, cl, k, v, u, x, r, xf, rf, kh, kl):
    n = 2 * F
    for t in range(6):
        rows = slice(t * 128, (t + 1) * 128)
        k[rows] = pv[rows] + other[rows]
    row, _, norm, peak = scaled(k, n)
    lane = iota((16, n), 1)
    sub = iota((16, n), 0)
    for h, source in enumerate((pv, other)):
        half = sc[0] if h == 0 else 1 - sc[0]
        pick = ((lane == half * F + sc[1] * N + sub) & (sub < N)).astype(F32)
        base = h * 128
        v[base : base + 96] = source[n : n + 96] * row
        v[base + 96 : base + 112] = pick * row
        v[base + 112 : base + 128] = jnp.zeros((16, n), F32)
    solve_right(k, v, u, x, r, xf, rf, kh, kl, n, norm, peak)
    u2 = u[...] * row
    u[...] = -u2
    k[:256, :F] = dot_three(split(u2, 2), split(wt[...], 2))
    k[:96, :F] = k[:96, :F] - y1[...]
    k[108:120, :F] = k[108:120, :F] - f1[:N]
    lanes = target[...]
    for b in range(2):
        keys = iota((n, 1), 0)
        if b == 1:
            keys = jnp.concatenate([column(perm_row[...]), keys[F:]], axis=0)
        hot = (keys == lanes).astype(BF)
        coef = jnp.concatenate([k[:256, :F], u[:, b * F : (b + 1) * F]], axis=1)
        high, low = split(coef, 2)
        ch[b] = dot(high, hot).astype(BF)
        cl[b] = dot(low, hot).astype(BF)


WIDE = 512


def product_kernel(ch, cl, g, dl, own, part):
    block = g[...].reshape(2 * F, WIDE)
    acc = dot_three((ch[0], cl[0]), split(block, 2))
    own[:96] = acc[:96] + dl[...]
    own[96:] = acc[96:128]
    part[...] = acc[128:240]


def product(b, ch, cl, g, dl):
    steps = 4 * F // WIDE
    coef = pl.BlockSpec((1, 256, 2 * F), lambda j: (b, 0, 0))
    return pl.pallas_call(
        product_kernel,
        grid=(steps,),
        in_specs=[
            coef,
            coef,
            pl.BlockSpec((ROWS, 1, 2 * N, WIDE), lambda j: (0, b, 0, j)),
            pl.BlockSpec((8 * N, WIDE), lambda j: (0, b * steps + j)),
        ],
        out_specs=[
            pl.BlockSpec((128, WIDE), lambda j: (0, j)),
            pl.BlockSpec((112, WIDE), lambda j: (0, j)),
        ],
        out_shape=[
            jax.ShapeDtypeStruct((128, 4 * F), F32),
            jax.ShapeDtypeStruct((112, 4 * F), F32),
        ],
        compiler_params=LIMIT,
        cost_estimate=pl.CostEstimate(flops=4 * 10**9, bytes_accessed=10**7, transcendentals=0),
    )(ch, cl, g, dl)


def finish_kernel(sc, own_a, own_b, other_a, other_b, sf2, sf, ss, mm):
    wide = 4 * F
    for h in range(2):
        @pl.when(sc[0] == h)
        def _():
            for b, (own, other) in enumerate(((own_a, other_a), (own_b, other_b))):
                near = slice((2 * h + b) * wide, (2 * h + b + 1) * wide)
                far = slice((2 - 2 * h + b) * wide, (3 - 2 * h + b) * wide)
                for i in range(N):
                    mm[i, :, near] = own[8 * i : 8 * i + 8]
                    mm[i, :, far] = other[8 * i : 8 * i + 8]
                    ss[i, :, near] = own[96 + i : 97 + i]
                    ss[i, :, far] = other[96 + i : 97 + i]
                    row = own[108 + i : 109 + i]
                    at = 5 * b * F
                    sf[i, :, at : at + F] = row[:, :F]
                    outer, inner = (at + F, at + 2 * F) if h == 0 else (at + 2 * F, at + F)
                    sf[i, :, outer : outer + F] = row[:, F : 2 * F]
                    sf[i, :, inner : inner + F] = sf2[i : i + 1, b * F : (b + 1) * F]
                    sf[i, :, at + 3 * F : at + 5 * F] = row[:, 2 * F :]


def swap(x, axis, bit):
    return lax.ppermute(x, axis, [(i, i ^ bit) for i in range(lax.axis_size(axis))])


GROUPS = [list(range(z * PLANE, (z + 1) * PLANE)) for z in range(2)]


def both_planes(x):
    other = swap(x, "row", PLANE)
    low = lax.axis_index("row") < PLANE
    return jnp.stack([jnp.where(low, x, other), jnp.where(low, other, x)])


def gather_plane(x):
    spread = jnp.broadcast_to(x[None], (PLANE,) + x.shape)
    return lax.all_to_all(spread, "row", 0, 0, axis_index_groups=GROUPS)


def body(dtn, interface_perm):
    half = lax.axis_index("box") % 2
    row = lax.axis_index("row")
    sc = jnp.stack([half, row]).astype(jnp.int32)
    perm_row = interface_perm
    ks, gs, x1, x2, dl = pack(sc, dtn.transpose(1, 2, 0, 3))
    gz = both_planes(gs)
    kz = both_planes(ks)
    k1g = gather_plane(kz[:, : 2 * N])
    k2g = gather_plane(kz[:, 2 * N :])
    g = lax.all_gather(gz, "row", axis_index_groups=GROUPS)
    g = g.reshape(ROWS, 2, 2 * N, 4 * F)
    inv, y1, f1 = level_one(sc, k1g, perm_row, x1)
    pv, wt, sf2 = level_two(k2g, perm_row, inv, x2, y1, f1)
    other = swap(pv, "box", 1)
    ch, cl = couple(sc, pv, other, wt, y1, f1, perm_row)
    own_a, part_a = product(0, ch, cl, g, dl)
    arrived_a = swap(part_a, "box", 1)
    own_b, part_b = product(1, ch, cl, g, dl)
    arrived_b = swap(part_b, "box", 1)
    sf, ss, mm = finish(sc, own_a, own_b, arrived_a, arrived_b, sf2)
    return sf.transpose(1, 0, 2), ss.transpose(1, 0, 2), mm[None].transpose(0, 2, 1, 3)


def pack(*operands):
    return call(
        pack_kernel,
        [
            ((6 * N, F), F32),
            ((2, 2 * N, 4 * F), F32),
            ((8 * N, F), F32),
            ((8 * N, F), F32),
            ((8 * N, 8 * F), F32),
        ],
        operands,
        smem=(0,),
    )


def level_one(*operands):
    return call(
        level_one_kernel,
        [((F, F), F32), ((8 * N, F), F32), ((16, F), F32)],
        operands,
        smem=(0,),
        scratch=solve_scratch(F, F),
        flops=10 * 10**9,
    )


def level_two(*operands):
    return call(
        level_two_kernel,
        [((864, 2 * F), F32), ((2 * F, F), F32), ((16, 2 * F), F32)],
        operands,
        scratch=[pltpu.VMEM((2 * F, F), F32)],
        flops=5 * 10**9,
    )


def couple(*operands):
    natural_row = np.arange(F).reshape(2, PLANE, N).transpose(1, 0, 2)
    target = np.stack([natural_row, natural_row + F], axis=2).reshape(1, 2 * F)
    return call(
        couple_kernel,
        [((2, 256, 2 * F), BF), ((2, 256, 2 * F), BF)],
        operands + (jnp.asarray(target, jnp.int32),),
        smem=(0,),
        scratch=solve_scratch(2 * F, 256),
        flops=20 * 10**9,
    )


def finish(*operands):
    return call(
        finish_kernel,
        [((N, 1, 10 * F), F32), ((N, 1, 16 * F), F32), ((N, 8, 16 * F), F32)],
        operands,
        smem=(0,),
    )


def solution(mesh):
    return jax.shard_map(
        body,
        mesh=mesh,
        in_specs=(P("box", None, "row", None), P("box", None)),
        out_specs=(P("box", "row", None), P("box", "row", None), P("box", None, "row", None)),
        check_vma=False,
    )
```

```python
import functools

import jax
import jax.numpy as jnp
import numpy as np
from jax import lax
from jax.experimental import pallas as pl
from jax.experimental.pallas import tpu as pltpu
from jax.sharding import PartitionSpec as P

F = 384
N = 12
ROWS = 32
PLANE = 16
BF = jnp.bfloat16
F32 = jnp.float32
LIMIT = pltpu.CompilerParams(vmem_limit_bytes=56 * 1024 * 1024)
VMEM = pl.BlockSpec(memory_space=pltpu.VMEM)
SMEM = pl.BlockSpec(memory_space=pltpu.SMEM)


def call(kernel, outs, operands, smem=(), scratch=(), flops=10**9):
    return pl.pallas_call(
        kernel,
        out_shape=[jax.ShapeDtypeStruct(s, d) for s, d in outs],
        in_specs=[SMEM if i in smem else VMEM for i in range(len(operands))],
        out_specs=[VMEM] * len(outs),
        scratch_shapes=list(scratch),
        compiler_params=LIMIT,
        cost_estimate=pl.CostEstimate(flops=flops, bytes_accessed=10**6, transcendentals=0),
    )(*operands)


def dot(a, b):
    return jnp.dot(a, b, preferred_element_type=F32)


def dot_full(a, b):
    return jnp.dot(a, b, preferred_element_type=F32, precision=lax.Precision.HIGHEST)


def dot_t(a, b):
    return lax.dot_general(a, b, (((1,), (1,)), ((), ())), preferred_element_type=F32)


def dot_three(a, b, kernel=dot):
    (ah, al), (bh, bl) = a, b
    return kernel(ah, bh) + (kernel(ah, bl) + kernel(al, bh))


def split(x, parts):
    out = []
    for _ in range(parts):
        top = x.astype(BF)
        out.append(top)
        x = x - top.astype(F32)
    return out


def iota(shape, dim):
    return lax.broadcasted_iota(jnp.int32, shape, dim)


def pack_kernel(sc, dtn, ks, gs, x1, x2, dl):
    even = sc[0] == 0
    empty = jnp.zeros((4, 4 * F), F32)
    for i in range(N):
        one, two, block = [], [], []
        for b in range(2):
            i1 = 1 - b
            def second(rows):
                return jnp.where(even, rows[:, 3 * F : 4 * F], rows[:, 2 * F : 3 * F])

            def others(rows):
                mid = jnp.where(even, rows[:, 2 * F : 3 * F], rows[:, 3 * F : 4 * F])
                return jnp.concatenate([rows[:, b * F : (b + 1) * F], mid, rows[:, 4 * F :]], axis=1)

            face = [dtn[f, i, b : b + 1] for f in range(6)]
            row_one = face[i1]
            row_two = jnp.where(even, face[3], face[2])
            middle = jnp.where(even, face[2], face[3])
            outer = jnp.concatenate([face[b], middle, face[4], face[5]], axis=0)
            cols = slice(i1 * F, (i1 + 1) * F)
            ks[b * N + i : b * N + i + 1] = row_one[:, cols]
            at = 2 * (b + 1) * N + i
            ks[at : at + 1] = row_two[:, cols]
            ks[at + N : at + N + 1] = second(row_two)
            gs[b, i : i + 1] = others(row_one)
            gs[b, N + i : N + i + 1] = others(row_two)
            one.append(outer[:, cols])
            two.append(second(outer))
            block.append(others(outer))
        rows = slice(8 * i, 8 * i + 8)
        x1[rows] = jnp.concatenate(one, axis=0)
        x2[rows] = jnp.concatenate(two, axis=0)
        dl[rows, : 4 * F] = jnp.concatenate([block[0], empty], axis=0)
        dl[rows, 4 * F :] = jnp.concatenate([empty, block[1]], axis=0)


def place(distance):
    return jnp.where(distance == 0, 0, jnp.where(distance == 3, 1, distance + 1))


def natural(dst, src, sc, offset, base=0):
    ys = [place((y + 4 - sc[2]) & 3) for y in range(4)]
    xs = [place((x + 4 - sc[3]) & 3) for x in range(4)]
    for z in range(2):
        for q in range(PLANE):
            at = base + (z * PLANE + q) * N
            dst[at : at + N] = src[ys[q // 4], xs[q % 4], z, offset : offset + N]


def scaled(k_ref, n):
    total = jnp.zeros((1, n), F32)
    cols = []
    for t in range(n // 128):
        rows = slice(t * 128, (t + 1) * 128)
        eye = iota((128, n), 0) + t * 128 == iota((128, n), 1)
        diag = jnp.where(eye, k_ref[rows], 0.0)
        total = total + jnp.sum(diag, axis=0, keepdims=True)
        cols.append(lax.rsqrt(jnp.sum(diag, axis=1, keepdims=True)))
    row = lax.rsqrt(total)
    norm = jnp.float32(0.0)
    peak = jnp.float32(0.0)
    for t in range(n // 128):
        rows = slice(t * 128, (t + 1) * 128)
        part = k_ref[rows] * cols[t] * row
        k_ref[rows] = part
        norm = norm + jnp.sum(part * part)
        peak = jnp.maximum(peak, jnp.max(jnp.sum(jnp.abs(part), axis=1, keepdims=True)))
    return row, cols, norm, peak


TILE = 384
MTILE = 384


def solve_right(k_ref, v_ref, u_ref, x_ref, r_ref, xf_ref, rf_ref, kh_ref, kl_ref, n, norm, peak):
    tile = TILE
    count = n // tile
    m = v_ref.shape[0]
    mtile = min(m, MTILE)
    alpha = n / norm

    def eye(t, width):
        return (iota((width, n), 0) + t * width == iota((width, n), 1)).astype(F32)

    for t in range(count):
        rows = slice(t * tile, (t + 1) * tile)
        e = eye(t, tile)
        kh_ref[rows], kl_ref[rows] = split(k_ref[rows], 2)
        first = e - alpha * k_ref[rows]
        r_ref[0, rows] = first.astype(BF)
        x_ref[rows] = (alpha * (e + first)).astype(BF)

    def square(src, dst):
        def step(t, acc):
            rows = pl.ds(pl.multiple_of(t * tile, tile), tile)
            new = dot(r_ref[src, rows], r_ref[src])
            r_ref[dst, rows] = new.astype(BF)
            return acc + jnp.sum(new * new)

        return lax.fori_loop(0, count, step, jnp.float32(0.0))

    def advance(src):
        def step(t, carry):
            rows = pl.ds(pl.multiple_of(t * tile, tile), tile)
            old = x_ref[rows]
            x_ref[rows] = (old.astype(F32) + dot(old, r_ref[src])).astype(BF)
            return carry

        lax.fori_loop(0, count, step, 0)

    size = square(0, 1)

    def more(state):
        k, size = state
        return (size > 0.003 * n) & (k < 12)

    def iterate(state):
        k, _ = state
        src = (k + 1) % 2
        advance(src)
        return k + 1, square(src, k % 2)

    k, _ = lax.while_loop(more, iterate, (jnp.int32(0), size))
    advance((k + 1) % 2)

    def start(t, acc):
        rows = pl.ds(pl.multiple_of(t * mtile, mtile), mtile)
        v = v_ref[rows]
        u_ref[rows] = dot(v.astype(BF), x_ref[...])
        return acc + jnp.sum(v * v)

    scale = lax.fori_loop(0, m // mtile, start, jnp.float32(0.0))

    def refine(full):
        def step(t, acc):
            rows = pl.ds(pl.multiple_of(t * mtile, mtile), mtile)
            u = u_ref[rows]
            if full:
                left = v_ref[rows] - dot_full(u, k_ref[...])
                u_ref[rows] = u + dot_full(left, xf_ref[...])
            else:
                left = v_ref[rows] - dot_three(split(u, 2), (kh_ref[...], kl_ref[...]))
                u_ref[rows] = u + dot(left.astype(BF), x_ref[...])
            return acc + jnp.sum(left * left)

        return lax.fori_loop(0, m // mtile, step, jnp.float32(0.0))

    def unfinished(state):
        k, left = state
        return (left > 1e-7 * scale) & (left < 0.1 * scale) & (k < 12)

    done, left = lax.while_loop(
        unfinished, lambda s: (s[0] + 1, refine(False)), (jnp.int32(1), refine(False))
    )

    @pl.when(jnp.logical_not(left <= 1e-7 * scale))
    def _():
        def rows_of(t):
            return pl.ds(pl.multiple_of(t * 128, 128), 128)

        def begin(t, carry):
            xf_ref[rows_of(t)] = eye(t, 128) / peak
            return carry

        lax.fori_loop(0, n // 128, begin, 0)

        def newton(state):
            k, _ = state

            def residual(t, acc):
                rows = rows_of(t)
                new = eye(t, 128) - dot_full(xf_ref[rows], k_ref[...])
                rf_ref[rows] = new
                return acc + jnp.sum(new * new)

            size = lax.fori_loop(0, n // 128, residual, jnp.float32(0.0))
            for t in range(n // 128):
                r_t = slice(t * 128, (t + 1) * 128)
                rf_ref[n + t * 128 : n + (t + 1) * 128] = xf_ref[r_t]

            def update(t, carry):
                rows = rows_of(t)
                xf_ref[rows] = xf_ref[rows] + dot_full(rf_ref[rows], rf_ref[n : 2 * n])
                return carry

            lax.fori_loop(0, n // 128, update, 0)
            return k + 1, size

        lax.while_loop(
            lambda s: (s[1] > 1e-5) & (s[0] < 80), newton, (jnp.int32(0), jnp.float32(1.0) * n)
        )

        def again(t, carry):
            rows = pl.ds(pl.multiple_of(t * mtile, mtile), mtile)
            u_ref[rows] = dot_full(v_ref[rows], xf_ref[...])
            return carry

        lax.fori_loop(0, m // mtile, again, 0)
        refine(True)
        refine(True)


def solve_scratch(n, m):
    return [
        pltpu.VMEM((n, n), F32),
        pltpu.VMEM((m, n), F32),
        pltpu.VMEM((m, n), F32),
        pltpu.VMEM((n, n), BF),
        pltpu.VMEM((2, n, n), BF),
        pltpu.VMEM((n, n), F32),
        pltpu.VMEM((2 * n, n), F32),
        pltpu.VMEM((n, n), BF),
        pltpu.VMEM((n, n), BF),
    ]


def column(row):
    eye = iota((F, F), 0) == iota((F, F), 1)
    spread = jnp.where(eye, row.astype(F32), 0.0)
    return jnp.sum(spread, axis=1, keepdims=True).astype(jnp.int32)


def permute_cols(x, perm_row):
    hot = (iota((F, F), 0) == perm_row).astype(BF)
    return sum(dot(part, hot) for part in split(x, 3))


def from_second(rows):
    return (iota((rows, 1), 0) & 7) >= 4


def level_one_kernel(sc, kg, perm_row, x1, inv, y1, f1, k, v, u, x, r, xf, rf, kh, kl):
    natural(v, kg, sc, N)
    hot = (column(perm_row[...]) == iota((F, F), 1)).astype(BF)
    turned = sum(dot(hot, part) for part in split(v[...], 3))
    u[...] = permute_cols(turned, perm_row[...])
    natural(k, kg, sc, 0)
    k[...] = k[...] + u[...]
    row, cols, norm, peak = scaled(k, F)
    v[...] = (iota((F, F), 0) == iota((F, F), 1)).astype(F32)
    solve_right(k, v, u, x, r, xf, rf, kh, kl, F, norm, peak)
    for t in range(F // 128):
        rows = slice(t * 128, (t + 1) * 128)
        inv[rows] = u[rows] * cols[t] * row
    inverse = split(inv[...], 2)
    points = x1[...]
    points = jnp.where(from_second(8 * N), permute_cols(points, perm_row[...]), points)
    y1[...] = dot_three(split(points, 2), inverse)
    lane = iota((16, F), 1)
    sub = iota((16, F), 0)
    pick = ((lane == sub + sc[1] * N) & (sub < N)).astype(BF)
    f1[...] = sum(dot(pick, part) for part in split(inv[...], 3))


def level_two_kernel(sc, kg, perm_row, inv, x2, y1, f1, pv, wt, sf2, st):
    natural(st, kg, sc, 0)
    natural(st, kg, sc, 2 * N, F)
    st[F:] = permute_cols(st[F:], perm_row[...])
    natural(wt, kg, sc, N)
    natural(wt, kg, sc, 3 * N, F)
    inverse = split(inv[...], 2)
    second = split(st[...], 2)
    for t in range(2):
        rows = slice(t * F, (t + 1) * F)
        other = slice((1 - t) * F, (2 - t) * F)
        base = wt[rows]
        w = dot_three([part[rows] for part in second], inverse)
        wt[rows] = w
        part = dot_three(split(w, 2), second, dot_t)
        pv[rows, rows] = base - part[:, rows]
        pv[rows, other] = -part[:, other]
    part = dot_three(split(y1[...], 2), second, dot_t)
    late = from_second(8 * N)
    n = 2 * F
    pv[n : n + 96, :F] = jnp.where(late, 0.0, x2[...]) - part[:, :F]
    pv[n : n + 96, F:] = jnp.where(late, x2[...], 0.0) - part[:, F:]
    sf2[...] = -dot_three(split(f1[...], 2), second, dot_t)


def couple_kernel(sc, pv, other, wt, y1, f1, perm_row, target, ch, cl, k, v, u, x, r, xf, rf, kh, kl):
    n = 2 * F
    for t in range(6):
        rows = slice(t * 128, (t + 1) * 128)
        k[rows] = pv[rows] + other[rows]
    row, _, norm, peak = scaled(k, n)
    lane = iota((16, n), 1)
    sub = iota((16, n), 0)
    for h, source in enumerate((pv, other)):
        half = sc[0] if h == 0 else 1 - sc[0]
        pick = ((lane == half * F + sc[1] * N + sub) & (sub < N)).astype(F32)
        base = h * 128
        v[base : base + 96] = source[n : n + 96] * row
        v[base + 96 : base + 112] = pick * row
        v[base + 112 : base + 128] = jnp.zeros((16, n), F32)
    solve_right(k, v, u, x, r, xf, rf, kh, kl, n, norm, peak)
    u2 = u[...] * row
    u[...] = -u2
    k[:256, :F] = dot_three(split(u2, 2), split(wt[...], 2))
    k[:96, :F] = k[:96, :F] - y1[...]
    k[108:120, :F] = k[108:120, :F] - f1[:N]
    lanes = target[...]
    for b in range(2):
        keys = iota((n, 1), 0)
        if b == 1:
            keys = jnp.concatenate([column(perm_row[...]), keys[F:]], axis=0)
        hot = (keys == lanes).astype(BF)
        coef = jnp.concatenate([k[:256, :F], u[:, b * F : (b + 1) * F]], axis=1)
        high, low = split(coef, 2)
        ch[b] = dot(high, hot).astype(BF)
        cl[b] = dot(low, hot).astype(BF)


WIDE = 512


def product_kernel(ch, cl, g, dl, own, part):
    block = g[...].reshape(2 * F, WIDE)
    acc = dot_three((ch[0], cl[0]), split(block, 2))
    own[:96] = acc[:96] + dl[...]
    own[96:] = acc[96:128]
    part[...] = acc[128:240]


def product(b, ch, cl, g, dl):
    steps = 4 * F // WIDE
    coef = pl.BlockSpec((1, 256, 2 * F), lambda j: (b, 0, 0))
    return pl.pallas_call(
        product_kernel,
        grid=(steps,),
        in_specs=[
            coef,
            coef,
            pl.BlockSpec((ROWS, 1, 2 * N, WIDE), lambda j: (0, b, 0, j)),
            pl.BlockSpec((8 * N, WIDE), lambda j: (0, b * steps + j)),
        ],
        out_specs=[
            pl.BlockSpec((128, WIDE), lambda j: (0, j)),
            pl.BlockSpec((112, WIDE), lambda j: (0, j)),
        ],
        out_shape=[
            jax.ShapeDtypeStruct((128, 4 * F), F32),
            jax.ShapeDtypeStruct((112, 4 * F), F32),
        ],
        compiler_params=LIMIT,
        cost_estimate=pl.CostEstimate(flops=4 * 10**9, bytes_accessed=10**7, transcendentals=0),
    )(ch, cl, g, dl)


def finish_kernel(sc, own_a, own_b, other_a, other_b, sf2, sf, ss, mm):
    wide = 4 * F
    for h in range(2):
        @pl.when(sc[0] == h)
        def _():
            for b, (own, other) in enumerate(((own_a, other_a), (own_b, other_b))):
                near = slice((2 * h + b) * wide, (2 * h + b + 1) * wide)
                far = slice((2 - 2 * h + b) * wide, (3 - 2 * h + b) * wide)
                for i in range(N):
                    mm[i, :, near] = own[8 * i : 8 * i + 8]
                    mm[i, :, far] = other[8 * i : 8 * i + 8]
                    ss[i, :, near] = own[96 + i : 97 + i]
                    ss[i, :, far] = other[96 + i : 97 + i]
                    row = own[108 + i : 109 + i]
                    at = 5 * b * F
                    sf[i, :, at : at + F] = row[:, :F]
                    outer, inner = (at + F, at + 2 * F) if h == 0 else (at + 2 * F, at + F)
                    sf[i, :, outer : outer + F] = row[:, F : 2 * F]
                    sf[i, :, inner : inner + F] = sf2[i : i + 1, b * F : (b + 1) * F]
                    sf[i, :, at + 3 * F : at + 5 * F] = row[:, 2 * F :]


PLANE_AXES = ("y", "x")


def swap(x, axis):
    return lax.ppermute(x, axis, [(0, 1), (1, 0)])


def both_planes(x):
    other = swap(x, "z_hi")
    low = lax.axis_index("z_hi") == 0
    return jnp.stack([jnp.where(low, x, other), jnp.where(low, other, x)])


def around(x, axis):
    return jnp.stack(
        [x] + [lax.ppermute(x, axis, [(i, (i + k) % 4) for i in range(4)]) for k in (1, 3, 2)]
    )


def gather_plane(x):
    return around(around(x, "x"), "y")


def body(dtn, interface_perm):
    half = lax.axis_index("core")
    spots = [lax.axis_index(name) for name in ("z_hi", "y", "x")]
    row = (spots[0] * 4 + spots[1]) * 4 + spots[2]
    sc = jnp.stack([half, row] + spots[1:]).astype(jnp.int32)
    perm_row = interface_perm
    ks, gs, x1, x2, dl = pack(sc, dtn.transpose(1, 2, 0, 3))
    kz = both_planes(ks)
    gs, kz = lax.optimization_barrier((gs, kz))
    gz = both_planes(gs)
    k1g = gather_plane(kz[:, : 2 * N])
    k2g = gather_plane(kz[:, 2 * N :])
    g = lax.all_gather(gz, PLANE_AXES)
    g = g.reshape(ROWS, 2, 2 * N, 4 * F)
    inv, y1, f1 = level_one(sc, k1g, perm_row, x1)
    pv, wt, sf2 = level_two(sc, k2g, perm_row, inv, x2, y1, f1)
    other = swap(pv, "core")
    ch, cl = couple(sc, pv, other, wt, y1, f1, perm_row)
    own_a, part_a = product(0, ch, cl, g, dl)
    arrived_a = swap(part_a, "core")
    own_b, part_b = product(1, ch, cl, g, dl)
    arrived_b = swap(part_b, "core")
    sf, ss, mm = finish(sc, own_a, own_b, arrived_a, arrived_b, sf2)
    return sf.transpose(1, 0, 2), ss.transpose(1, 0, 2), mm[None].transpose(0, 2, 1, 3)


def pack(*operands):
    return call(
        pack_kernel,
        [
            ((6 * N, F), F32),
            ((2, 2 * N, 4 * F), F32),
            ((8 * N, F), F32),
            ((8 * N, F), F32),
            ((8 * N, 8 * F), F32),
        ],
        operands,
        smem=(0,),
    )


def level_one(*operands):
    return call(
        level_one_kernel,
        [((F, F), F32), ((8 * N, F), F32), ((16, F), F32)],
        operands,
        smem=(0,),
        scratch=solve_scratch(F, F),
        flops=10 * 10**9,
    )


def level_two(*operands):
    return call(
        level_two_kernel,
        [((864, 2 * F), F32), ((2 * F, F), F32), ((16, 2 * F), F32)],
        operands,
        smem=(0,),
        scratch=[pltpu.VMEM((2 * F, F), F32)],
        flops=5 * 10**9,
    )


def couple(*operands):
    natural_row = np.arange(F).reshape(2, PLANE, N).transpose(1, 0, 2)
    target = np.stack([natural_row, natural_row + F], axis=2).reshape(1, 2 * F)
    return call(
        couple_kernel,
        [((2, 256, 2 * F), BF), ((2, 256, 2 * F), BF)],
        operands + (jnp.asarray(target, jnp.int32),),
        smem=(0,),
        scratch=solve_scratch(2 * F, 256),
        flops=20 * 10**9,
    )


def finish(*operands):
    return call(
        finish_kernel,
        [((N, 1, 10 * F), F32), ((N, 1, 16 * F), F32), ((N, 8, 16 * F), F32)],
        operands,
        smem=(0,),
    )


def solution(mesh):
    split_mesh = jax.sharding.Mesh(
        mesh.devices.reshape(-1, 2, 2, 4, 4), ("z_lo", "core", "z_hi", "y", "x")
    )
    pair, rows = ("z_lo", "core"), ("z_hi", "y", "x")
    return jax.shard_map(
        body,
        mesh=split_mesh,
        in_specs=(P(pair, None, rows, None), P(pair, None)),
        out_specs=(P(pair, rows, None), P(pair, rows, None), P(pair, None, rows, None)),
        check_vma=False,
    )
```

```python
import functools

import jax
import jax.numpy as jnp
import numpy as np
from jax import lax
from jax.experimental import pallas as pl
from jax.experimental.pallas import tpu as pltpu
from jax.sharding import PartitionSpec as P

F = 384
N = 12
ROWS = 32
PLANE = 16
BF = jnp.bfloat16
F32 = jnp.float32
LIMIT = pltpu.CompilerParams(vmem_limit_bytes=56 * 1024 * 1024)
VMEM = pl.BlockSpec(memory_space=pltpu.VMEM)
SMEM = pl.BlockSpec(memory_space=pltpu.SMEM)


def call(kernel, outs, operands, smem=(), scratch=(), flops=10**9):
    return pl.pallas_call(
        kernel,
        out_shape=[jax.ShapeDtypeStruct(s, d) for s, d in outs],
        in_specs=[SMEM if i in smem else VMEM for i in range(len(operands))],
        out_specs=[VMEM] * len(outs),
        scratch_shapes=list(scratch),
        compiler_params=LIMIT,
        cost_estimate=pl.CostEstimate(flops=flops, bytes_accessed=10**6, transcendentals=0),
    )(*operands)


def dot(a, b):
    return jnp.dot(a, b, preferred_element_type=F32)


def dot_full(a, b):
    return jnp.dot(a, b, preferred_element_type=F32, precision=lax.Precision.HIGHEST)


def dot_t(a, b):
    return lax.dot_general(a, b, (((1,), (1,)), ((), ())), preferred_element_type=F32)


def dot_three(a, b, kernel=dot):
    (ah, al), (bh, bl) = a, b
    m = ah.shape[0]
    both = kernel(jnp.concatenate([ah, al], axis=0), bh)
    return both[:m] + (both[m:] + kernel(ah, bl))


def split(x, parts):
    out = []
    for _ in range(parts):
        top = x.astype(BF)
        out.append(top)
        x = x - top.astype(F32)
    return out


def iota(shape, dim):
    return lax.broadcasted_iota(jnp.int32, shape, dim)


def pack_kernel(sc, dtn, send, x1, x2, dl):
    even = sc[0] == 0
    empty = jnp.zeros((4, 4 * F), F32)
    send[4 * N :, 3 * F :] = jnp.zeros((2 * N, F), F32)
    for i in range(N):
        one, two, block = [], [], []
        for b in range(2):
            i1 = 1 - b

            def second(rows):
                return jnp.where(even, rows[:, 3 * F : 4 * F], rows[:, 2 * F : 3 * F])

            def others(rows):
                mid = jnp.where(even, rows[:, 2 * F : 3 * F], rows[:, 3 * F : 4 * F])
                return jnp.concatenate([rows[:, b * F : (b + 1) * F], mid, rows[:, 4 * F :]], axis=1)

            face = [dtn[f, i, b : b + 1] for f in range(6)]
            row_one = face[i1]
            row_two = jnp.where(even, face[3], face[2])
            middle = jnp.where(even, face[2], face[3])
            outer = jnp.concatenate([face[b], middle, face[4], face[5]], axis=0)
            cols = slice(i1 * F, (i1 + 1) * F)
            at = 2 * b * N + i
            send[at : at + 1] = others(row_one)
            send[at + N : at + N + 1] = others(row_two)
            at = 4 * N + i
            send[at : at + 1, b * F : (b + 1) * F] = row_two[:, cols]
            send[at + N : at + N + 1, b * F : (b + 1) * F] = second(row_two)
            at += b * N
            send[at : at + 1, 2 * F : 3 * F] = row_one[:, cols]
            one.append(outer[:, cols])
            two.append(second(outer))
            block.append(others(outer))
        rows = slice(8 * i, 8 * i + 8)
        x1[rows] = jnp.concatenate(one, axis=0)
        x2[rows] = jnp.concatenate(two, axis=0)
        dl[rows, : 4 * F] = jnp.concatenate([block[0], empty], axis=0)
        dl[rows, 4 * F :] = jnp.concatenate([empty, block[1]], axis=0)


def place(distance):
    return jnp.where(distance == 0, 0, jnp.where(distance == 3, 1, distance + 1))


def natural(dst, base, src, sc, offset, col=0, y_first=True):
    ys = [place((y + 4 - sc[2]) & 3) for y in range(4)]
    xs = [place((x + 4 - sc[3]) & 3) for x in range(4)]
    for z in range(2):
        for q in range(PLANE):
            at = base + (z * PLANE + q) * N
            y, x = ys[q // 4], xs[q % 4]
            first, then = (y, x) if y_first else (x, y)
            dst[at : at + N] = src[first, then, z, offset : offset + N, col : col + F]


def scaled(k_ref, n):
    eye = iota((128, 128), 0) == iota((128, 128), 1)
    row, cols = [], []
    for t in range(n // 128):
        rows = slice(t * 128, (t + 1) * 128)
        diag = jnp.where(eye, k_ref[rows, rows], 0.0)
        row.append(jnp.sum(diag, axis=0, keepdims=True))
        cols.append(lax.rsqrt(jnp.sum(diag, axis=1, keepdims=True)))
    row = lax.rsqrt(jnp.concatenate(row, axis=1))
    norm = jnp.zeros((8, n), F32)
    for t in range(n // 128):
        rows = slice(t * 128, (t + 1) * 128)
        part = k_ref[rows] * cols[t] * row
        k_ref[rows] = part
        norm = norm + jnp.sum((part * part).reshape(16, 8, n), axis=0)
    return row, cols, jnp.sum(norm)


TILE = 384
MTILE = 384


def solve_right(k_ref, v_ref, u_ref, x_ref, r_ref, xf_ref, rf_ref, kh_ref, kl_ref, n, norm):
    tile = TILE
    count = n // tile
    m = v_ref.shape[0]
    mtile = min(m, MTILE)
    alpha = n / norm

    def eye(t, width):
        return (iota((width, n), 0) + t * width == iota((width, n), 1)).astype(F32)

    for t in range(count):
        rows = slice(t * tile, (t + 1) * tile)
        e = eye(t, tile)
        part = k_ref[rows]
        kh_ref[rows], kl_ref[rows] = split(part, 2)
        first = e - alpha * part
        r_ref[0, rows] = first.astype(BF)
        x_ref[rows] = (alpha * (e + first)).astype(BF)

    def square(src, dst, with_x):
        def step(t, acc):
            rows = pl.ds(pl.multiple_of(t * tile, tile), tile)
            left = r_ref[src, rows]
            if with_x:
                old = x_ref[rows]
                both = dot(jnp.concatenate([left, old], axis=0), r_ref[src])
                new = both[:tile]
                x_ref[rows] = (old.astype(F32) + both[tile:]).astype(BF)
            else:
                new = dot(left, r_ref[src])
            r_ref[dst, rows] = new.astype(BF)
            return acc + jnp.sum(new * new)

        return lax.fori_loop(0, count, step, jnp.float32(0.0))

    def advance(src):
        def step(t, carry):
            rows = pl.ds(pl.multiple_of(t * tile, tile), tile)
            old = x_ref[rows]
            x_ref[rows] = (old.astype(F32) + dot(old, r_ref[src])).astype(BF)
            return carry

        lax.fori_loop(0, count, step, 0)

    size = square(0, 1, False)

    def more(state):
        k, size = state
        return (size > 0.003 * n) & (k < 12)

    def iterate(state):
        k, _ = state
        src = (k + 1) % 2
        return k + 1, square(src, k % 2, True)

    k, _ = lax.while_loop(more, iterate, (jnp.int32(0), size))
    advance((k + 1) % 2)

    def start(t, acc):
        rows = pl.ds(pl.multiple_of(t * mtile, mtile), mtile)
        v = v_ref[rows]
        u_ref[rows] = dot(v.astype(BF), x_ref[...])
        return acc + jnp.sum(v * v)

    scale = lax.fori_loop(0, m // mtile, start, jnp.float32(0.0))

    def refine(full):
        def step(t, acc):
            rows = pl.ds(pl.multiple_of(t * mtile, mtile), mtile)
            u = u_ref[rows]
            if full:
                left = v_ref[rows] - dot_full(u, k_ref[...])
                u_ref[rows] = u + dot_full(left, xf_ref[...])
            else:
                left = v_ref[rows] - dot_three(split(u, 2), (kh_ref[...], kl_ref[...]))
                u_ref[rows] = u + dot(left.astype(BF), x_ref[...])
            return acc + jnp.sum(left * left)

        return lax.fori_loop(0, m // mtile, step, jnp.float32(0.0))

    def unfinished(state):
        k, left = state
        return (left > 1e-7 * scale) & (left < 0.1 * scale) & (k < 12)

    done, left = lax.while_loop(
        unfinished, lambda s: (s[0] + 1, refine(False)), (jnp.int32(1), refine(False))
    )

    @pl.when(jnp.logical_not(left <= 1e-7 * scale))
    def _():
        def rows_of(t):
            return pl.ds(pl.multiple_of(t * 128, 128), 128)

        def highest(t, acc):
            return jnp.maximum(acc, jnp.max(jnp.sum(jnp.abs(k_ref[rows_of(t)]), axis=1, keepdims=True)))

        peak = lax.fori_loop(0, n // 128, highest, jnp.float32(0.0))

        def begin(t, carry):
            xf_ref[rows_of(t)] = eye(t, 128) / peak
            return carry

        lax.fori_loop(0, n // 128, begin, 0)

        def newton(state):
            k, _ = state

            def residual(t, acc):
                rows = rows_of(t)
                new = eye(t, 128) - dot_full(xf_ref[rows], k_ref[...])
                rf_ref[rows] = new
                return acc + jnp.sum(new * new)

            size = lax.fori_loop(0, n // 128, residual, jnp.float32(0.0))
            for t in range(n // 128):
                r_t = slice(t * 128, (t + 1) * 128)
                rf_ref[n + t * 128 : n + (t + 1) * 128] = xf_ref[r_t]

            def update(t, carry):
                rows = rows_of(t)
                xf_ref[rows] = xf_ref[rows] + dot_full(rf_ref[rows], rf_ref[n : 2 * n])
                return carry

            lax.fori_loop(0, n // 128, update, 0)
            return k + 1, size

        lax.while_loop(
            lambda s: (s[1] > 1e-5) & (s[0] < 80), newton, (jnp.int32(0), jnp.float32(1.0) * n)
        )

        def again(t, carry):
            rows = pl.ds(pl.multiple_of(t * mtile, mtile), mtile)
            u_ref[rows] = dot_full(v_ref[rows], xf_ref[...])
            return carry

        lax.fori_loop(0, m // mtile, again, 0)
        refine(True)
        refine(True)


def solve_scratch(n, m):
    return [
        pltpu.VMEM((n, n), F32),
        pltpu.VMEM((m, n), F32),
        pltpu.VMEM((m, n), F32),
        pltpu.VMEM((n, n), BF),
        pltpu.VMEM((2, n, n), BF),
        pltpu.VMEM((n, n), F32),
        pltpu.VMEM((2 * n, n), F32),
        pltpu.VMEM((n, n), BF),
        pltpu.VMEM((n, n), BF),
    ]


def column(row):
    eye = iota((F, F), 0) == iota((F, F), 1)
    spread = jnp.where(eye, row.astype(F32), 0.0)
    return jnp.sum(spread, axis=1, keepdims=True).astype(jnp.int32)


def permute_cols(x, perm_row):
    hot = (iota((F, F), 0) == perm_row).astype(BF)
    return sum(dot(part, hot) for part in split(x, 3))


def from_second(rows):
    return (iota((rows, 1), 0) & 7) >= 4


def level_one_kernel(sc, kg, perm_row, x1, inv, y1, f1, k, v, u, x, r, xf, rf, kh, kl):
    natural(v, 0, kg, sc, N)
    hot = (column(perm_row[...]) == iota((F, F), 1)).astype(BF)
    turned = sum(dot(hot, part) for part in split(v[...], 3))
    u[...] = permute_cols(turned, perm_row[...])
    natural(k, 0, kg, sc, 0)
    k[...] = k[...] + u[...]
    row, cols, norm = scaled(k, F)
    v[...] = (iota((F, F), 0) == iota((F, F), 1)).astype(F32)
    solve_right(k, v, u, x, r, xf, rf, kh, kl, F, norm)
    for t in range(F // 128):
        rows = slice(t * 128, (t + 1) * 128)
        inv[rows] = u[rows] * cols[t] * row
    inverse = split(inv[...], 2)
    points = x1[...]
    points = jnp.where(from_second(8 * N), permute_cols(points, perm_row[...]), points)
    y1[...] = dot_three(split(points, 2), inverse)
    lane = iota((16, F), 1)
    sub = iota((16, F), 0)
    pick = ((lane == sub + sc[1] * N) & (sub < N)).astype(BF)
    f1[...] = sum(dot(pick, part) for part in split(inv[...], 3))


def level_two_kernel(sc, kg, perm_row, inv, x2, y1, f1, pv, wt, sf2, st):
    natural(st, 0, kg, sc, 0, 0, False)
    natural(st, F, kg, sc, 0, F, False)
    st[F:] = permute_cols(st[F:], perm_row[...])
    natural(wt, 0, kg, sc, N, 0, False)
    natural(wt, F, kg, sc, N, F, False)
    inverse = split(inv[...], 2)
    second = split(st[...], 2)
    for t in range(2):
        rows = slice(t * F, (t + 1) * F)
        other = slice((1 - t) * F, (2 - t) * F)
        base = wt[rows]
        w = dot_three([part[rows] for part in second], inverse)
        wt[rows] = w
        part = dot_three(split(w, 2), second, dot_t)
        pv[rows, rows] = base - part[:, rows]
        pv[rows, other] = -part[:, other]
    part = dot_three(split(y1[...], 2), second, dot_t)
    late = from_second(8 * N)
    n = 2 * F
    pv[n : n + 96, :F] = jnp.where(late, 0.0, x2[...]) - part[:, :F]
    pv[n : n + 96, F:] = jnp.where(late, x2[...], 0.0) - part[:, F:]
    sf2[...] = -dot_three(split(f1[...], 2), second, dot_t)


def couple_kernel(sc, pv, other, wt, y1, f1, perm_row, target, cc, k, v, u, x, r, xf, rf, kh, kl):
    n = 2 * F
    for t in range(6):
        rows = slice(t * 128, (t + 1) * 128)
        k[rows] = pv[rows] + other[rows]
    row, _, norm = scaled(k, n)
    lane = iota((16, n), 1)
    sub = iota((16, n), 0)
    for h, source in enumerate((pv, other)):
        half = sc[0] if h == 0 else 1 - sc[0]
        pick = ((lane == half * F + sc[1] * N + sub) & (sub < N)).astype(F32)
        base = h * 128
        v[base : base + 96] = source[n : n + 96] * row
        v[base + 96 : base + 112] = pick * row
        v[base + 112 : base + 128] = jnp.zeros((16, n), F32)
    solve_right(k, v, u, x, r, xf, rf, kh, kl, n, norm)
    u2 = u[...] * row
    u[...] = -u2
    k[:256, :F] = dot_three(split(u2, 2), split(wt[...], 2))
    k[:96, :F] = k[:96, :F] - y1[...]
    k[108:120, :F] = k[108:120, :F] - f1[:N]
    lanes = target[...]
    for b in range(2):
        keys = iota((n, 1), 0)
        if b == 1:
            keys = jnp.concatenate([column(perm_row[...]), keys[F:]], axis=0)
        hot = (keys == lanes).astype(BF)
        coef = jnp.concatenate([k[:256, :F], u[:, b * F : (b + 1) * F]], axis=1)
        high, low = split(coef, 2)
        cc[b] = dot(jnp.concatenate([high, low], axis=0), hot).astype(BF)


WIDE = 512


def product_kernel(cc, g, dl, own, part):
    block = g[...].reshape(2 * F, WIDE)
    high, low = split(block, 2)
    both = dot(cc[0], high)
    acc = both[:256] + (both[256:] + dot(cc[0, :256], low))
    own[:96] = acc[:96] + dl[...]
    own[96:] = acc[96:128]
    part[...] = acc[128:240]


def product(b, cc, g, dl):
    steps = 4 * F // WIDE
    return pl.pallas_call(
        product_kernel,
        grid=(steps,),
        in_specs=[
            pl.BlockSpec((1, 512, 2 * F), lambda j: (b, 0, 0)),
            pl.BlockSpec((ROWS, 1, 2 * N, WIDE), lambda j: (0, b, 0, j)),
            pl.BlockSpec((8 * N, WIDE), lambda j: (0, b * steps + j)),
        ],
        out_specs=[
            pl.BlockSpec((128, WIDE), lambda j: (0, j)),
            pl.BlockSpec((112, WIDE), lambda j: (0, j)),
        ],
        out_shape=[
            jax.ShapeDtypeStruct((128, 4 * F), F32),
            jax.ShapeDtypeStruct((112, 4 * F), F32),
        ],
        compiler_params=LIMIT,
        cost_estimate=pl.CostEstimate(flops=4 * 10**9, bytes_accessed=10**7, transcendentals=0),
    )(cc, g, dl)


def finish_kernel(sc, own_a, own_b, other_a, other_b, sf2, sf, ss, mm):
    wide = 4 * F
    for h in range(2):
        @pl.when(sc[0] == h)
        def _():
            for b, (own, other) in enumerate(((own_a, other_a), (own_b, other_b))):
                near = slice((2 * h + b) * wide, (2 * h + b + 1) * wide)
                far = slice((2 - 2 * h + b) * wide, (3 - 2 * h + b) * wide)
                for i in range(N):
                    mm[i, :, near] = own[8 * i : 8 * i + 8]
                    mm[i, :, far] = other[8 * i : 8 * i + 8]
                    ss[i, :, near] = own[96 + i : 97 + i]
                    ss[i, :, far] = other[96 + i : 97 + i]
                    row = own[108 + i : 109 + i]
                    at = 5 * b * F
                    sf[i, :, at : at + F] = row[:, :F]
                    outer, inner = (at + F, at + 2 * F) if h == 0 else (at + 2 * F, at + F)
                    sf[i, :, outer : outer + F] = row[:, F : 2 * F]
                    sf[i, :, inner : inner + F] = sf2[i : i + 1, b * F : (b + 1) * F]
                    sf[i, :, at + 3 * F : at + 5 * F] = row[:, 2 * F :]


PLANE_AXES = ("y", "x")


def swap(x, axis):
    return lax.ppermute(x, axis, [(0, 1), (1, 0)])


def around(x, axis):
    return jnp.stack(
        [x] + [lax.ppermute(x, axis, [(i, (i + k) % 4) for i in range(4)]) for k in (1, 3, 2)]
    )


def body(dtn, interface_perm):
    half = lax.axis_index("core")
    spots = [lax.axis_index(name) for name in ("z_hi", "y", "x")]
    row = (spots[0] * 4 + spots[1]) * 4 + spots[2]
    sc = jnp.stack([half, row] + spots[1:]).astype(jnp.int32)
    perm_row = interface_perm
    send, x1, x2, dl = pack(sc, dtn.transpose(1, 2, 0, 3))
    other = swap(send, "z_hi")
    low = lax.axis_index("z_hi") == 0

    def both_planes(lo, hi, left, right):
        mine, theirs = send[lo:hi, left:right], other[lo:hi, left:right]
        return jnp.stack([jnp.where(low, mine, theirs), jnp.where(low, theirs, mine)])

    k1g = around(around(both_planes(4 * N, 6 * N, 2 * F, 3 * F), "x"), "y")
    k2g = around(around(both_planes(4 * N, 6 * N, 0, 2 * F), "y"), "x")
    g = lax.all_gather(both_planes(0, 4 * N, 0, 4 * F), PLANE_AXES)
    g = g.reshape(ROWS, 2, 2 * N, 4 * F)
    inv, y1, f1 = level_one(sc, k1g, perm_row, x1)
    pv, wt, sf2 = level_two(sc, k2g, perm_row, inv, x2, y1, f1)
    paired = swap(pv, "core")
    (cc,) = couple(sc, pv, paired, wt, y1, f1, perm_row)
    own_a, part_a = product(0, cc, g, dl)
    arrived_a = swap(part_a, "core")
    own_b, part_b = product(1, cc, g, dl)
    arrived_b = swap(part_b, "core")
    sf, ss, mm = finish(sc, own_a, own_b, arrived_a, arrived_b, sf2)
    return sf.transpose(1, 0, 2), ss.transpose(1, 0, 2), mm[None].transpose(0, 2, 1, 3)


def pack(*operands):
    return call(
        pack_kernel,
        [
            ((6 * N, 4 * F), F32),
            ((8 * N, F), F32),
            ((8 * N, F), F32),
            ((8 * N, 8 * F), F32),
        ],
        operands,
        smem=(0,),
    )


def level_one(*operands):
    return call(
        level_one_kernel,
        [((F, F), F32), ((8 * N, F), F32), ((16, F), F32)],
        operands,
        smem=(0,),
        scratch=solve_scratch(F, F),
        flops=10 * 10**9,
    )


def level_two(*operands):
    return call(
        level_two_kernel,
        [((864, 2 * F), F32), ((2 * F, F), F32), ((16, 2 * F), F32)],
        operands,
        smem=(0,),
        scratch=[pltpu.VMEM((2 * F, F), F32)],
        flops=5 * 10**9,
    )


def couple(*operands):
    natural_row = np.arange(F).reshape(2, PLANE, N).transpose(1, 0, 2)
    target = np.stack([natural_row, natural_row + F], axis=2).reshape(1, 2 * F)
    return call(
        couple_kernel,
        [((2, 512, 2 * F), BF)],
        operands + (jnp.asarray(target, jnp.int32),),
        smem=(0,),
        scratch=solve_scratch(2 * F, 256),
        flops=20 * 10**9,
    )


def finish(*operands):
    return call(
        finish_kernel,
        [((N, 1, 10 * F), F32), ((N, 1, 16 * F), F32), ((N, 8, 16 * F), F32)],
        operands,
        smem=(0,),
    )


def solution(mesh):
    split_mesh = jax.sharding.Mesh(
        mesh.devices.reshape(-1, 2, 2, 4, 4), ("z_lo", "core", "z_hi", "y", "x")
    )
    pair, rows = ("z_lo", "core"), ("z_hi", "y", "x")
    return jax.shard_map(
        body,
        mesh=split_mesh,
        in_specs=(P(pair, None, rows, None), P(pair, None)),
        out_specs=(P(pair, rows, None), P(pair, rows, None), P(pair, None, rows, None)),
        check_vma=False,
    )
```

```python
import functools

import jax
import jax.numpy as jnp
import numpy as np
from jax import lax
from jax.experimental import pallas as pl
from jax.experimental.pallas import tpu as pltpu
from jax.sharding import PartitionSpec as P

F = 384
N = 12
ROWS = 32
PLANE = 16
BF = jnp.bfloat16
F32 = jnp.float32
LIMIT = pltpu.CompilerParams(vmem_limit_bytes=56 * 1024 * 1024)
VMEM = pl.BlockSpec(memory_space=pltpu.VMEM)
SMEM = pl.BlockSpec(memory_space=pltpu.SMEM)


def call(kernel, outs, operands, smem=(), scratch=(), flops=10**9):
    return pl.pallas_call(
        kernel,
        out_shape=[jax.ShapeDtypeStruct(s, d) for s, d in outs],
        in_specs=[SMEM if i in smem else VMEM for i in range(len(operands))],
        out_specs=[VMEM] * len(outs),
        scratch_shapes=list(scratch),
        compiler_params=LIMIT,
        cost_estimate=pl.CostEstimate(flops=flops, bytes_accessed=10**6, transcendentals=0),
    )(*operands)


def dot(a, b):
    return jnp.dot(a, b, preferred_element_type=F32)


def dot_full(a, b):
    return jnp.dot(a, b, preferred_element_type=F32, precision=lax.Precision.HIGHEST)


def dot_t(a, b):
    return lax.dot_general(a, b, (((1,), (1,)), ((), ())), preferred_element_type=F32)


def dot_three(a, b, kernel=dot):
    (ah, al), (bh, bl) = a, b
    m = ah.shape[0]
    both = kernel(jnp.concatenate([ah, al], axis=0), bh)
    return both[:m] + (both[m:] + kernel(ah, bl))


def split(x, parts):
    out = []
    for _ in range(parts):
        top = x.astype(BF)
        out.append(top)
        x = x - top.astype(F32)
    return out


def iota(shape, dim):
    return lax.broadcasted_iota(jnp.int32, shape, dim)


def pack_kernel(sc, dtn, ks, ga, x1, x2, dl):
    even = sc[0] == 0
    empty = jnp.zeros((4, 4 * F), F32)
    for i in range(N):
        one, two, block = [], [], []
        for b in range(2):
            i1 = 1 - b

            def second(rows):
                return jnp.where(even, rows[:, 3 * F : 4 * F], rows[:, 2 * F : 3 * F])

            def others(rows):
                mid = jnp.where(even, rows[:, 2 * F : 3 * F], rows[:, 3 * F : 4 * F])
                return jnp.concatenate([rows[:, b * F : (b + 1) * F], mid, rows[:, 4 * F :]], axis=1)

            face = [dtn[f, i, b : b + 1] for f in range(6)]
            row_one = face[i1]
            row_two = jnp.where(even, face[3], face[2])
            middle = jnp.where(even, face[2], face[3])
            outer = jnp.concatenate([face[b], middle, face[4], face[5]], axis=0)
            cols = slice(i1 * F, (i1 + 1) * F)
            dst, at = (ga, 0) if b == 0 else (ks, 3 * F)
            dst[i : i + 1, at : at + 4 * F] = others(row_one)
            dst[N + i : N + i + 1, at : at + 4 * F] = others(row_two)
            ks[i : i + 1, b * F : (b + 1) * F] = row_two[:, cols]
            ks[N + i : N + i + 1, b * F : (b + 1) * F] = second(row_two)
            ks[b * N + i : b * N + i + 1, 2 * F : 3 * F] = row_one[:, cols]
            one.append(outer[:, cols])
            two.append(second(outer))
            block.append(others(outer))
        rows = slice(8 * i, 8 * i + 8)
        x1[rows] = jnp.concatenate(one, axis=0)
        x2[rows] = jnp.concatenate(two, axis=0)
        dl[rows, : 4 * F] = jnp.concatenate([block[0], empty], axis=0)
        dl[rows, 4 * F :] = jnp.concatenate([empty, block[1]], axis=0)


def place(distance):
    return jnp.where(distance == 0, 0, jnp.where(distance == 3, 1, distance + 1))


def natural(dst, base, src, sc, offset, col=0, y_first=True):
    ys = [place((y + 4 - sc[2]) & 3) for y in range(4)]
    xs = [place((x + 4 - sc[3]) & 3) for x in range(4)]
    for z in range(2):
        for q in range(PLANE):
            at = base + (z * PLANE + q) * N
            y, x = ys[q // 4], xs[q % 4]
            first, then = (y, x) if y_first else (x, y)
            dst[at : at + N] = src[first, then, z, offset : offset + N, col : col + F]


def scaled(k_ref, n):
    eye = iota((128, 128), 0) == iota((128, 128), 1)
    row, cols = [], []
    for t in range(n // 128):
        rows = slice(t * 128, (t + 1) * 128)
        diag = jnp.where(eye, k_ref[rows, rows], 0.0)
        row.append(jnp.sum(diag, axis=0, keepdims=True))
        cols.append(lax.rsqrt(jnp.sum(diag, axis=1, keepdims=True)))
    row = lax.rsqrt(jnp.concatenate(row, axis=1))
    norm = jnp.zeros((8, n), F32)
    for t in range(n // 128):
        rows = slice(t * 128, (t + 1) * 128)
        part = k_ref[rows] * cols[t] * row
        k_ref[rows] = part
        norm = norm + jnp.sum((part * part).reshape(16, 8, n), axis=0)
    return row, cols, jnp.sum(norm)


TILE = 384
MTILE = 384


def solve_right(k_ref, v_ref, u_ref, x_ref, r_ref, xf_ref, rf_ref, kh_ref, kl_ref, n, norm):
    tile = TILE
    count = n // tile
    m = v_ref.shape[0]
    mtile = min(m, MTILE)
    alpha = n / norm

    def eye(t, width):
        return (iota((width, n), 0) + t * width == iota((width, n), 1)).astype(F32)

    for t in range(count):
        rows = slice(t * tile, (t + 1) * tile)
        e = eye(t, tile)
        part = k_ref[rows]
        kh_ref[rows], kl_ref[rows] = split(part, 2)
        first = e - alpha * part
        r_ref[0, rows] = first.astype(BF)
        x_ref[rows] = (alpha * (e + first)).astype(BF)

    def square(src, dst, with_x):
        def step(t, acc):
            rows = pl.ds(pl.multiple_of(t * tile, tile), tile)
            left = r_ref[src, rows]
            if with_x:
                old = x_ref[rows]
                both = dot(jnp.concatenate([left, old], axis=0), r_ref[src])
                new = both[:tile]
                x_ref[rows] = (old.astype(F32) + both[tile:]).astype(BF)
            else:
                new = dot(left, r_ref[src])
            r_ref[dst, rows] = new.astype(BF)
            return acc + jnp.sum(new * new)

        return lax.fori_loop(0, count, step, jnp.float32(0.0))

    def advance(src):
        def step(t, carry):
            rows = pl.ds(pl.multiple_of(t * tile, tile), tile)
            old = x_ref[rows]
            x_ref[rows] = (old.astype(F32) + dot(old, r_ref[src])).astype(BF)
            return carry

        lax.fori_loop(0, count, step, 0)

    size = square(0, 1, False)

    def more(state):
        k, size = state
        return (size > 0.003 * n) & (k < 12)

    def iterate(state):
        k, _ = state
        src = (k + 1) % 2
        return k + 1, square(src, k % 2, True)

    k, _ = lax.while_loop(more, iterate, (jnp.int32(0), size))
    advance((k + 1) % 2)

    def start(t, acc):
        rows = pl.ds(pl.multiple_of(t * mtile, mtile), mtile)
        v = v_ref[rows]
        u_ref[rows] = dot(v.astype(BF), x_ref[...])
        return acc + jnp.sum(v * v)

    scale = lax.fori_loop(0, m // mtile, start, jnp.float32(0.0))

    def refine(full):
        def step(t, acc):
            rows = pl.ds(pl.multiple_of(t * mtile, mtile), mtile)
            u = u_ref[rows]
            if full:
                left = v_ref[rows] - dot_full(u, k_ref[...])
                u_ref[rows] = u + dot_full(left, xf_ref[...])
            else:
                left = v_ref[rows] - dot_three(split(u, 2), (kh_ref[...], kl_ref[...]))
                u_ref[rows] = u + dot(left.astype(BF), x_ref[...])
            return acc + jnp.sum(left * left)

        return lax.fori_loop(0, m // mtile, step, jnp.float32(0.0))

    def unfinished(state):
        k, left = state
        return (left > 1e-7 * scale) & (left < 0.1 * scale) & (k < 12)

    done, left = lax.while_loop(
        unfinished, lambda s: (s[0] + 1, refine(False)), (jnp.int32(1), refine(False))
    )

    @pl.when(jnp.logical_not(left <= 1e-7 * scale))
    def _():
        def rows_of(t):
            return pl.ds(pl.multiple_of(t * 128, 128), 128)

        def highest(t, acc):
            return jnp.maximum(acc, jnp.max(jnp.sum(jnp.abs(k_ref[rows_of(t)]), axis=1, keepdims=True)))

        peak = lax.fori_loop(0, n // 128, highest, jnp.float32(0.0))

        def begin(t, carry):
            xf_ref[rows_of(t)] = eye(t, 128) / peak
            return carry

        lax.fori_loop(0, n // 128, begin, 0)

        def newton(state):
            k, _ = state

            def residual(t, acc):
                rows = rows_of(t)
                new = eye(t, 128) - dot_full(xf_ref[rows], k_ref[...])
                rf_ref[rows] = new
                return acc + jnp.sum(new * new)

            size = lax.fori_loop(0, n // 128, residual, jnp.float32(0.0))
            for t in range(n // 128):
                r_t = slice(t * 128, (t + 1) * 128)
                rf_ref[n + t * 128 : n + (t + 1) * 128] = xf_ref[r_t]

            def update(t, carry):
                rows = rows_of(t)
                xf_ref[rows] = xf_ref[rows] + dot_full(rf_ref[rows], rf_ref[n : 2 * n])
                return carry

            lax.fori_loop(0, n // 128, update, 0)
            return k + 1, size

        lax.while_loop(
            lambda s: (s[1] > 1e-5) & (s[0] < 80), newton, (jnp.int32(0), jnp.float32(1.0) * n)
        )

        def again(t, carry):
            rows = pl.ds(pl.multiple_of(t * mtile, mtile), mtile)
            u_ref[rows] = dot_full(v_ref[rows], xf_ref[...])
            return carry

        lax.fori_loop(0, m // mtile, again, 0)
        refine(True)
        refine(True)


def solve_scratch(n, m):
    return [
        pltpu.VMEM((n, n), F32),
        pltpu.VMEM((m, n), F32),
        pltpu.VMEM((m, n), F32),
        pltpu.VMEM((n, n), BF),
        pltpu.VMEM((2, n, n), BF),
        pltpu.VMEM((n, n), F32),
        pltpu.VMEM((2 * n, n), F32),
        pltpu.VMEM((n, n), BF),
        pltpu.VMEM((n, n), BF),
    ]


def column(row):
    eye = iota((F, F), 0) == iota((F, F), 1)
    spread = jnp.where(eye, row.astype(F32), 0.0)
    return jnp.sum(spread, axis=1, keepdims=True).astype(jnp.int32)


def permute_cols(x, perm_row):
    hot = (iota((F, F), 0) == perm_row).astype(BF)
    return sum(dot(part, hot) for part in split(x, 3))


def from_second(rows):
    return (iota((rows, 1), 0) & 7) >= 4


def level_one_kernel(sc, kg, perm_row, x1, inv, y1, f1, k, v, u, x, r, xf, rf, kh, kl):
    natural(v, 0, kg, sc, N)
    hot = (column(perm_row[...]) == iota((F, F), 1)).astype(BF)
    turned = sum(dot(hot, part) for part in split(v[...], 3))
    u[...] = permute_cols(turned, perm_row[...])
    natural(k, 0, kg, sc, 0)
    k[...] = k[...] + u[...]
    row, cols, norm = scaled(k, F)
    v[...] = (iota((F, F), 0) == iota((F, F), 1)).astype(F32)
    solve_right(k, v, u, x, r, xf, rf, kh, kl, F, norm)
    for t in range(F // 128):
        rows = slice(t * 128, (t + 1) * 128)
        inv[rows] = u[rows] * cols[t] * row
    inverse = split(inv[...], 2)
    points = x1[...]
    points = jnp.where(from_second(8 * N), permute_cols(points, perm_row[...]), points)
    y1[...] = dot_three(split(points, 2), inverse)
    lane = iota((16, F), 1)
    sub = iota((16, F), 0)
    pick = ((lane == sub + sc[1] * N) & (sub < N)).astype(BF)
    f1[...] = sum(dot(pick, part) for part in split(inv[...], 3))


def level_two_kernel(sc, kg, perm_row, inv, x2, y1, f1, pv, wt, sf2, st):
    natural(st, 0, kg, sc, 0, 0, False)
    natural(st, F, kg, sc, 0, F, False)
    st[F:] = permute_cols(st[F:], perm_row[...])
    natural(wt, 0, kg, sc, N, 0, False)
    natural(wt, F, kg, sc, N, F, False)
    inverse = split(inv[...], 2)
    second = split(st[...], 2)
    for t in range(2):
        rows = slice(t * F, (t + 1) * F)
        other = slice((1 - t) * F, (2 - t) * F)
        base = wt[rows]
        w = dot_three([part[rows] for part in second], inverse)
        wt[rows] = w
        part = dot_three(split(w, 2), second, dot_t)
        pv[rows, rows] = base - part[:, rows]
        pv[rows, other] = -part[:, other]
    part = dot_three(split(y1[...], 2), second, dot_t)
    late = from_second(8 * N)
    n = 2 * F
    pv[n : n + 96, :F] = jnp.where(late, 0.0, x2[...]) - part[:, :F]
    pv[n : n + 96, F:] = jnp.where(late, x2[...], 0.0) - part[:, F:]
    sf2[...] = -dot_three(split(f1[...], 2), second, dot_t)


def couple_kernel(sc, pv, other, wt, y1, f1, perm_row, target, cc, k, v, u, x, r, xf, rf, kh, kl):
    n = 2 * F
    for t in range(6):
        rows = slice(t * 128, (t + 1) * 128)
        k[rows] = pv[rows] + other[rows]
    row, _, norm = scaled(k, n)
    lane = iota((16, n), 1)
    sub = iota((16, n), 0)
    for h, source in enumerate((pv, other)):
        half = sc[0] if h == 0 else 1 - sc[0]
        pick = ((lane == half * F + sc[1] * N + sub) & (sub < N)).astype(F32)
        base = h * 128
        v[base : base + 96] = source[n : n + 96] * row
        v[base + 96 : base + 112] = pick * row
        v[base + 112 : base + 128] = jnp.zeros((16, n), F32)
    solve_right(k, v, u, x, r, xf, rf, kh, kl, n, norm)
    u2 = u[...] * row
    u[...] = -u2
    k[:256, :F] = dot_three(split(u2, 2), split(wt[...], 2))
    k[:96, :F] = k[:96, :F] - y1[...]
    k[108:120, :F] = k[108:120, :F] - f1[:N]
    for b in range(2):
        y, x_at = ((target[2 * b + i : 2 * b + i + 1] + (1 - b) * sc[2 + i]) & 3 for i in range(2))
        lanes = target[4:5] + N * (4 * y + x_at)
        keys = iota((n, 1), 0)
        if b == 1:
            keys = jnp.concatenate([column(perm_row[...]), keys[F:]], axis=0)
        hot = (keys == lanes).astype(BF)
        coef = jnp.concatenate([k[:256, :F], u[:, b * F : (b + 1) * F]], axis=1)
        high, low = split(coef, 2)
        cc[b] = dot(jnp.concatenate([high, low], axis=0), hot).astype(BF)


WIDE = 512


def product_kernel(cc, g0, g1, g2, g3, dl, own, part):
    block = jnp.concatenate([g[...].reshape(F // 2, WIDE) for g in (g0, g1, g2, g3)], axis=0)
    high, low = split(block, 2)
    both = dot(cc[0], high)
    acc = both[:256] + (both[256:] + dot(cc[0, :256], low))
    own[:96] = acc[:96] + dl[...]
    own[96:] = acc[96:128]
    part[...] = acc[128:240]


def product(b, cc, g, dl):
    steps = 4 * F // WIDE
    if b == 0:
        blocks = [pl.BlockSpec((4, 2, 2 * N, WIDE), lambda j: (0, 0, 0, j))] * 4
    else:
        blocks = [
            pl.BlockSpec((1, 4, 2, 2 * N, WIDE), lambda j, y=y: (y, 0, 0, 0, j)) for y in range(4)
        ]
    return pl.pallas_call(
        product_kernel,
        grid=(steps,),
        in_specs=[
            pl.BlockSpec((1, 512, 2 * F), lambda j: (b, 0, 0)),
        ]
        + blocks
        + [
            pl.BlockSpec((8 * N, WIDE), lambda j: (0, b * steps + j)),
        ],
        out_specs=[
            pl.BlockSpec((128, WIDE), lambda j: (0, j)),
            pl.BlockSpec((112, WIDE), lambda j: (0, j)),
        ],
        out_shape=[
            jax.ShapeDtypeStruct((128, 4 * F), F32),
            jax.ShapeDtypeStruct((112, 4 * F), F32),
        ],
        compiler_params=LIMIT,
        cost_estimate=pl.CostEstimate(flops=4 * 10**9, bytes_accessed=10**7, transcendentals=0),
    )(cc, *g, dl)


def finish_kernel(sc, own_a, own_b, other_a, other_b, sf2, sf, ss, mm):
    wide = 4 * F
    for h in range(2):
        @pl.when(sc[0] == h)
        def _():
            for b, (own, other) in enumerate(((own_a, other_a), (own_b, other_b))):
                near = slice((2 * h + b) * wide, (2 * h + b + 1) * wide)
                far = slice((2 - 2 * h + b) * wide, (3 - 2 * h + b) * wide)
                for i in range(N):
                    mm[i, :, near] = own[8 * i : 8 * i + 8]
                    mm[i, :, far] = other[8 * i : 8 * i + 8]
                    ss[i, :, near] = own[96 + i : 97 + i]
                    ss[i, :, far] = other[96 + i : 97 + i]
                    row = own[108 + i : 109 + i]
                    at = 5 * b * F
                    sf[i, :, at : at + F] = row[:, :F]
                    outer, inner = (at + F, at + 2 * F) if h == 0 else (at + 2 * F, at + F)
                    sf[i, :, outer : outer + F] = row[:, F : 2 * F]
                    sf[i, :, inner : inner + F] = sf2[i : i + 1, b * F : (b + 1) * F]
                    sf[i, :, at + 3 * F : at + 5 * F] = row[:, 2 * F :]


def swap(x, axis):
    return lax.ppermute(x, axis, [(0, 1), (1, 0)])


def beside(x, axis):
    return [x] + [lax.ppermute(x, axis, [(i, (i + k) % 4) for i in range(4)]) for k in (1, 3, 2)]


def body(dtn, interface_perm):
    half = lax.axis_index("core")
    spots = [lax.axis_index(name) for name in ("z_hi", "y", "x")]
    row = (spots[0] * 4 + spots[1]) * 4 + spots[2]
    sc = jnp.stack([half, row] + spots[1:]).astype(jnp.int32)
    perm_row = interface_perm
    ks, ga, x1, x2, dl = pack(sc, dtn.transpose(1, 2, 0, 3))
    low = lax.axis_index("z_hi") == 0

    def both_planes(x, other):
        return jnp.stack([jnp.where(low, x, other), jnp.where(low, other, x)])

    across = swap(ks, "z_hi")
    cuts = (slice(0, 2 * F), slice(2 * F, 3 * F), slice(3 * F, 7 * F))
    z2, z1, zb = (both_planes(ks[:, cut], across[:, cut]) for cut in cuts)
    g_b = lax.all_gather(zb, ("y", "x")).reshape(4, 4, 2, 2 * N, 4 * F)
    k1 = beside(z1, "x")
    k2 = beside(z2, "y")
    ga, k1, k2 = lax.optimization_barrier((ga, k1, k2))
    k1g = jnp.stack(beside(jnp.stack(k1), "y"))
    k2g = jnp.stack(beside(jnp.stack(k2), "x"))
    line = jnp.stack(beside(both_planes(ga, swap(ga, "z_hi")), "x"))
    k2g, line = lax.optimization_barrier((k2g, line))
    g_a = beside(line, "y")
    inv, y1, f1 = level_one(sc, k1g, perm_row, x1)
    pv, wt, sf2 = level_two(sc, k2g, perm_row, inv, x2, y1, f1)
    paired = swap(pv, "core")
    (cc,) = couple(sc, pv, paired, wt, y1, f1, perm_row)
    own_a, part_a = product(0, cc, g_a, dl)
    arrived_a = swap(part_a, "core")
    own_b, part_b = product(1, cc, [g_b] * 4, dl)
    arrived_b = swap(part_b, "core")
    sf, ss, mm = finish(sc, own_a, own_b, arrived_a, arrived_b, sf2)
    return sf.transpose(1, 0, 2), ss.transpose(1, 0, 2), mm[None].transpose(0, 2, 1, 3)


def pack(*operands):
    return call(
        pack_kernel,
        [
            ((2 * N, 7 * F), F32),
            ((2 * N, 4 * F), F32),
            ((8 * N, F), F32),
            ((8 * N, F), F32),
            ((8 * N, 8 * F), F32),
        ],
        operands,
        smem=(0,),
    )


def level_one(*operands):
    return call(
        level_one_kernel,
        [((F, F), F32), ((8 * N, F), F32), ((16, F), F32)],
        operands,
        smem=(0,),
        scratch=solve_scratch(F, F),
        flops=10 * 10**9,
    )


def level_two(*operands):
    return call(
        level_two_kernel,
        [((864, 2 * F), F32), ((2 * F, F), F32), ((16, 2 * F), F32)],
        operands,
        smem=(0,),
        scratch=[pltpu.VMEM((2 * F, F), F32)],
        flops=5 * 10**9,
    )


def couple(*operands):
    shape = (4, 4, 2, 2, N)
    ring = np.array([0, -1, 1, 2])
    rest = np.arange(2)[:, None, None] * (PLANE * N) + np.arange(2)[:, None] * F + np.arange(N)
    tables = [order.reshape(s) for order in (ring, np.arange(4)) for s in ((4, 1, 1, 1, 1), (1, 4, 1, 1, 1))]
    tables.append(rest)
    target = np.stack([np.broadcast_to(t, shape).reshape(-1) for t in tables])
    return call(
        couple_kernel,
        [((2, 512, 2 * F), BF)],
        operands + (jnp.asarray(target, jnp.int32),),
        smem=(0,),
        scratch=solve_scratch(2 * F, 256),
        flops=20 * 10**9,
    )


def finish(*operands):
    return call(
        finish_kernel,
        [((N, 1, 10 * F), F32), ((N, 1, 16 * F), F32), ((N, 8, 16 * F), F32)],
        operands,
        smem=(0,),
    )


def solution(mesh):
    split_mesh = jax.sharding.Mesh(
        mesh.devices.reshape(-1, 2, 2, 4, 4), ("z_lo", "core", "z_hi", "y", "x")
    )
    pair, rows = ("z_lo", "core"), ("z_hi", "y", "x")
    return jax.shard_map(
        body,
        mesh=split_mesh,
        in_specs=(P(pair, None, rows, None), P(pair, None)),
        out_specs=(P(pair, rows, None), P(pair, rows, None), P(pair, None, rows, None)),
        check_vma=False,
    )
```

```python
import functools

import jax
import jax.numpy as jnp
import numpy as np
from jax import lax
from jax.experimental import pallas as pl
from jax.experimental.pallas import tpu as pltpu
from jax.sharding import PartitionSpec as P

F = 384
N = 12
ROWS = 32
PLANE = 16
BF = jnp.bfloat16
F32 = jnp.float32
LIMIT = pltpu.CompilerParams(vmem_limit_bytes=56 * 1024 * 1024)
VMEM = pl.BlockSpec(memory_space=pltpu.VMEM)
SMEM = pl.BlockSpec(memory_space=pltpu.SMEM)


def call(kernel, outs, operands, smem=(), scratch=(), flops=10**9):
    return pl.pallas_call(
        kernel,
        out_shape=[jax.ShapeDtypeStruct(s, d) for s, d in outs],
        in_specs=[SMEM if i in smem else VMEM for i in range(len(operands))],
        out_specs=[VMEM] * len(outs),
        scratch_shapes=list(scratch),
        compiler_params=LIMIT,
        cost_estimate=pl.CostEstimate(flops=flops, bytes_accessed=10**6, transcendentals=0),
    )(*operands)


def dot(a, b):
    return jnp.dot(a, b, preferred_element_type=F32)


def dot_full(a, b):
    return jnp.dot(a, b, preferred_element_type=F32, precision=lax.Precision.HIGHEST)


def dot_t(a, b):
    return lax.dot_general(a, b, (((1,), (1,)), ((), ())), preferred_element_type=F32)


def dot_three(a, b, kernel=dot):
    (ah, al), (bh, bl) = a, b
    m = ah.shape[0]
    both = kernel(jnp.concatenate([ah, al], axis=0), bh)
    return both[:m] + (both[m:] + kernel(ah, bl))


def split(x, parts):
    out = []
    for _ in range(parts):
        top = x.astype(BF)
        out.append(top)
        x = x - top.astype(F32)
    return out


def iota(shape, dim):
    return lax.broadcasted_iota(jnp.int32, shape, dim)


def pack_kernel(sc, dtn, ks, gs, x1, x2, dl):
    even = sc[0] == 0
    empty = jnp.zeros((4, 4 * F), F32)

    def two_thirds(row, at):
        x, y, z = (row[:, k * 128 : (k + 1) * 128] for k in range(3))
        early, late = at < 128, at >= 256
        first = jnp.where(early, x, jnp.where(late, z, y))
        then = jnp.where(early, y, jnp.where(late, x, z))
        return jnp.concatenate([first, then], axis=1)

    for i in range(N):
        one, two, block = [], [], []
        for b in range(2):
            i1 = 1 - b

            def second(rows):
                return jnp.where(even, rows[:, 3 * F : 4 * F], rows[:, 2 * F : 3 * F])

            def others(rows):
                mid = jnp.where(even, rows[:, 2 * F : 3 * F], rows[:, 3 * F : 4 * F])
                return jnp.concatenate([rows[:, b * F : (b + 1) * F], mid, rows[:, 4 * F :]], axis=1)

            face = [dtn[f, i, b : b + 1] for f in range(6)]
            row_one = face[i1]
            row_two = jnp.where(even, face[3], face[2])
            middle = jnp.where(even, face[2], face[3])
            outer = jnp.concatenate([face[b], middle, face[4], face[5]], axis=0)
            cols = slice(i1 * F, (i1 + 1) * F)
            gs[b, i : i + 1] = others(row_one)
            gs[b, N + i : N + i + 1] = others(row_two)
            point = sc[1] * N + i
            at = b * N + i
            ks[at : at + 1, :F] = row_two[:, cols]
            ks[at : at + 1, F : F + 256] = two_thirds(second(row_two), point)
            ks[at : at + 1, F + 256 :] = two_thirds(row_one[:, cols], point)
            one.append(outer[:, cols])
            two.append(second(outer))
            block.append(others(outer))
        rows = slice(8 * i, 8 * i + 8)
        x1[rows] = jnp.concatenate(one, axis=0)
        x2[rows] = jnp.concatenate(two, axis=0)
        dl[rows, : 4 * F] = jnp.concatenate([block[0], empty], axis=0)
        dl[rows, 4 * F :] = jnp.concatenate([empty, block[1]], axis=0)


def place(distance):
    return jnp.where(distance == 0, 0, jnp.where(distance == 3, 1, distance + 1))


def natural(dst, base, src, sc, offset, col=0, width=F, y_first=True):
    ys = [place((y + 4 - sc[2]) & 3) for y in range(4)]
    xs = [place((x + 4 - sc[3]) & 3) for x in range(4)]
    for z in range(2):
        for q in range(PLANE):
            at = base + (z * PLANE + q) * N
            y, x = ys[q // 4], xs[q % 4]
            first, then = (y, x) if y_first else (x, y)
            dst[at : at + N, :width] = src[first, then, z, offset : offset + N, col : col + width]


def complete(ref, base):
    for a in range(3):
        b, c = (a + 1) % 3, (a + 2) % 3
        rows = slice(base + a * 128, base + (a + 1) * 128)
        own = ref[rows, :128]
        yield rows, a, own, b, ref[rows, 128:256], c, ref[base + c * 128 : base + (c + 1) * 128, 128:256].T


def symmetric(ref, base=0):
    parts = list(complete(ref, base))
    for rows, *pieces in parts:
        for at, block in zip(pieces[::2], pieces[1::2]):
            ref[rows, at * 128 : (at + 1) * 128] = block


def scaled(k_ref, n):
    eye = iota((128, 128), 0) == iota((128, 128), 1)
    row, cols = [], []
    for t in range(n // 128):
        rows = slice(t * 128, (t + 1) * 128)
        diag = jnp.where(eye, k_ref[rows, rows], 0.0)
        row.append(jnp.sum(diag, axis=0, keepdims=True))
        cols.append(lax.rsqrt(jnp.sum(diag, axis=1, keepdims=True)))
    row = lax.rsqrt(jnp.concatenate(row, axis=1))
    norm = jnp.zeros((8, n), F32)
    for t in range(n // 128):
        rows = slice(t * 128, (t + 1) * 128)
        part = k_ref[rows] * cols[t] * row
        k_ref[rows] = part
        norm = norm + jnp.sum((part * part).reshape(16, 8, n), axis=0)
    return row, cols, jnp.sum(norm)


TILE = 384
MTILE = 384


def solve_right(k_ref, v_ref, u_ref, x_ref, r_ref, xf_ref, rf_ref, kh_ref, kl_ref, n, norm):
    tile = TILE
    count = n // tile
    m = v_ref.shape[0]
    mtile = min(m, MTILE)
    alpha = n / norm

    def eye(t, width):
        return (iota((width, n), 0) + t * width == iota((width, n), 1)).astype(F32)

    for t in range(count):
        rows = slice(t * tile, (t + 1) * tile)
        e = eye(t, tile)
        part = k_ref[rows]
        kh_ref[rows], kl_ref[rows] = split(part, 2)
        first = e - alpha * part
        r_ref[0, rows] = first.astype(BF)
        x_ref[rows] = (alpha * (e + first)).astype(BF)

    def square(src, dst, with_x):
        def step(t, acc):
            rows = pl.ds(pl.multiple_of(t * tile, tile), tile)
            left = r_ref[src, rows]
            if with_x:
                old = x_ref[rows]
                both = dot(jnp.concatenate([left, old], axis=0), r_ref[src])
                new = both[:tile]
                x_ref[rows] = (old.astype(F32) + both[tile:]).astype(BF)
            else:
                new = dot(left, r_ref[src])
            r_ref[dst, rows] = new.astype(BF)
            return acc + jnp.sum(new * new)

        return lax.fori_loop(0, count, step, jnp.float32(0.0))

    def advance(src):
        def step(t, carry):
            rows = pl.ds(pl.multiple_of(t * tile, tile), tile)
            old = x_ref[rows]
            x_ref[rows] = (old.astype(F32) + dot(old, r_ref[src])).astype(BF)
            return carry

        lax.fori_loop(0, count, step, 0)

    size = square(0, 1, False)

    def more(state):
        k, size = state
        return (size > 0.003 * n) & (k < 12)

    def iterate(state):
        k, _ = state
        src = (k + 1) % 2
        return k + 1, square(src, k % 2, True)

    k, _ = lax.while_loop(more, iterate, (jnp.int32(0), size))
    advance((k + 1) % 2)

    def start(t, acc):
        rows = pl.ds(pl.multiple_of(t * mtile, mtile), mtile)
        v = v_ref[rows]
        u_ref[rows] = dot(v.astype(BF), x_ref[...])
        return acc + jnp.sum(v * v)

    scale = lax.fori_loop(0, m // mtile, start, jnp.float32(0.0))

    def refine(full):
        def step(t, acc):
            rows = pl.ds(pl.multiple_of(t * mtile, mtile), mtile)
            u = u_ref[rows]
            if full:
                left = v_ref[rows] - dot_full(u, k_ref[...])
                u_ref[rows] = u + dot_full(left, xf_ref[...])
            else:
                left = v_ref[rows] - dot_three(split(u, 2), (kh_ref[...], kl_ref[...]))
                u_ref[rows] = u + dot(left.astype(BF), x_ref[...])
            return acc + jnp.sum(left * left)

        return lax.fori_loop(0, m // mtile, step, jnp.float32(0.0))

    def unfinished(state):
        k, left = state
        return (left > 1e-7 * scale) & (left < 0.1 * scale) & (k < 12)

    done, left = lax.while_loop(
        unfinished, lambda s: (s[0] + 1, refine(False)), (jnp.int32(1), refine(False))
    )

    @pl.when(jnp.logical_not(left <= 1e-7 * scale))
    def _():
        def rows_of(t):
            return pl.ds(pl.multiple_of(t * 128, 128), 128)

        def highest(t, acc):
            return jnp.maximum(acc, jnp.max(jnp.sum(jnp.abs(k_ref[rows_of(t)]), axis=1, keepdims=True)))

        peak = lax.fori_loop(0, n // 128, highest, jnp.float32(0.0))

        def begin(t, carry):
            xf_ref[rows_of(t)] = eye(t, 128) / peak
            return carry

        lax.fori_loop(0, n // 128, begin, 0)

        def newton(state):
            k, _ = state

            def residual(t, acc):
                rows = rows_of(t)
                new = eye(t, 128) - dot_full(xf_ref[rows], k_ref[...])
                rf_ref[rows] = new
                return acc + jnp.sum(new * new)

            size = lax.fori_loop(0, n // 128, residual, jnp.float32(0.0))
            for t in range(n // 128):
                r_t = slice(t * 128, (t + 1) * 128)
                rf_ref[n + t * 128 : n + (t + 1) * 128] = xf_ref[r_t]

            def update(t, carry):
                rows = rows_of(t)
                xf_ref[rows] = xf_ref[rows] + dot_full(rf_ref[rows], rf_ref[n : 2 * n])
                return carry

            lax.fori_loop(0, n // 128, update, 0)
            return k + 1, size

        lax.while_loop(
            lambda s: (s[1] > 1e-5) & (s[0] < 80), newton, (jnp.int32(0), jnp.float32(1.0) * n)
        )

        def again(t, carry):
            rows = pl.ds(pl.multiple_of(t * mtile, mtile), mtile)
            u_ref[rows] = dot_full(v_ref[rows], xf_ref[...])
            return carry

        lax.fori_loop(0, m // mtile, again, 0)
        refine(True)
        refine(True)


def solve_scratch(n, m):
    return [
        pltpu.VMEM((n, n), F32),
        pltpu.VMEM((m, n), F32),
        pltpu.VMEM((m, n), F32),
        pltpu.VMEM((n, n), BF),
        pltpu.VMEM((2, n, n), BF),
        pltpu.VMEM((n, n), F32),
        pltpu.VMEM((2 * n, n), F32),
        pltpu.VMEM((n, n), BF),
        pltpu.VMEM((n, n), BF),
    ]


def column(row):
    eye = iota((F, F), 0) == iota((F, F), 1)
    spread = jnp.where(eye, row.astype(F32), 0.0)
    return jnp.sum(spread, axis=1, keepdims=True).astype(jnp.int32)


def permute_cols(x, perm_row):
    hot = (iota((F, F), 0) == perm_row).astype(BF)
    return sum(dot(part, hot) for part in split(x, 3))


def from_second(rows):
    return (iota((rows, 1), 0) & 7) >= 4


def level_one_kernel(sc, kg, perm_row, x1, inv, y1, f1, k, v, u, x, r, xf, rf, kh, kl):
    natural(v, 0, kg, sc, N, 0, 256)
    symmetric(v)
    hot = (column(perm_row[...]) == iota((F, F), 1)).astype(BF)
    turned = sum(dot(hot, part) for part in split(v[...], 3))
    u[...] = permute_cols(turned, perm_row[...])
    natural(k, 0, kg, sc, 0, 0, 256)
    symmetric(k)
    k[...] = k[...] + u[...]
    row, cols, norm = scaled(k, F)
    v[...] = (iota((F, F), 0) == iota((F, F), 1)).astype(F32)
    solve_right(k, v, u, x, r, xf, rf, kh, kl, F, norm)
    for t in range(F // 128):
        rows = slice(t * 128, (t + 1) * 128)
        inv[rows] = u[rows] * cols[t] * row
    inverse = split(inv[...], 2)
    points = x1[...]
    points = jnp.where(from_second(8 * N), permute_cols(points, perm_row[...]), points)
    y1[...] = dot_three(split(points, 2), inverse)
    lane = iota((16, F), 1)
    sub = iota((16, F), 0)
    pick = ((lane == sub + sc[1] * N) & (sub < N)).astype(BF)
    f1[...] = sum(dot(pick, part) for part in split(inv[...], 3))


def level_two_kernel(sc, kg, perm_row, inv, x2, y1, f1, pv, wt, sf2, st):
    for b in range(2):
        natural(st, b * F, kg, sc, b * N, 0, F, False)
        natural(wt, b * F, kg, sc, b * N, F, 256, False)
        symmetric(wt, b * F)
    st[F:] = permute_cols(st[F:], perm_row[...])
    inverse = split(inv[...], 2)
    second = split(st[...], 2)
    for t in range(2):
        rows = slice(t * F, (t + 1) * F)
        other = slice((1 - t) * F, (2 - t) * F)
        base = wt[rows]
        w = dot_three([part[rows] for part in second], inverse)
        wt[rows] = w
        part = dot_three(split(w, 2), second, dot_t)
        pv[rows, rows] = base - part[:, rows]
        pv[rows, other] = -part[:, other]
    part = dot_three(split(y1[...], 2), second, dot_t)
    late = from_second(8 * N)
    n = 2 * F
    pv[n : n + 96, :F] = jnp.where(late, 0.0, x2[...]) - part[:, :F]
    pv[n : n + 96, F:] = jnp.where(late, x2[...], 0.0) - part[:, F:]
    sf2[...] = -dot_three(split(f1[...], 2), second, dot_t)


def couple_kernel(sc, pv, other, wt, y1, f1, perm_row, target, cc, k, v, u, x, r, xf, rf, kh, kl):
    n = 2 * F
    for t in range(6):
        rows = slice(t * 128, (t + 1) * 128)
        k[rows] = pv[rows] + other[rows]
    row, _, norm = scaled(k, n)
    lane = iota((16, n), 1)
    sub = iota((16, n), 0)
    for h, source in enumerate((pv, other)):
        half = sc[0] if h == 0 else 1 - sc[0]
        pick = ((lane == half * F + sc[1] * N + sub) & (sub < N)).astype(F32)
        base = h * 128
        v[base : base + 96] = source[n : n + 96] * row
        v[base + 96 : base + 112] = pick * row
        v[base + 112 : base + 128] = jnp.zeros((16, n), F32)
    solve_right(k, v, u, x, r, xf, rf, kh, kl, n, norm)
    u2 = u[...] * row
    u[...] = -u2
    k[:256, :F] = dot_three(split(u2, 2), split(wt[...], 2))
    k[:96, :F] = k[:96, :F] - y1[...]
    k[108:120, :F] = k[108:120, :F] - f1[:N]
    lanes = target[...]
    for b in range(2):
        keys = iota((n, 1), 0)
        if b == 1:
            keys = jnp.concatenate([column(perm_row[...]), keys[F:]], axis=0)
        hot = (keys == lanes).astype(BF)
        coef = jnp.concatenate([k[:256, :F], u[:, b * F : (b + 1) * F]], axis=1)
        high, low = split(coef, 2)
        cc[b] = dot(jnp.concatenate([high, low], axis=0), hot).astype(BF)


WIDE = 512


def product_kernel(cc, g, dl, own, part):
    block = g[...].reshape(2 * F, WIDE)
    high, low = split(block, 2)
    both = dot(cc[0], high)
    acc = both[:256] + (both[256:] + dot(cc[0, :256], low))
    own[:96] = acc[:96] + dl[...]
    own[96:] = acc[96:128]
    part[...] = acc[128:240]


def product(b, cc, g, dl):
    steps = 4 * F // WIDE
    return pl.pallas_call(
        product_kernel,
        grid=(steps,),
        in_specs=[
            pl.BlockSpec((1, 512, 2 * F), lambda j: (b, 0, 0)),
            pl.BlockSpec((ROWS, 1, 2 * N, WIDE), lambda j: (0, b, 0, j)),
            pl.BlockSpec((8 * N, WIDE), lambda j: (0, b * steps + j)),
        ],
        out_specs=[
            pl.BlockSpec((128, WIDE), lambda j: (0, j)),
            pl.BlockSpec((112, WIDE), lambda j: (0, j)),
        ],
        out_shape=[
            jax.ShapeDtypeStruct((128, 4 * F), F32),
            jax.ShapeDtypeStruct((112, 4 * F), F32),
        ],
        compiler_params=LIMIT,
        cost_estimate=pl.CostEstimate(flops=4 * 10**9, bytes_accessed=10**7, transcendentals=0),
    )(cc, g, dl)


def finish_kernel(sc, own_a, own_b, other_a, other_b, sf2, sf, ss, mm):
    wide = 4 * F
    for h in range(2):
        @pl.when(sc[0] == h)
        def _():
            for b, (own, other) in enumerate(((own_a, other_a), (own_b, other_b))):
                near = slice((2 * h + b) * wide, (2 * h + b + 1) * wide)
                far = slice((2 - 2 * h + b) * wide, (3 - 2 * h + b) * wide)
                for i in range(N):
                    mm[i, :, near] = own[8 * i : 8 * i + 8]
                    mm[i, :, far] = other[8 * i : 8 * i + 8]
                    ss[i, :, near] = own[96 + i : 97 + i]
                    ss[i, :, far] = other[96 + i : 97 + i]
                    row = own[108 + i : 109 + i]
                    at = 5 * b * F
                    sf[i, :, at : at + F] = row[:, :F]
                    outer, inner = (at + F, at + 2 * F) if h == 0 else (at + 2 * F, at + F)
                    sf[i, :, outer : outer + F] = row[:, F : 2 * F]
                    sf[i, :, inner : inner + F] = sf2[i : i + 1, b * F : (b + 1) * F]
                    sf[i, :, at + 3 * F : at + 5 * F] = row[:, 2 * F :]


PLANE_AXES = ("y", "x")


def swap(x, axis):
    return lax.ppermute(x, axis, [(0, 1), (1, 0)])


def around(x, axis):
    return jnp.stack(
        [x] + [lax.ppermute(x, axis, [(i, (i + k) % 4) for i in range(4)]) for k in (1, 3, 2)]
    )


def body(dtn, interface_perm):
    half = lax.axis_index("core")
    spots = [lax.axis_index(name) for name in ("z_hi", "y", "x")]
    row = (spots[0] * 4 + spots[1]) * 4 + spots[2]
    sc = jnp.stack([half, row] + spots[1:]).astype(jnp.int32)
    perm_row = interface_perm
    ks, gs, x1, x2, dl = pack(sc, dtn.transpose(1, 2, 0, 3))
    low = lax.axis_index("z_hi") == 0

    def both_planes(x, other):
        return jnp.stack([jnp.where(low, x, other), jnp.where(low, other, x)])

    kz = both_planes(ks, swap(ks, "z_hi"))
    gs, kz = lax.optimization_barrier((gs, kz))
    across = swap(gs, "z_hi")
    k1 = around(kz[..., F + 256 :], "x")
    k2 = around(kz[..., : F + 256], "y")
    across, k1, k2 = lax.optimization_barrier((across, k1, k2))
    k1g = around(k1, "y")
    k2g = around(k2, "x")
    g = lax.all_gather(both_planes(gs, across), PLANE_AXES)
    g = g.reshape(ROWS, 2, 2 * N, 4 * F)
    inv, y1, f1 = level_one(sc, k1g, perm_row, x1)
    pv, wt, sf2 = level_two(sc, k2g, perm_row, inv, x2, y1, f1)
    paired = swap(pv, "core")
    (cc,) = couple(sc, pv, paired, wt, y1, f1, perm_row)
    own_a, part_a = product(0, cc, g, dl)
    arrived_a = swap(part_a, "core")
    own_b, part_b = product(1, cc, g, dl)
    arrived_b = swap(part_b, "core")
    sf, ss, mm = finish(sc, own_a, own_b, arrived_a, arrived_b, sf2)
    return sf.transpose(1, 0, 2), ss.transpose(1, 0, 2), mm[None].transpose(0, 2, 1, 3)


def pack(*operands):
    return call(
        pack_kernel,
        [
            ((2 * N, F + 512), F32),
            ((2, 2 * N, 4 * F), F32),
            ((8 * N, F), F32),
            ((8 * N, F), F32),
            ((8 * N, 8 * F), F32),
        ],
        operands,
        smem=(0,),
    )


def level_one(*operands):
    return call(
        level_one_kernel,
        [((F, F), F32), ((8 * N, F), F32), ((16, F), F32)],
        operands,
        smem=(0,),
        scratch=solve_scratch(F, F),
        flops=10 * 10**9,
    )


def level_two(*operands):
    return call(
        level_two_kernel,
        [((864, 2 * F), F32), ((2 * F, F), F32), ((16, 2 * F), F32)],
        operands,
        smem=(0,),
        scratch=[pltpu.VMEM((2 * F, F), F32)],
        flops=5 * 10**9,
    )


def couple(*operands):
    natural_row = np.arange(F).reshape(2, PLANE, N).transpose(1, 0, 2)
    target = np.stack([natural_row, natural_row + F], axis=2).reshape(1, 2 * F)
    return call(
        couple_kernel,
        [((2, 512, 2 * F), BF)],
        operands + (jnp.asarray(target, jnp.int32),),
        smem=(0,),
        scratch=solve_scratch(2 * F, 256),
        flops=20 * 10**9,
    )


def finish(*operands):
    return call(
        finish_kernel,
        [((N, 1, 10 * F), F32), ((N, 1, 16 * F), F32), ((N, 8, 16 * F), F32)],
        operands,
        smem=(0,),
    )


def solution(mesh):
    split_mesh = jax.sharding.Mesh(
        mesh.devices.reshape(-1, 2, 2, 4, 4), ("z_lo", "core", "z_hi", "y", "x")
    )
    pair, rows = ("z_lo", "core"), ("z_hi", "y", "x")
    return jax.shard_map(
        body,
        mesh=split_mesh,
        in_specs=(P(pair, None, rows, None), P(pair, None)),
        out_specs=(P(pair, rows, None), P(pair, rows, None), P(pair, None, rows, None)),
        check_vma=False,
    )
```

```python
import functools

import jax
import jax.numpy as jnp
import numpy as np
from jax import lax
from jax.experimental import pallas as pl
from jax.experimental.pallas import tpu as pltpu
from jax.sharding import PartitionSpec as P

F = 384
N = 12
ROWS = 32
PLANE = 16
BF = jnp.bfloat16
F32 = jnp.float32
LIMIT = pltpu.CompilerParams(vmem_limit_bytes=56 * 1024 * 1024)
VMEM = pl.BlockSpec(memory_space=pltpu.VMEM)
SMEM = pl.BlockSpec(memory_space=pltpu.SMEM)


def call(kernel, outs, operands, smem=(), scratch=(), flops=10**9):
    return pl.pallas_call(
        kernel,
        out_shape=[jax.ShapeDtypeStruct(s, d) for s, d in outs],
        in_specs=[SMEM if i in smem else VMEM for i in range(len(operands))],
        out_specs=[VMEM] * len(outs),
        scratch_shapes=list(scratch),
        compiler_params=LIMIT,
        cost_estimate=pl.CostEstimate(flops=flops, bytes_accessed=10**6, transcendentals=0),
    )(*operands)


def dot(a, b):
    return jnp.dot(a, b, preferred_element_type=F32)


def dot_full(a, b):
    return jnp.dot(a, b, preferred_element_type=F32, precision=lax.Precision.HIGHEST)


def dot_t(a, b):
    return lax.dot_general(a, b, (((1,), (1,)), ((), ())), preferred_element_type=F32)


def dot_three(a, b, kernel=dot):
    (ah, al), (bh, bl) = a, b
    m = ah.shape[0]
    both = kernel(jnp.concatenate([ah, al], axis=0), bh)
    return both[:m] + (both[m:] + kernel(ah, bl))


def split(x, parts):
    out = []
    for _ in range(parts):
        top = x.astype(BF)
        out.append(top)
        x = x - top.astype(F32)
    return out


def iota(shape, dim):
    return lax.broadcasted_iota(jnp.int32, shape, dim)


def pack_kernel(sc, dtn, ks, x1, x2, dl):
    even = sc[0] == 0
    empty = jnp.zeros((4, 4 * F), F32)

    def two_thirds(row, at):
        x, y, z = (row[:, k * 128 : (k + 1) * 128] for k in range(3))
        early, late = at < 128, at >= 256
        first = jnp.where(early, x, jnp.where(late, z, y))
        then = jnp.where(early, y, jnp.where(late, x, z))
        return jnp.concatenate([first, then], axis=1)

    for i in range(N):
        one, two, block = [], [], []
        for b in range(2):
            i1 = 1 - b

            def second(rows):
                return jnp.where(even, rows[:, 3 * F : 4 * F], rows[:, 2 * F : 3 * F])

            def others(rows):
                mid = jnp.where(even, rows[:, 2 * F : 3 * F], rows[:, 3 * F : 4 * F])
                return jnp.concatenate([rows[:, b * F : (b + 1) * F], mid, rows[:, 4 * F :]], axis=1)

            face = [dtn[f, i, b : b + 1] for f in range(6)]
            row_one = face[i1]
            row_two = jnp.where(even, face[3], face[2])
            middle = jnp.where(even, face[2], face[3])
            outer = jnp.concatenate([face[b], middle, face[4], face[5]], axis=0)
            cols = slice(i1 * F, (i1 + 1) * F)
            at = F + 512 + 4 * b * F
            ks[i : i + 1, at : at + 4 * F] = others(row_one)
            ks[N + i : N + i + 1, at : at + 4 * F] = others(row_two)
            point = sc[1] * N + i
            at = b * N + i
            ks[at : at + 1, :F] = row_two[:, cols]
            ks[at : at + 1, F : F + 256] = two_thirds(second(row_two), point)
            ks[at : at + 1, F + 256 : F + 512] = two_thirds(row_one[:, cols], point)
            one.append(outer[:, cols])
            two.append(second(outer))
            block.append(others(outer))
        rows = slice(8 * i, 8 * i + 8)
        x1[rows] = jnp.concatenate(one, axis=0)
        x2[rows] = jnp.concatenate(two, axis=0)
        dl[rows, : 4 * F] = jnp.concatenate([block[0], empty], axis=0)
        dl[rows, 4 * F :] = jnp.concatenate([empty, block[1]], axis=0)


def place(distance):
    return jnp.where(distance == 0, 0, jnp.where(distance == 3, 1, distance + 1))


def natural(dst, base, src, sc, offset, col=0, width=F, y_first=True):
    ys = [place((y + 4 - sc[2]) & 3) for y in range(4)]
    xs = [place((x + 4 - sc[3]) & 3) for x in range(4)]
    for z in range(2):
        for q in range(PLANE):
            at = base + (z * PLANE + q) * N
            y, x = ys[q // 4], xs[q % 4]
            first, then = (y, x) if y_first else (x, y)
            dst[at : at + N, :width] = src[first, then, z, offset : offset + N, col : col + width]


def complete(ref, base):
    for a in range(3):
        b, c = (a + 1) % 3, (a + 2) % 3
        rows = slice(base + a * 128, base + (a + 1) * 128)
        own = ref[rows, :128]
        yield rows, a, own, b, ref[rows, 128:256], c, ref[base + c * 128 : base + (c + 1) * 128, 128:256].T


def symmetric(ref, base=0):
    parts = list(complete(ref, base))
    for rows, *pieces in parts:
        for at, block in zip(pieces[::2], pieces[1::2]):
            ref[rows, at * 128 : (at + 1) * 128] = block


def scaled(k_ref, n):
    eye = iota((128, 128), 0) == iota((128, 128), 1)
    row, cols = [], []
    for t in range(n // 128):
        rows = slice(t * 128, (t + 1) * 128)
        diag = jnp.where(eye, k_ref[rows, rows], 0.0)
        row.append(jnp.sum(diag, axis=0, keepdims=True))
        cols.append(lax.rsqrt(jnp.sum(diag, axis=1, keepdims=True)))
    row = lax.rsqrt(jnp.concatenate(row, axis=1))
    norm = jnp.zeros((8, n), F32)
    for t in range(n // 128):
        rows = slice(t * 128, (t + 1) * 128)
        part = k_ref[rows] * cols[t] * row
        k_ref[rows] = part
        norm = norm + jnp.sum((part * part).reshape(16, 8, n), axis=0)
    return row, cols, jnp.sum(norm)


TILE = 384
MTILE = 384


def solve_right(k_ref, v_ref, u_ref, x_ref, r_ref, xf_ref, rf_ref, kh_ref, kl_ref, n, norm):
    tile = TILE
    count = n // tile
    m = v_ref.shape[0]
    mtile = min(m, MTILE)
    alpha = n / norm

    def eye(t, width):
        return (iota((width, n), 0) + t * width == iota((width, n), 1)).astype(F32)

    for t in range(count):
        rows = slice(t * tile, (t + 1) * tile)
        e = eye(t, tile)
        part = k_ref[rows]
        kh_ref[rows], kl_ref[rows] = split(part, 2)
        first = e - alpha * part
        r_ref[0, rows] = first.astype(BF)
        x_ref[rows] = (alpha * (e + first)).astype(BF)

    def square(src, dst, with_x):
        def step(t, acc):
            rows = pl.ds(pl.multiple_of(t * tile, tile), tile)
            left = r_ref[src, rows]
            if with_x:
                old = x_ref[rows]
                both = dot(jnp.concatenate([left, old], axis=0), r_ref[src])
                new = both[:tile]
                x_ref[rows] = (old.astype(F32) + both[tile:]).astype(BF)
            else:
                new = dot(left, r_ref[src])
            r_ref[dst, rows] = new.astype(BF)
            return acc + jnp.sum(new * new)

        return lax.fori_loop(0, count, step, jnp.float32(0.0))

    def advance(src):
        def step(t, carry):
            rows = pl.ds(pl.multiple_of(t * tile, tile), tile)
            old = x_ref[rows]
            x_ref[rows] = (old.astype(F32) + dot(old, r_ref[src])).astype(BF)
            return carry

        lax.fori_loop(0, count, step, 0)

    size = square(0, 1, False)

    def more(state):
        k, size = state
        return (size > 0.003 * n) & (k < 12)

    def iterate(state):
        k, _ = state
        src = (k + 1) % 2
        return k + 1, square(src, k % 2, True)

    k, _ = lax.while_loop(more, iterate, (jnp.int32(0), size))
    advance((k + 1) % 2)

    def start(t, acc):
        rows = pl.ds(pl.multiple_of(t * mtile, mtile), mtile)
        v = v_ref[rows]
        u_ref[rows] = dot(v.astype(BF), x_ref[...])
        return acc + jnp.sum(v * v)

    scale = lax.fori_loop(0, m // mtile, start, jnp.float32(0.0))

    def refine(full):
        def step(t, acc):
            rows = pl.ds(pl.multiple_of(t * mtile, mtile), mtile)
            u = u_ref[rows]
            if full:
                left = v_ref[rows] - dot_full(u, k_ref[...])
                u_ref[rows] = u + dot_full(left, xf_ref[...])
            else:
                left = v_ref[rows] - dot_three(split(u, 2), (kh_ref[...], kl_ref[...]))
                u_ref[rows] = u + dot(left.astype(BF), x_ref[...])
            return acc + jnp.sum(left * left)

        return lax.fori_loop(0, m // mtile, step, jnp.float32(0.0))

    def unfinished(state):
        k, left = state
        return (left > 1e-7 * scale) & (left < 0.1 * scale) & (k < 12)

    done, left = lax.while_loop(
        unfinished, lambda s: (s[0] + 1, refine(False)), (jnp.int32(1), refine(False))
    )

    @pl.when(jnp.logical_not(left <= 1e-7 * scale))
    def _():
        def rows_of(t):
            return pl.ds(pl.multiple_of(t * 128, 128), 128)

        def highest(t, acc):
            return jnp.maximum(acc, jnp.max(jnp.sum(jnp.abs(k_ref[rows_of(t)]), axis=1, keepdims=True)))

        peak = lax.fori_loop(0, n // 128, highest, jnp.float32(0.0))

        def begin(t, carry):
            xf_ref[rows_of(t)] = eye(t, 128) / peak
            return carry

        lax.fori_loop(0, n // 128, begin, 0)

        def newton(state):
            k, _ = state

            def residual(t, acc):
                rows = rows_of(t)
                new = eye(t, 128) - dot_full(xf_ref[rows], k_ref[...])
                rf_ref[rows] = new
                return acc + jnp.sum(new * new)

            size = lax.fori_loop(0, n // 128, residual, jnp.float32(0.0))
            for t in range(n // 128):
                r_t = slice(t * 128, (t + 1) * 128)
                rf_ref[n + t * 128 : n + (t + 1) * 128] = xf_ref[r_t]

            def update(t, carry):
                rows = rows_of(t)
                xf_ref[rows] = xf_ref[rows] + dot_full(rf_ref[rows], rf_ref[n : 2 * n])
                return carry

            lax.fori_loop(0, n // 128, update, 0)
            return k + 1, size

        lax.while_loop(
            lambda s: (s[1] > 1e-5) & (s[0] < 80), newton, (jnp.int32(0), jnp.float32(1.0) * n)
        )

        def again(t, carry):
            rows = pl.ds(pl.multiple_of(t * mtile, mtile), mtile)
            u_ref[rows] = dot_full(v_ref[rows], xf_ref[...])
            return carry

        lax.fori_loop(0, m // mtile, again, 0)
        refine(True)
        refine(True)


def solve_scratch(n, m):
    return [
        pltpu.VMEM((n, n), F32),
        pltpu.VMEM((m, n), F32),
        pltpu.VMEM((m, n), F32),
        pltpu.VMEM((n, n), BF),
        pltpu.VMEM((2, n, n), BF),
        pltpu.VMEM((n, n), F32),
        pltpu.VMEM((2 * n, n), F32),
        pltpu.VMEM((n, n), BF),
        pltpu.VMEM((n, n), BF),
    ]


def column(row):
    eye = iota((F, F), 0) == iota((F, F), 1)
    spread = jnp.where(eye, row.astype(F32), 0.0)
    return jnp.sum(spread, axis=1, keepdims=True).astype(jnp.int32)


def permute_cols(x, perm_row):
    hot = (iota((F, F), 0) == perm_row).astype(BF)
    return sum(dot(part, hot) for part in split(x, 3))


def from_second(rows):
    return (iota((rows, 1), 0) & 7) >= 4


def level_one_kernel(sc, kg, perm_row, x1, inv, y1, f1, k, v, u, x, r, xf, rf, kh, kl):
    natural(v, 0, kg, sc, N, 0, 256)
    symmetric(v)
    hot = (column(perm_row[...]) == iota((F, F), 1)).astype(BF)
    turned = sum(dot(hot, part) for part in split(v[...], 3))
    u[...] = permute_cols(turned, perm_row[...])
    natural(k, 0, kg, sc, 0, 0, 256)
    symmetric(k)
    k[...] = k[...] + u[...]
    row, cols, norm = scaled(k, F)
    v[...] = (iota((F, F), 0) == iota((F, F), 1)).astype(F32)
    solve_right(k, v, u, x, r, xf, rf, kh, kl, F, norm)
    for t in range(F // 128):
        rows = slice(t * 128, (t + 1) * 128)
        inv[rows] = u[rows] * cols[t] * row
    inverse = split(inv[...], 2)
    points = x1[...]
    points = jnp.where(from_second(8 * N), permute_cols(points, perm_row[...]), points)
    y1[...] = dot_three(split(points, 2), inverse)
    lane = iota((16, F), 1)
    sub = iota((16, F), 0)
    pick = ((lane == sub + sc[1] * N) & (sub < N)).astype(BF)
    f1[...] = sum(dot(pick, part) for part in split(inv[...], 3))


def level_two_kernel(sc, kg, perm_row, inv, x2, y1, f1, pv, wt, sf2, st):
    for b in range(2):
        natural(st, b * F, kg, sc, b * N, 0, F, False)
        natural(wt, b * F, kg, sc, b * N, F, 256, False)
        symmetric(wt, b * F)
    st[F:] = permute_cols(st[F:], perm_row[...])
    inverse = split(inv[...], 2)
    second = split(st[...], 2)
    for t in range(2):
        rows = slice(t * F, (t + 1) * F)
        other = slice((1 - t) * F, (2 - t) * F)
        base = wt[rows]
        w = dot_three([part[rows] for part in second], inverse)
        wt[rows] = w
        part = dot_three(split(w, 2), second, dot_t)
        pv[rows, rows] = base - part[:, rows]
        pv[rows, other] = -part[:, other]
    part = dot_three(split(y1[...], 2), second, dot_t)
    late = from_second(8 * N)
    n = 2 * F
    pv[n : n + 96, :F] = jnp.where(late, 0.0, x2[...]) - part[:, :F]
    pv[n : n + 96, F:] = jnp.where(late, x2[...], 0.0) - part[:, F:]
    sf2[...] = -dot_three(split(f1[...], 2), second, dot_t)


def couple_kernel(sc, pv, other, wt, y1, f1, perm_row, target, cc, k, v, u, x, r, xf, rf, kh, kl):
    n = 2 * F
    for t in range(6):
        rows = slice(t * 128, (t + 1) * 128)
        k[rows] = pv[rows] + other[rows]
    row, _, norm = scaled(k, n)
    lane = iota((16, n), 1)
    sub = iota((16, n), 0)
    for h, source in enumerate((pv, other)):
        half = sc[0] if h == 0 else 1 - sc[0]
        pick = ((lane == half * F + sc[1] * N + sub) & (sub < N)).astype(F32)
        base = h * 128
        v[base : base + 96] = source[n : n + 96] * row
        v[base + 96 : base + 112] = pick * row
        v[base + 112 : base + 128] = jnp.zeros((16, n), F32)
    solve_right(k, v, u, x, r, xf, rf, kh, kl, n, norm)
    u2 = u[...] * row
    u[...] = -u2
    k[:256, :F] = dot_three(split(u2, 2), split(wt[...], 2))
    k[:96, :F] = k[:96, :F] - y1[...]
    k[108:120, :F] = k[108:120, :F] - f1[:N]
    lanes = target[...]
    for b in range(2):
        keys = iota((n, 1), 0)
        if b == 1:
            keys = jnp.concatenate([column(perm_row[...]), keys[F:]], axis=0)
        hot = (keys == lanes).astype(BF)
        coef = jnp.concatenate([k[:256, :F], u[:, b * F : (b + 1) * F]], axis=1)
        high, low = split(coef, 2)
        cc[b] = dot(jnp.concatenate([high, low], axis=0), hot).astype(BF)


WIDE = 768


def product_kernel(cc, g, dl, own, part):
    block = g[...].reshape(2 * F, WIDE)
    high, low = split(block, 2)
    both = dot(cc[0], high)
    acc = both[:256] + (both[256:] + dot(cc[0, :256], low))
    own[:96] = acc[:96] + dl[...]
    own[96:] = acc[96:128]
    part[...] = acc[128:240]


def product(b, cc, g, dl):
    steps = 4 * F // WIDE
    return pl.pallas_call(
        product_kernel,
        grid=(steps,),
        in_specs=[
            pl.BlockSpec((1, 512, 2 * F), lambda j: (b, 0, 0)),
            pl.BlockSpec((ROWS, 1, 2 * N, WIDE), lambda j: (0, b, 0, j)),
            pl.BlockSpec((8 * N, WIDE), lambda j: (0, b * steps + j)),
        ],
        out_specs=[
            pl.BlockSpec((128, WIDE), lambda j: (0, j)),
            pl.BlockSpec((112, WIDE), lambda j: (0, j)),
        ],
        out_shape=[
            jax.ShapeDtypeStruct((128, 4 * F), F32),
            jax.ShapeDtypeStruct((112, 4 * F), F32),
        ],
        compiler_params=LIMIT,
        cost_estimate=pl.CostEstimate(flops=4 * 10**9, bytes_accessed=10**7, transcendentals=0),
    )(cc, g, dl)


def finish_kernel(sc, own_a, own_b, other_a, other_b, sf2, sf, ss, mm):
    wide = 4 * F
    for h in range(2):
        @pl.when(sc[0] == h)
        def _():
            for b, (own, other) in enumerate(((own_a, other_a), (own_b, other_b))):
                near = slice((2 * h + b) * wide, (2 * h + b + 1) * wide)
                far = slice((2 - 2 * h + b) * wide, (3 - 2 * h + b) * wide)
                for i in range(N):
                    mm[i, :, near] = own[8 * i : 8 * i + 8]
                    mm[i, :, far] = other[8 * i : 8 * i + 8]
                    ss[i, :, near] = own[96 + i : 97 + i]
                    ss[i, :, far] = other[96 + i : 97 + i]
                    row = own[108 + i : 109 + i]
                    at = 5 * b * F
                    sf[i, :, at : at + F] = row[:, :F]
                    outer, inner = (at + F, at + 2 * F) if h == 0 else (at + 2 * F, at + F)
                    sf[i, :, outer : outer + F] = row[:, F : 2 * F]
                    sf[i, :, inner : inner + F] = sf2[i : i + 1, b * F : (b + 1) * F]
                    sf[i, :, at + 3 * F : at + 5 * F] = row[:, 2 * F :]


PLANE_AXES = ("y", "x")


def swap(x, axis):
    return lax.ppermute(x, axis, [(0, 1), (1, 0)])


def around(x, axis):
    return jnp.stack(
        [x] + [lax.ppermute(x, axis, [(i, (i + k) % 4) for i in range(4)]) for k in (1, 3, 2)]
    )


def body(dtn, interface_perm):
    half = lax.axis_index("core")
    spots = [lax.axis_index(name) for name in ("z_hi", "y", "x")]
    row = (spots[0] * 4 + spots[1]) * 4 + spots[2]
    sc = jnp.stack([half, row] + spots[1:]).astype(jnp.int32)
    perm_row = interface_perm
    ks, x1, x2, dl = pack(sc, dtn.transpose(1, 2, 0, 3))
    low = lax.axis_index("z_hi") == 0

    across = swap(ks, "z_hi")

    def both_planes(left, right):
        x, other = ks[:, left:right], across[:, left:right]
        return jnp.stack([jnp.where(low, x, other), jnp.where(low, other, x)])

    begin = F + 512
    rest = jnp.stack([both_planes(begin + 4 * b * F, begin + 4 * (b + 1) * F) for b in range(2)], axis=1)
    g = lax.all_gather(rest, PLANE_AXES).reshape(ROWS, 2, 2 * N, 4 * F)
    k1g = around(around(both_planes(F + 256, begin), "x"), "y")
    k2g = around(around(both_planes(0, F + 256), "y"), "x")
    inv, y1, f1 = level_one(sc, k1g, perm_row, x1)
    pv, wt, sf2 = level_two(sc, k2g, perm_row, inv, x2, y1, f1)
    paired = swap(pv, "core")
    (cc,) = couple(sc, pv, paired, wt, y1, f1, perm_row)
    own_a, part_a = product(0, cc, g, dl)
    arrived_a = swap(part_a, "core")
    own_b, part_b = product(1, cc, g, dl)
    arrived_b = swap(part_b, "core")
    sf, ss, mm = finish(sc, own_a, own_b, arrived_a, arrived_b, sf2)
    return sf.transpose(1, 0, 2), ss.transpose(1, 0, 2), mm[None].transpose(0, 2, 1, 3)


def pack(*operands):
    return call(
        pack_kernel,
        [
            ((2 * N, 9 * F + 512), F32),
            ((8 * N, F), F32),
            ((8 * N, F), F32),
            ((8 * N, 8 * F), F32),
        ],
        operands,
        smem=(0,),
    )


def level_one(*operands):
    return call(
        level_one_kernel,
        [((F, F), F32), ((8 * N, F), F32), ((16, F), F32)],
        operands,
        smem=(0,),
        scratch=solve_scratch(F, F),
        flops=10 * 10**9,
    )


def level_two(*operands):
    return call(
        level_two_kernel,
        [((864, 2 * F), F32), ((2 * F, F), F32), ((16, 2 * F), F32)],
        operands,
        smem=(0,),
        scratch=[pltpu.VMEM((2 * F, F), F32)],
        flops=5 * 10**9,
    )


def couple(*operands):
    natural_row = np.arange(F).reshape(2, PLANE, N).transpose(1, 0, 2)
    target = np.stack([natural_row, natural_row + F], axis=2).reshape(1, 2 * F)
    return call(
        couple_kernel,
        [((2, 512, 2 * F), BF)],
        operands + (jnp.asarray(target, jnp.int32),),
        smem=(0,),
        scratch=solve_scratch(2 * F, 256),
        flops=20 * 10**9,
    )


def finish(*operands):
    return call(
        finish_kernel,
        [((N, 1, 10 * F), F32), ((N, 1, 16 * F), F32), ((N, 8, 16 * F), F32)],
        operands,
        smem=(0,),
    )


def solution(mesh):
    split_mesh = jax.sharding.Mesh(
        mesh.devices.reshape(-1, 2, 2, 4, 4), ("z_lo", "core", "z_hi", "y", "x")
    )
    pair, rows = ("z_lo", "core"), ("z_hi", "y", "x")
    return jax.shard_map(
        body,
        mesh=split_mesh,
        in_specs=(P(pair, None, rows, None), P(pair, None)),
        out_specs=(P(pair, rows, None), P(pair, rows, None), P(pair, None, rows, None)),
        check_vma=False,
    )
```

```python
import functools

import jax
import jax.numpy as jnp
import numpy as np
from jax import lax
from jax.experimental import pallas as pl
from jax.experimental.pallas import tpu as pltpu
from jax.sharding import PartitionSpec as P

F = 384
N = 12
ROWS = 32
PLANE = 16
BF = jnp.bfloat16
F32 = jnp.float32
LIMIT = pltpu.CompilerParams(vmem_limit_bytes=56 * 1024 * 1024)
VMEM = pl.BlockSpec(memory_space=pltpu.VMEM)
SMEM = pl.BlockSpec(memory_space=pltpu.SMEM)


def call(kernel, outs, operands, smem=(), scratch=(), flops=10**9):
    return pl.pallas_call(
        kernel,
        out_shape=[jax.ShapeDtypeStruct(s, d) for s, d in outs],
        in_specs=[SMEM if i in smem else VMEM for i in range(len(operands))],
        out_specs=[VMEM] * len(outs),
        scratch_shapes=list(scratch),
        compiler_params=LIMIT,
        cost_estimate=pl.CostEstimate(flops=flops, bytes_accessed=10**6, transcendentals=0),
    )(*operands)


def dot(a, b):
    return jnp.dot(a, b, preferred_element_type=F32)


def dot_full(a, b):
    return jnp.dot(a, b, preferred_element_type=F32, precision=lax.Precision.HIGHEST)


def dot_t(a, b):
    return lax.dot_general(a, b, (((1,), (1,)), ((), ())), preferred_element_type=F32)


def dot_three(a, b, kernel=dot):
    (ah, al), (bh, bl) = a, b
    m = ah.shape[0]
    both = kernel(jnp.concatenate([ah, al], axis=0), bh)
    return both[:m] + (both[m:] + kernel(ah, bl))


def split(x, parts):
    out = []
    for _ in range(parts):
        top = x.astype(BF)
        out.append(top)
        x = x - top.astype(F32)
    return out


def iota(shape, dim):
    return lax.broadcasted_iota(jnp.int32, shape, dim)


def chosen(even, face, rows):
    low, high = (rows[:, k * F : (k + 1) * F] for k in face)
    return jnp.where(even, high, low), jnp.where(even, low, high)


def pack_first_kernel(sc, dtn, ks):
    even = sc[0] == 0

    def two_thirds(row, at):
        x, y, z = (row[:, k * 128 : (k + 1) * 128] for k in range(3))
        early, late = at < 128, at >= 256
        first = jnp.where(early, x, jnp.where(late, z, y))
        then = jnp.where(early, y, jnp.where(late, x, z))
        return jnp.concatenate([first, then], axis=1)

    for i in range(N):
        point = sc[1] * N + i
        for b in range(2):
            i1 = 1 - b
            cols = slice(i1 * F, (i1 + 1) * F)
            row_one = dtn[i1, i, b : b + 1]
            row_two = jnp.where(even, dtn[3, i, b : b + 1], dtn[2, i, b : b + 1])
            at = b * N + i
            ks[at : at + 1, :F] = row_two[:, cols]
            ks[at : at + 1, F : F + 256] = two_thirds(chosen(even, (2, 3), row_two)[0], point)
            ks[at : at + 1, F + 256 :] = two_thirds(row_one[:, cols], point)


def pack_kernel(sc, dtn, gs, x1, x2, dl):
    even = sc[0] == 0
    empty = jnp.zeros((4, 4 * F), F32)
    for i in range(N):
        one, two, block = [], [], []
        for b in range(2):
            i1 = 1 - b

            def others(rows):
                mid = chosen(even, (2, 3), rows)[1]
                return jnp.concatenate([rows[:, b * F : (b + 1) * F], mid, rows[:, 4 * F :]], axis=1)

            face = [dtn[f, i, b : b + 1] for f in range(6)]
            row_two = jnp.where(even, face[3], face[2])
            middle = jnp.where(even, face[2], face[3])
            outer = jnp.concatenate([face[b], middle, face[4], face[5]], axis=0)
            gs[b, i : i + 1] = others(face[i1])
            gs[b, N + i : N + i + 1] = others(row_two)
            one.append(outer[:, i1 * F : (i1 + 1) * F])
            two.append(chosen(even, (2, 3), outer)[0])
            block.append(others(outer))
        rows = slice(8 * i, 8 * i + 8)
        x1[rows] = jnp.concatenate(one, axis=0)
        x2[rows] = jnp.concatenate(two, axis=0)
        dl[rows, : 4 * F] = jnp.concatenate([block[0], empty], axis=0)
        dl[rows, 4 * F :] = jnp.concatenate([empty, block[1]], axis=0)


def place(distance):
    return jnp.where(distance == 0, 0, jnp.where(distance == 3, 1, distance + 1))


def natural(dst, base, src, sc, offset, col=0, width=F):
    ys = [place((y + 4 - sc[2]) & 3) for y in range(4)]
    xs = [place((x + 4 - sc[3]) & 3) for x in range(4)]
    for z in range(2):
        for q in range(PLANE):
            at = base + (z * PLANE + q) * N
            y, x = ys[q // 4], xs[q % 4]
            dst[at : at + N, :width] = src[y, x, z, offset : offset + N, col : col + width]


def complete(ref, base):
    for a in range(3):
        b, c = (a + 1) % 3, (a + 2) % 3
        rows = slice(base + a * 128, base + (a + 1) * 128)
        own = ref[rows, :128]
        yield rows, a, own, b, ref[rows, 128:256], c, ref[base + c * 128 : base + (c + 1) * 128, 128:256].T


def symmetric(ref, base=0):
    parts = list(complete(ref, base))
    for rows, *pieces in parts:
        for at, block in zip(pieces[::2], pieces[1::2]):
            ref[rows, at * 128 : (at + 1) * 128] = block


def scaled(k_ref, n):
    eye = iota((128, 128), 0) == iota((128, 128), 1)
    row, cols = [], []
    for t in range(n // 128):
        rows = slice(t * 128, (t + 1) * 128)
        diag = jnp.where(eye, k_ref[rows, rows], 0.0)
        row.append(jnp.sum(diag, axis=0, keepdims=True))
        cols.append(lax.rsqrt(jnp.sum(diag, axis=1, keepdims=True)))
    row = lax.rsqrt(jnp.concatenate(row, axis=1))
    norm = jnp.zeros((8, n), F32)
    for t in range(n // 128):
        rows = slice(t * 128, (t + 1) * 128)
        part = k_ref[rows] * cols[t] * row
        k_ref[rows] = part
        norm = norm + jnp.sum((part * part).reshape(16, 8, n), axis=0)
    return row, cols, jnp.sum(norm)


TILE = 384
MTILE = 384


def solve_right(k_ref, v_ref, u_ref, x_ref, r_ref, xf_ref, rf_ref, kh_ref, kl_ref, n, norm):
    tile = TILE
    count = n // tile
    m = v_ref.shape[0]
    mtile = min(m, MTILE)
    alpha = n / norm

    def eye(t, width):
        return (iota((width, n), 0) + t * width == iota((width, n), 1)).astype(F32)

    for t in range(count):
        rows = slice(t * tile, (t + 1) * tile)
        e = eye(t, tile)
        part = k_ref[rows]
        kh_ref[rows], kl_ref[rows] = split(part, 2)
        first = e - alpha * part
        r_ref[0, rows] = first.astype(BF)
        x_ref[rows] = (alpha * (e + first)).astype(BF)

    def square(src, dst, with_x):
        def step(t, acc):
            rows = pl.ds(pl.multiple_of(t * tile, tile), tile)
            left = r_ref[src, rows]
            if with_x:
                old = x_ref[rows]
                both = dot(jnp.concatenate([left, old], axis=0), r_ref[src])
                new = both[:tile]
                x_ref[rows] = (old.astype(F32) + both[tile:]).astype(BF)
            else:
                new = dot(left, r_ref[src])
            r_ref[dst, rows] = new.astype(BF)
            return acc + jnp.sum(new * new)

        return lax.fori_loop(0, count, step, jnp.float32(0.0))

    def advance(src):
        def step(t, carry):
            rows = pl.ds(pl.multiple_of(t * tile, tile), tile)
            old = x_ref[rows]
            x_ref[rows] = (old.astype(F32) + dot(old, r_ref[src])).astype(BF)
            return carry

        lax.fori_loop(0, count, step, 0)

    size = square(0, 1, False)

    def more(state):
        k, size = state
        return (size > 0.003 * n) & (k < 12)

    def iterate(state):
        k, _ = state
        src = (k + 1) % 2
        return k + 1, square(src, k % 2, True)

    k, _ = lax.while_loop(more, iterate, (jnp.int32(0), size))
    advance((k + 1) % 2)

    def start(t, acc):
        rows = pl.ds(pl.multiple_of(t * mtile, mtile), mtile)
        v = v_ref[rows]
        u_ref[rows] = dot(v.astype(BF), x_ref[...])
        return acc + jnp.sum(v * v)

    scale = lax.fori_loop(0, m // mtile, start, jnp.float32(0.0))

    def refine(full):
        def step(t, acc):
            rows = pl.ds(pl.multiple_of(t * mtile, mtile), mtile)
            u = u_ref[rows]
            if full:
                left = v_ref[rows] - dot_full(u, k_ref[...])
                u_ref[rows] = u + dot_full(left, xf_ref[...])
            else:
                left = v_ref[rows] - dot_three(split(u, 2), (kh_ref[...], kl_ref[...]))
                u_ref[rows] = u + dot(left.astype(BF), x_ref[...])
            return acc + jnp.sum(left * left)

        return lax.fori_loop(0, m // mtile, step, jnp.float32(0.0))

    def unfinished(state):
        k, left = state
        return (left > 1e-7 * scale) & (left < 0.1 * scale) & (k < 12)

    done, left = lax.while_loop(
        unfinished, lambda s: (s[0] + 1, refine(False)), (jnp.int32(1), refine(False))
    )

    @pl.when(jnp.logical_not(left <= 1e-7 * scale))
    def _():
        def rows_of(t):
            return pl.ds(pl.multiple_of(t * 128, 128), 128)

        def highest(t, acc):
            return jnp.maximum(acc, jnp.max(jnp.sum(jnp.abs(k_ref[rows_of(t)]), axis=1, keepdims=True)))

        peak = lax.fori_loop(0, n // 128, highest, jnp.float32(0.0))

        def begin(t, carry):
            xf_ref[rows_of(t)] = eye(t, 128) / peak
            return carry

        lax.fori_loop(0, n // 128, begin, 0)

        def newton(state):
            k, _ = state

            def residual(t, acc):
                rows = rows_of(t)
                new = eye(t, 128) - dot_full(xf_ref[rows], k_ref[...])
                rf_ref[rows] = new
                return acc + jnp.sum(new * new)

            size = lax.fori_loop(0, n // 128, residual, jnp.float32(0.0))
            for t in range(n // 128):
                r_t = slice(t * 128, (t + 1) * 128)
                rf_ref[n + t * 128 : n + (t + 1) * 128] = xf_ref[r_t]

            def update(t, carry):
                rows = rows_of(t)
                xf_ref[rows] = xf_ref[rows] + dot_full(rf_ref[rows], rf_ref[n : 2 * n])
                return carry

            lax.fori_loop(0, n // 128, update, 0)
            return k + 1, size

        lax.while_loop(
            lambda s: (s[1] > 1e-5) & (s[0] < 80), newton, (jnp.int32(0), jnp.float32(1.0) * n)
        )

        def again(t, carry):
            rows = pl.ds(pl.multiple_of(t * mtile, mtile), mtile)
            u_ref[rows] = dot_full(v_ref[rows], xf_ref[...])
            return carry

        lax.fori_loop(0, m // mtile, again, 0)
        refine(True)
        refine(True)


def solve_scratch(n, m):
    return [
        pltpu.VMEM((n, n), F32),
        pltpu.VMEM((m, n), F32),
        pltpu.VMEM((m, n), F32),
        pltpu.VMEM((n, n), BF),
        pltpu.VMEM((2, n, n), BF),
        pltpu.VMEM((n, n), F32),
        pltpu.VMEM((2 * n, n), F32),
        pltpu.VMEM((n, n), BF),
        pltpu.VMEM((n, n), BF),
    ]


def column(row):
    eye = iota((F, F), 0) == iota((F, F), 1)
    spread = jnp.where(eye, row.astype(F32), 0.0)
    return jnp.sum(spread, axis=1, keepdims=True).astype(jnp.int32)


def permute_cols(x, perm_row):
    hot = (iota((F, F), 0) == perm_row).astype(BF)
    return sum(dot(part, hot) for part in split(x, 3))


def from_second(rows):
    return (iota((rows, 1), 0) & 7) >= 4


def level_one_kernel(sc, kg, perm_row, x1, inv, y1, f1, k, v, u, x, r, xf, rf, kh, kl):
    natural(v, 0, kg, sc, N, F + 256, 256)
    symmetric(v)
    hot = (column(perm_row[...]) == iota((F, F), 1)).astype(BF)
    turned = sum(dot(hot, part) for part in split(v[...], 3))
    u[...] = permute_cols(turned, perm_row[...])
    natural(k, 0, kg, sc, 0, F + 256, 256)
    symmetric(k)
    k[...] = k[...] + u[...]
    row, cols, norm = scaled(k, F)
    v[...] = (iota((F, F), 0) == iota((F, F), 1)).astype(F32)
    solve_right(k, v, u, x, r, xf, rf, kh, kl, F, norm)
    for t in range(F // 128):
        rows = slice(t * 128, (t + 1) * 128)
        inv[rows] = u[rows] * cols[t] * row
    inverse = split(inv[...], 2)
    points = x1[...]
    points = jnp.where(from_second(8 * N), permute_cols(points, perm_row[...]), points)
    y1[...] = dot_three(split(points, 2), inverse)
    lane = iota((16, F), 1)
    sub = iota((16, F), 0)
    pick = ((lane == sub + sc[1] * N) & (sub < N)).astype(BF)
    f1[...] = sum(dot(pick, part) for part in split(inv[...], 3))


def level_two_kernel(sc, kg, perm_row, inv, x2, y1, f1, pv, wt, sf2, st):
    for b in range(2):
        natural(st, b * F, kg, sc, b * N)
        natural(wt, b * F, kg, sc, b * N, F, 256)
        symmetric(wt, b * F)
    st[F:] = permute_cols(st[F:], perm_row[...])
    inverse = split(inv[...], 2)
    second = split(st[...], 2)
    for t in range(2):
        rows = slice(t * F, (t + 1) * F)
        other = slice((1 - t) * F, (2 - t) * F)
        base = wt[rows]
        w = dot_three([part[rows] for part in second], inverse)
        wt[rows] = w
        part = dot_three(split(w, 2), second, dot_t)
        pv[rows, rows] = base - part[:, rows]
        pv[rows, other] = -part[:, other]
    part = dot_three(split(y1[...], 2), second, dot_t)
    late = from_second(8 * N)
    n = 2 * F
    pv[n : n + 96, :F] = jnp.where(late, 0.0, x2[...]) - part[:, :F]
    pv[n : n + 96, F:] = jnp.where(late, x2[...], 0.0) - part[:, F:]
    sf2[...] = -dot_three(split(f1[...], 2), second, dot_t)


def couple_kernel(sc, pv, other, wt, y1, f1, perm_row, target, cc, k, v, u, x, r, xf, rf, kh, kl):
    n = 2 * F
    for t in range(6):
        rows = slice(t * 128, (t + 1) * 128)
        k[rows] = pv[rows] + other[rows]
    row, _, norm = scaled(k, n)
    lane = iota((16, n), 1)
    sub = iota((16, n), 0)
    for h, source in enumerate((pv, other)):
        half = sc[0] if h == 0 else 1 - sc[0]
        pick = ((lane == half * F + sc[1] * N + sub) & (sub < N)).astype(F32)
        base = h * 128
        v[base : base + 96] = source[n : n + 96] * row
        v[base + 96 : base + 112] = pick * row
        v[base + 112 : base + 128] = jnp.zeros((16, n), F32)
    solve_right(k, v, u, x, r, xf, rf, kh, kl, n, norm)
    u2 = u[...] * row
    u[...] = -u2
    k[:256, :F] = dot_three(split(u2, 2), split(wt[...], 2))
    k[:96, :F] = k[:96, :F] - y1[...]
    k[108:120, :F] = k[108:120, :F] - f1[:N]
    lanes = target[...]
    for b in range(2):
        keys = iota((n, 1), 0)
        if b == 1:
            keys = jnp.concatenate([column(perm_row[...]), keys[F:]], axis=0)
        hot = (keys == lanes).astype(BF)
        coef = jnp.concatenate([k[:256, :F], u[:, b * F : (b + 1) * F]], axis=1)
        high, low = split(coef, 2)
        cc[b] = dot(jnp.concatenate([high, low], axis=0), hot).astype(BF)


WIDE = 768


def product_kernel(cc, g, dl, own, part):
    block = g[...].reshape(2 * F, WIDE)
    high, low = split(block, 2)
    both = dot(cc[0], high)
    acc = both[:256] + (both[256:] + dot(cc[0, :256], low))
    own[:96] = acc[:96] + dl[...]
    own[96:] = acc[96:128]
    part[...] = acc[128:240]


def product(b, cc, g, dl):
    steps = 4 * F // WIDE
    return pl.pallas_call(
        product_kernel,
        grid=(steps,),
        in_specs=[
            pl.BlockSpec((1, 512, 2 * F), lambda j: (b, 0, 0)),
            pl.BlockSpec((ROWS, 1, 2 * N, WIDE), lambda j: (0, b, 0, j)),
            pl.BlockSpec((8 * N, WIDE), lambda j: (0, b * steps + j)),
        ],
        out_specs=[
            pl.BlockSpec((128, WIDE), lambda j: (0, j)),
            pl.BlockSpec((112, WIDE), lambda j: (0, j)),
        ],
        out_shape=[
            jax.ShapeDtypeStruct((128, 4 * F), F32),
            jax.ShapeDtypeStruct((112, 4 * F), F32),
        ],
        compiler_params=LIMIT,
        cost_estimate=pl.CostEstimate(flops=4 * 10**9, bytes_accessed=10**7, transcendentals=0),
    )(cc, g, dl)


def finish_kernel(sc, own_a, own_b, other_a, other_b, sf2, sf, ss, mm):
    wide = 4 * F
    for h in range(2):
        @pl.when(sc[0] == h)
        def _():
            for b, (own, other) in enumerate(((own_a, other_a), (own_b, other_b))):
                near = slice((2 * h + b) * wide, (2 * h + b + 1) * wide)
                far = slice((2 - 2 * h + b) * wide, (3 - 2 * h + b) * wide)
                for i in range(N):
                    mm[i, :, near] = own[8 * i : 8 * i + 8]
                    mm[i, :, far] = other[8 * i : 8 * i + 8]
                    ss[i, :, near] = own[96 + i : 97 + i]
                    ss[i, :, far] = other[96 + i : 97 + i]
                    row = own[108 + i : 109 + i]
                    at = 5 * b * F
                    sf[i, :, at : at + F] = row[:, :F]
                    outer, inner = (at + F, at + 2 * F) if h == 0 else (at + 2 * F, at + F)
                    sf[i, :, outer : outer + F] = row[:, F : 2 * F]
                    sf[i, :, inner : inner + F] = sf2[i : i + 1, b * F : (b + 1) * F]
                    sf[i, :, at + 3 * F : at + 5 * F] = row[:, 2 * F :]


PLANE_AXES = ("y", "x")


def swap(x, axis):
    return lax.ppermute(x, axis, [(0, 1), (1, 0)])


def around(x, axis):
    return jnp.stack(
        [x] + [lax.ppermute(x, axis, [(i, (i + k) % 4) for i in range(4)]) for k in (1, 3, 2)]
    )


def body(dtn, interface_perm):
    half = lax.axis_index("core")
    spots = [lax.axis_index(name) for name in ("z_hi", "y", "x")]
    row = (spots[0] * 4 + spots[1]) * 4 + spots[2]
    sc = jnp.stack([half, row] + spots[1:]).astype(jnp.int32)
    perm_row = interface_perm
    local = dtn.transpose(1, 2, 0, 3)
    (ks,) = pack_first(sc, local)
    gs, x1, x2, dl = pack(sc, local)
    low = lax.axis_index("z_hi") == 0

    def both_planes(x, other):
        return jnp.stack([jnp.where(low, x, other), jnp.where(low, other, x)])

    kz = both_planes(ks, swap(ks, "z_hi"))
    gs, kz = lax.optimization_barrier((gs, kz))
    across = swap(gs, "z_hi")
    kg = around(around(kz, "x"), "y")
    across, kg = lax.optimization_barrier((across, kg))
    g = lax.all_gather(both_planes(gs, across), PLANE_AXES)
    g = g.reshape(ROWS, 2, 2 * N, 4 * F)
    inv, y1, f1 = level_one(sc, kg, perm_row, x1)
    pv, wt, sf2 = level_two(sc, kg, perm_row, inv, x2, y1, f1)
    paired = swap(pv, "core")
    (cc,) = couple(sc, pv, paired, wt, y1, f1, perm_row)
    own_a, part_a = product(0, cc, g, dl)
    arrived_a = swap(part_a, "core")
    own_b, part_b = product(1, cc, g, dl)
    arrived_b = swap(part_b, "core")
    sf, ss, mm = finish(sc, own_a, own_b, arrived_a, arrived_b, sf2)
    return sf.transpose(1, 0, 2), ss.transpose(1, 0, 2), mm[None].transpose(0, 2, 1, 3)


def pack_first(*operands):
    return call(pack_first_kernel, [((2 * N, F + 512), F32)], operands, smem=(0,))


def pack(*operands):
    return call(
        pack_kernel,
        [
            ((2, 2 * N, 4 * F), F32),
            ((8 * N, F), F32),
            ((8 * N, F), F32),
            ((8 * N, 8 * F), F32),
        ],
        operands,
        smem=(0,),
    )


def level_one(*operands):
    return call(
        level_one_kernel,
        [((F, F), F32), ((8 * N, F), F32), ((16, F), F32)],
        operands,
        smem=(0,),
        scratch=solve_scratch(F, F),
        flops=10 * 10**9,
    )


def level_two(*operands):
    return call(
        level_two_kernel,
        [((864, 2 * F), F32), ((2 * F, F), F32), ((16, 2 * F), F32)],
        operands,
        smem=(0,),
        scratch=[pltpu.VMEM((2 * F, F), F32)],
        flops=5 * 10**9,
    )


def couple(*operands):
    natural_row = np.arange(F).reshape(2, PLANE, N).transpose(1, 0, 2)
    target = np.stack([natural_row, natural_row + F], axis=2).reshape(1, 2 * F)
    return call(
        couple_kernel,
        [((2, 512, 2 * F), BF)],
        operands + (jnp.asarray(target, jnp.int32),),
        smem=(0,),
        scratch=solve_scratch(2 * F, 256),
        flops=20 * 10**9,
    )


def finish(*operands):
    return call(
        finish_kernel,
        [((N, 1, 10 * F), F32), ((N, 1, 16 * F), F32), ((N, 8, 16 * F), F32)],
        operands,
        smem=(0,),
    )


def solution(mesh):
    split_mesh = jax.sharding.Mesh(
        mesh.devices.reshape(-1, 2, 2, 4, 4), ("z_lo", "core", "z_hi", "y", "x")
    )
    pair, rows = ("z_lo", "core"), ("z_hi", "y", "x")
    return jax.shard_map(
        body,
        mesh=split_mesh,
        in_specs=(P(pair, None, rows, None), P(pair, None)),
        out_specs=(P(pair, rows, None), P(pair, rows, None), P(pair, None, rows, None)),
        check_vma=False,
    )
```

```python
import functools

import jax
import jax.numpy as jnp
import numpy as np
from jax import lax
from jax.experimental import pallas as pl
from jax.experimental.pallas import tpu as pltpu
from jax.sharding import PartitionSpec as P

F = 384
N = 12
ROWS = 32
PLANE = 16
BF = jnp.bfloat16
F32 = jnp.float32
LIMIT = pltpu.CompilerParams(vmem_limit_bytes=56 * 1024 * 1024)
VMEM = pl.BlockSpec(memory_space=pltpu.VMEM)
SMEM = pl.BlockSpec(memory_space=pltpu.SMEM)


def call(kernel, outs, operands, smem=(), scratch=(), flops=10**9):
    return pl.pallas_call(
        kernel,
        out_shape=[jax.ShapeDtypeStruct(s, d) for s, d in outs],
        in_specs=[SMEM if i in smem else VMEM for i in range(len(operands))],
        out_specs=[VMEM] * len(outs),
        scratch_shapes=list(scratch),
        compiler_params=LIMIT,
        cost_estimate=pl.CostEstimate(flops=flops, bytes_accessed=10**6, transcendentals=0),
    )(*operands)


def dot(a, b):
    return jnp.dot(a, b, preferred_element_type=F32)


def dot_full(a, b):
    return jnp.dot(a, b, preferred_element_type=F32, precision=lax.Precision.HIGHEST)


def dot_t(a, b):
    return lax.dot_general(a, b, (((1,), (1,)), ((), ())), preferred_element_type=F32)


def dot_three(a, b, kernel=dot):
    (ah, al), (bh, bl) = a, b
    m = ah.shape[0]
    both = kernel(jnp.concatenate([ah, al], axis=0), bh)
    return both[:m] + (both[m:] + kernel(ah, bl))


def split(x, parts):
    out = []
    for _ in range(parts):
        top = x.astype(BF)
        out.append(top)
        x = x - top.astype(F32)
    return out


def iota(shape, dim):
    return lax.broadcasted_iota(jnp.int32, shape, dim)


def chosen(even, face, rows):
    low, high = (rows[:, k * F : (k + 1) * F] for k in face)
    return jnp.where(even, high, low), jnp.where(even, low, high)


def others(even, b, rows):
    mid = chosen(even, (2, 3), rows)[1]
    return jnp.concatenate([rows[:, b * F : (b + 1) * F], mid, rows[:, 4 * F :]], axis=1)


def pack_first_kernel(sc, dtn, ks):
    even = sc[0] == 0

    def two_thirds(row, at):
        x, y, z = (row[:, k * 128 : (k + 1) * 128] for k in range(3))
        early, late = at < 128, at >= 256
        first = jnp.where(early, x, jnp.where(late, z, y))
        then = jnp.where(early, y, jnp.where(late, x, z))
        return jnp.concatenate([first, then], axis=1)

    begin = F + 512
    for i in range(N):
        point = sc[1] * N + i
        for b in range(2):
            i1 = 1 - b
            cols = slice(i1 * F, (i1 + 1) * F)
            row_one = dtn[i1, i, b : b + 1]
            row_two = jnp.where(even, dtn[3, i, b : b + 1], dtn[2, i, b : b + 1])
            for k, row in enumerate((row_one, row_two)):
                at, left = k * N + i, begin + 4 * b * F
                ks[at : at + 1, left : left + 4 * F] = others(even, b, row)
            at = b * N + i
            ks[at : at + 1, :F] = row_two[:, cols]
            ks[at : at + 1, F : F + 256] = two_thirds(chosen(even, (2, 3), row_two)[0], point)
            ks[at : at + 1, F + 256 : begin] = two_thirds(row_one[:, cols], point)


def pack_kernel(sc, dtn, x1, x2, dl):
    even = sc[0] == 0
    empty = jnp.zeros((4, 4 * F), F32)
    for i in range(N):
        one, two, block = [], [], []
        for b in range(2):
            i1 = 1 - b

            face = [dtn[f, i, b : b + 1] for f in range(6)]
            middle = jnp.where(even, face[2], face[3])
            outer = jnp.concatenate([face[b], middle, face[4], face[5]], axis=0)
            one.append(outer[:, i1 * F : (i1 + 1) * F])
            two.append(chosen(even, (2, 3), outer)[0])
            block.append(others(even, b, outer))
        rows = slice(8 * i, 8 * i + 8)
        x1[rows] = jnp.concatenate(one, axis=0)
        x2[rows] = jnp.concatenate(two, axis=0)
        dl[rows, : 4 * F] = jnp.concatenate([block[0], empty], axis=0)
        dl[rows, 4 * F :] = jnp.concatenate([empty, block[1]], axis=0)


def place(distance):
    return jnp.where(distance == 0, 0, jnp.where(distance == 3, 1, distance + 1))


def natural(dst, base, src, sc, offset, col=0, width=F, y_first=True):
    ys = [place((y + 4 - sc[2]) & 3) for y in range(4)]
    xs = [place((x + 4 - sc[3]) & 3) for x in range(4)]
    for z in range(2):
        for q in range(PLANE):
            at = base + (z * PLANE + q) * N
            y, x = ys[q // 4], xs[q % 4]
            first, then = (y, x) if y_first else (x, y)
            dst[at : at + N, :width] = src[first, then, (z + sc[4]) & 1, offset : offset + N, col : col + width]


def complete(ref, base):
    for a in range(3):
        b, c = (a + 1) % 3, (a + 2) % 3
        rows = slice(base + a * 128, base + (a + 1) * 128)
        own = ref[rows, :128]
        yield rows, a, own, b, ref[rows, 128:256], c, ref[base + c * 128 : base + (c + 1) * 128, 128:256].T


def symmetric(ref, base=0):
    parts = list(complete(ref, base))
    for rows, *pieces in parts:
        for at, block in zip(pieces[::2], pieces[1::2]):
            ref[rows, at * 128 : (at + 1) * 128] = block


def scaled(k_ref, n):
    eye = iota((128, 128), 0) == iota((128, 128), 1)
    row, cols = [], []
    for t in range(n // 128):
        rows = slice(t * 128, (t + 1) * 128)
        diag = jnp.where(eye, k_ref[rows, rows], 0.0)
        row.append(jnp.sum(diag, axis=0, keepdims=True))
        cols.append(lax.rsqrt(jnp.sum(diag, axis=1, keepdims=True)))
    row = lax.rsqrt(jnp.concatenate(row, axis=1))
    norm = jnp.zeros((8, n), F32)
    for t in range(n // 128):
        rows = slice(t * 128, (t + 1) * 128)
        part = k_ref[rows] * cols[t] * row
        k_ref[rows] = part
        norm = norm + jnp.sum((part * part).reshape(16, 8, n), axis=0)
    return row, cols, jnp.sum(norm)


TILE = 384
MTILE = 384


def solve_right(k_ref, v_ref, u_ref, x_ref, r_ref, xf_ref, rf_ref, kh_ref, kl_ref, n, norm):
    tile = TILE
    count = n // tile
    m = v_ref.shape[0]
    mtile = min(m, MTILE)
    alpha = n / norm

    def eye(t, width):
        return (iota((width, n), 0) + t * width == iota((width, n), 1)).astype(F32)

    for t in range(count):
        rows = slice(t * tile, (t + 1) * tile)
        e = eye(t, tile)
        part = k_ref[rows]
        kh_ref[rows], kl_ref[rows] = split(part, 2)
        first = e - alpha * part
        r_ref[0, rows] = first.astype(BF)
        x_ref[rows] = (alpha * (e + first)).astype(BF)

    def square(src, dst, with_x):
        def step(t, acc):
            rows = pl.ds(pl.multiple_of(t * tile, tile), tile)
            left = r_ref[src, rows]
            if with_x:
                old = x_ref[rows]
                both = dot(jnp.concatenate([left, old], axis=0), r_ref[src])
                new = both[:tile]
                x_ref[rows] = (old.astype(F32) + both[tile:]).astype(BF)
            else:
                new = dot(left, r_ref[src])
            r_ref[dst, rows] = new.astype(BF)
            return acc + jnp.sum(new * new)

        return lax.fori_loop(0, count, step, jnp.float32(0.0))

    def advance(src):
        def step(t, carry):
            rows = pl.ds(pl.multiple_of(t * tile, tile), tile)
            old = x_ref[rows]
            x_ref[rows] = (old.astype(F32) + dot(old, r_ref[src])).astype(BF)
            return carry

        lax.fori_loop(0, count, step, 0)

    size = square(0, 1, False)

    def more(state):
        k, size = state
        return (size > 0.003 * n) & (k < 12)

    def iterate(state):
        k, _ = state
        src = (k + 1) % 2
        return k + 1, square(src, k % 2, True)

    k, _ = lax.while_loop(more, iterate, (jnp.int32(0), size))
    advance((k + 1) % 2)

    def start(t, acc):
        rows = pl.ds(pl.multiple_of(t * mtile, mtile), mtile)
        v = v_ref[rows]
        u_ref[rows] = dot(v.astype(BF), x_ref[...])
        return acc + jnp.sum(v * v)

    scale = lax.fori_loop(0, m // mtile, start, jnp.float32(0.0))

    def refine(full):
        def step(t, acc):
            rows = pl.ds(pl.multiple_of(t * mtile, mtile), mtile)
            u = u_ref[rows]
            if full:
                left = v_ref[rows] - dot_full(u, k_ref[...])
                u_ref[rows] = u + dot_full(left, xf_ref[...])
            else:
                left = v_ref[rows] - dot_three(split(u, 2), (kh_ref[...], kl_ref[...]))
                u_ref[rows] = u + dot(left.astype(BF), x_ref[...])
            return acc + jnp.sum(left * left)

        return lax.fori_loop(0, m // mtile, step, jnp.float32(0.0))

    def unfinished(state):
        k, left = state
        return (left > 1e-7 * scale) & (left < 0.1 * scale) & (k < 12)

    done, left = lax.while_loop(
        unfinished, lambda s: (s[0] + 1, refine(False)), (jnp.int32(1), refine(False))
    )

    @pl.when(jnp.logical_not(left <= 1e-7 * scale))
    def _():
        def rows_of(t):
            return pl.ds(pl.multiple_of(t * 128, 128), 128)

        def highest(t, acc):
            return jnp.maximum(acc, jnp.max(jnp.sum(jnp.abs(k_ref[rows_of(t)]), axis=1, keepdims=True)))

        peak = lax.fori_loop(0, n // 128, highest, jnp.float32(0.0))

        def begin(t, carry):
            xf_ref[rows_of(t)] = eye(t, 128) / peak
            return carry

        lax.fori_loop(0, n // 128, begin, 0)

        def newton(state):
            k, _ = state

            def residual(t, acc):
                rows = rows_of(t)
                new = eye(t, 128) - dot_full(xf_ref[rows], k_ref[...])
                rf_ref[rows] = new
                return acc + jnp.sum(new * new)

            size = lax.fori_loop(0, n // 128, residual, jnp.float32(0.0))
            for t in range(n // 128):
                r_t = slice(t * 128, (t + 1) * 128)
                rf_ref[n + t * 128 : n + (t + 1) * 128] = xf_ref[r_t]

            def update(t, carry):
                rows = rows_of(t)
                xf_ref[rows] = xf_ref[rows] + dot_full(rf_ref[rows], rf_ref[n : 2 * n])
                return carry

            lax.fori_loop(0, n // 128, update, 0)
            return k + 1, size

        lax.while_loop(
            lambda s: (s[1] > 1e-5) & (s[0] < 80), newton, (jnp.int32(0), jnp.float32(1.0) * n)
        )

        def again(t, carry):
            rows = pl.ds(pl.multiple_of(t * mtile, mtile), mtile)
            u_ref[rows] = dot_full(v_ref[rows], xf_ref[...])
            return carry

        lax.fori_loop(0, m // mtile, again, 0)
        refine(True)
        refine(True)


def solve_scratch(n, m):
    return [
        pltpu.VMEM((n, n), F32),
        pltpu.VMEM((m, n), F32),
        pltpu.VMEM((m, n), F32),
        pltpu.VMEM((n, n), BF),
        pltpu.VMEM((2, n, n), BF),
        pltpu.VMEM((n, n), F32),
        pltpu.VMEM((2 * n, n), F32),
        pltpu.VMEM((n, n), BF),
        pltpu.VMEM((n, n), BF),
    ]


def column(row):
    eye = iota((F, F), 0) == iota((F, F), 1)
    spread = jnp.where(eye, row.astype(F32), 0.0)
    return jnp.sum(spread, axis=1, keepdims=True).astype(jnp.int32)


def permute_cols(x, perm_row):
    hot = (iota((F, F), 0) == perm_row).astype(BF)
    return sum(dot(part, hot) for part in split(x, 3))


def from_second(rows):
    return (iota((rows, 1), 0) & 7) >= 4


def level_one_kernel(sc, kg, perm_row, x1, inv, y1, f1, k, v, u, x, r, xf, rf, kh, kl):
    natural(v, 0, kg, sc, N, 0, 256)
    symmetric(v)
    hot = (column(perm_row[...]) == iota((F, F), 1)).astype(BF)
    turned = sum(dot(hot, part) for part in split(v[...], 3))
    u[...] = permute_cols(turned, perm_row[...])
    natural(k, 0, kg, sc, 0, 0, 256)
    symmetric(k)
    k[...] = k[...] + u[...]
    row, cols, norm = scaled(k, F)
    v[...] = (iota((F, F), 0) == iota((F, F), 1)).astype(F32)
    solve_right(k, v, u, x, r, xf, rf, kh, kl, F, norm)
    for t in range(F // 128):
        rows = slice(t * 128, (t + 1) * 128)
        inv[rows] = u[rows] * cols[t] * row
    inverse = split(inv[...], 2)
    points = x1[...]
    points = jnp.where(from_second(8 * N), permute_cols(points, perm_row[...]), points)
    y1[...] = dot_three(split(points, 2), inverse)
    lane = iota((16, F), 1)
    sub = iota((16, F), 0)
    pick = ((lane == sub + sc[1] * N) & (sub < N)).astype(BF)
    f1[...] = sum(dot(pick, part) for part in split(inv[...], 3))


def level_two_kernel(sc, kg, perm_row, inv, x2, y1, f1, pv, wt, sf2, st):
    for b in range(2):
        natural(st, b * F, kg, sc, b * N, 0, F, False)
        natural(wt, b * F, kg, sc, b * N, F, 256, False)
        symmetric(wt, b * F)
    st[F:] = permute_cols(st[F:], perm_row[...])
    inverse = split(inv[...], 2)
    second = split(st[...], 2)
    for t in range(2):
        rows = slice(t * F, (t + 1) * F)
        other = slice((1 - t) * F, (2 - t) * F)
        base = wt[rows]
        w = dot_three([part[rows] for part in second], inverse)
        wt[rows] = w
        part = dot_three(split(w, 2), second, dot_t)
        pv[rows, rows] = base - part[:, rows]
        pv[rows, other] = -part[:, other]
    part = dot_three(split(y1[...], 2), second, dot_t)
    late = from_second(8 * N)
    n = 2 * F
    pv[n : n + 96, :F] = jnp.where(late, 0.0, x2[...]) - part[:, :F]
    pv[n : n + 96, F:] = jnp.where(late, x2[...], 0.0) - part[:, F:]
    sf2[...] = -dot_three(split(f1[...], 2), second, dot_t)


def couple_kernel(sc, pv, other, wt, y1, f1, perm_row, target, cc, k, v, u, x, r, xf, rf, kh, kl):
    n = 2 * F
    for t in range(6):
        rows = slice(t * 128, (t + 1) * 128)
        k[rows] = pv[rows] + other[rows]
    row, _, norm = scaled(k, n)
    lane = iota((16, n), 1)
    sub = iota((16, n), 0)
    for h, source in enumerate((pv, other)):
        half = sc[0] if h == 0 else 1 - sc[0]
        pick = ((lane == half * F + sc[1] * N + sub) & (sub < N)).astype(F32)
        base = h * 128
        v[base : base + 96] = source[n : n + 96] * row
        v[base + 96 : base + 112] = pick * row
        v[base + 112 : base + 128] = jnp.zeros((16, n), F32)
    solve_right(k, v, u, x, r, xf, rf, kh, kl, n, norm)
    u2 = u[...] * row
    u[...] = -u2
    k[:256, :F] = dot_three(split(u2, 2), split(wt[...], 2))
    k[:96, :F] = k[:96, :F] - y1[...]
    k[108:120, :F] = k[108:120, :F] - f1[:N]
    lanes = target[:1] + PLANE * N * ((target[1:] + sc[4]) & 1)
    for b in range(2):
        keys = iota((n, 1), 0)
        if b == 1:
            keys = jnp.concatenate([column(perm_row[...]), keys[F:]], axis=0)
        hot = (keys == lanes).astype(BF)
        coef = jnp.concatenate([k[:256, :F], u[:, b * F : (b + 1) * F]], axis=1)
        high, low = split(coef, 2)
        cc[b] = dot(jnp.concatenate([high, low], axis=0), hot).astype(BF)


WIDE = 768


def product_kernel(cc, g, dl, own, part):
    block = g[...].reshape(2 * F, WIDE)
    high, low = split(block, 2)
    both = dot(cc[0], high)
    acc = both[:256] + (both[256:] + dot(cc[0, :256], low))
    own[:96] = acc[:96] + dl[...]
    own[96:] = acc[96:128]
    part[...] = acc[128:240]


def product(b, cc, g, dl):
    steps = 4 * F // WIDE
    return pl.pallas_call(
        product_kernel,
        grid=(steps,),
        in_specs=[
            pl.BlockSpec((1, 512, 2 * F), lambda j: (b, 0, 0)),
            pl.BlockSpec((ROWS, 2 * N, WIDE), lambda j: (0, 0, b * steps + j)),
            pl.BlockSpec((8 * N, WIDE), lambda j: (0, b * steps + j)),
        ],
        out_specs=[
            pl.BlockSpec((128, WIDE), lambda j: (0, j)),
            pl.BlockSpec((112, WIDE), lambda j: (0, j)),
        ],
        out_shape=[
            jax.ShapeDtypeStruct((128, 4 * F), F32),
            jax.ShapeDtypeStruct((112, 4 * F), F32),
        ],
        compiler_params=LIMIT,
        cost_estimate=pl.CostEstimate(flops=4 * 10**9, bytes_accessed=10**7, transcendentals=0),
    )(cc, g, dl)


def finish_kernel(sc, own_a, own_b, other_a, other_b, sf2, sf, ss, mm):
    wide = 4 * F
    for h in range(2):
        @pl.when(sc[0] == h)
        def _():
            for b, (own, other) in enumerate(((own_a, other_a), (own_b, other_b))):
                near = slice((2 * h + b) * wide, (2 * h + b + 1) * wide)
                far = slice((2 - 2 * h + b) * wide, (3 - 2 * h + b) * wide)
                for i in range(N):
                    mm[i, :, near] = own[8 * i : 8 * i + 8]
                    mm[i, :, far] = other[8 * i : 8 * i + 8]
                    ss[i, :, near] = own[96 + i : 97 + i]
                    ss[i, :, far] = other[96 + i : 97 + i]
                    row = own[108 + i : 109 + i]
                    at = 5 * b * F
                    sf[i, :, at : at + F] = row[:, :F]
                    outer, inner = (at + F, at + 2 * F) if h == 0 else (at + 2 * F, at + F)
                    sf[i, :, outer : outer + F] = row[:, F : 2 * F]
                    sf[i, :, inner : inner + F] = sf2[i : i + 1, b * F : (b + 1) * F]
                    sf[i, :, at + 3 * F : at + 5 * F] = row[:, 2 * F :]


PLANE_AXES = ("y", "x")


def swap(x, axis):
    return lax.ppermute(x, axis, [(0, 1), (1, 0)])


def around(x, axis):
    return jnp.stack(
        [x] + [lax.ppermute(x, axis, [(i, (i + k) % 4) for i in range(4)]) for k in (1, 3, 2)]
    )


def body(dtn, interface_perm):
    half = lax.axis_index("core")
    spots = [lax.axis_index(name) for name in ("z_hi", "y", "x")]
    row = (spots[0] * 4 + spots[1]) * 4 + spots[2]
    sc = jnp.stack([half, row] + spots[1:] + spots[:1]).astype(jnp.int32)
    perm_row = interface_perm
    local = dtn.transpose(1, 2, 0, 3)
    (ks,) = pack_first(sc, local)
    x1, x2, dl = pack(sc, local)
    across = swap(ks, "z_hi")
    begin = F + 512

    def planes(left, right):
        return jnp.stack([ks[:, left:right], across[:, left:right]])

    g = lax.all_gather(planes(begin, begin + 8 * F), PLANE_AXES).reshape(ROWS, 2 * N, 8 * F)
    k1g = around(around(planes(F + 256, begin), "x"), "y")
    k2g = around(around(planes(0, F + 256), "y"), "x")
    inv, y1, f1 = level_one(sc, k1g, perm_row, x1)
    pv, wt, sf2 = level_two(sc, k2g, perm_row, inv, x2, y1, f1)
    paired = swap(pv, "core")
    (cc,) = couple(sc, pv, paired, wt, y1, f1, perm_row)
    own_a, part_a = product(0, cc, g, dl)
    arrived_a = swap(part_a, "core")
    own_b, part_b = product(1, cc, g, dl)
    arrived_b = swap(part_b, "core")
    sf, ss, mm = finish(sc, own_a, own_b, arrived_a, arrived_b, sf2)
    return sf.transpose(1, 0, 2), ss.transpose(1, 0, 2), mm[None].transpose(0, 2, 1, 3)


def pack_first(*operands):
    return call(pack_first_kernel, [((2 * N, 9 * F + 512), F32)], operands, smem=(0,))


def pack(*operands):
    return call(
        pack_kernel,
        [
            ((8 * N, F), F32),
            ((8 * N, F), F32),
            ((8 * N, 8 * F), F32),
        ],
        operands,
        smem=(0,),
    )


def level_one(*operands):
    return call(
        level_one_kernel,
        [((F, F), F32), ((8 * N, F), F32), ((16, F), F32)],
        operands,
        smem=(0,),
        scratch=solve_scratch(F, F),
        flops=10 * 10**9,
    )


def level_two(*operands):
    return call(
        level_two_kernel,
        [((864, 2 * F), F32), ((2 * F, F), F32), ((16, 2 * F), F32)],
        operands,
        smem=(0,),
        scratch=[pltpu.VMEM((2 * F, F), F32)],
        flops=5 * 10**9,
    )


def couple(*operands):
    shape = (PLANE, 2, 2, N)
    rows = np.arange(PLANE * N).reshape(PLANE, 1, 1, N) + F * np.arange(2).reshape(1, 1, 2, 1)
    turn = np.arange(2).reshape(1, 2, 1, 1)
    target = np.stack([np.broadcast_to(t, shape).reshape(-1) for t in (rows, turn)])
    return call(
        couple_kernel,
        [((2, 512, 2 * F), BF)],
        operands + (jnp.asarray(target, jnp.int32),),
        smem=(0,),
        scratch=solve_scratch(2 * F, 256),
        flops=20 * 10**9,
    )


def finish(*operands):
    return call(
        finish_kernel,
        [((N, 1, 10 * F), F32), ((N, 1, 16 * F), F32), ((N, 8, 16 * F), F32)],
        operands,
        smem=(0,),
    )


def solution(mesh):
    split_mesh = jax.sharding.Mesh(
        mesh.devices.reshape(-1, 2, 2, 4, 4), ("z_lo", "core", "z_hi", "y", "x")
    )
    pair, rows = ("z_lo", "core"), ("z_hi", "y", "x")
    return jax.shard_map(
        body,
        mesh=split_mesh,
        in_specs=(P(pair, None, rows, None), P(pair, None)),
        out_specs=(P(pair, rows, None), P(pair, rows, None), P(pair, None, rows, None)),
        check_vma=False,
    )
```

```python
import functools

import jax
import jax.numpy as jnp
import numpy as np
from jax import lax
from jax.experimental import pallas as pl
from jax.experimental.pallas import tpu as pltpu
from jax.sharding import PartitionSpec as P

F = 384
N = 12
ROWS = 32
PLANE = 16
BF = jnp.bfloat16
F32 = jnp.float32
LIMIT = pltpu.CompilerParams(vmem_limit_bytes=56 * 1024 * 1024)
VMEM = pl.BlockSpec(memory_space=pltpu.VMEM)
SMEM = pl.BlockSpec(memory_space=pltpu.SMEM)


def call(kernel, outs, operands, smem=(), scratch=(), flops=10**9):
    return pl.pallas_call(
        kernel,
        out_shape=[jax.ShapeDtypeStruct(s, d) for s, d in outs],
        in_specs=[SMEM if i in smem else VMEM for i in range(len(operands))],
        out_specs=[VMEM] * len(outs),
        scratch_shapes=list(scratch),
        compiler_params=LIMIT,
        cost_estimate=pl.CostEstimate(flops=flops, bytes_accessed=10**6, transcendentals=0),
    )(*operands)


def dot(a, b):
    return jnp.dot(a, b, preferred_element_type=F32)


def dot_full(a, b):
    return jnp.dot(a, b, preferred_element_type=F32, precision=lax.Precision.HIGHEST)


def dot_t(a, b):
    return lax.dot_general(a, b, (((1,), (1,)), ((), ())), preferred_element_type=F32)


def dot_three(a, b, kernel=dot):
    (ah, al), (bh, bl) = a, b
    m = ah.shape[0]
    both = kernel(jnp.concatenate([ah, al], axis=0), bh)
    return both[:m] + (both[m:] + kernel(ah, bl))


def split(x, parts):
    out = []
    for _ in range(parts):
        top = x.astype(BF)
        out.append(top)
        x = x - top.astype(F32)
    return out


def iota(shape, dim):
    return lax.broadcasted_iota(jnp.int32, shape, dim)


def chosen(even, face, rows):
    low, high = (rows[:, k * F : (k + 1) * F] for k in face)
    return jnp.where(even, high, low), jnp.where(even, low, high)


def others(even, b, rows):
    mid = chosen(even, (2, 3), rows)[1]
    return jnp.concatenate([rows[:, b * F : (b + 1) * F], mid, rows[:, 4 * F :]], axis=1)


def pack_first_kernel(dtn, ks):
    even = lax.axis_index("core") == 0
    spot = (lax.axis_index("z_hi") * 4 + lax.axis_index("y")) * 4 + lax.axis_index("x")

    def two_thirds(row, at):
        x, y, z = (row[:, k * 128 : (k + 1) * 128] for k in range(3))
        early, late = at < 128, at >= 256
        first = jnp.where(early, x, jnp.where(late, z, y))
        then = jnp.where(early, y, jnp.where(late, x, z))
        return jnp.concatenate([first, then], axis=1)

    begin = F + 512
    for i in range(N):
        point = spot * N + i
        for b in range(2):
            i1 = 1 - b
            cols = slice(i1 * F, (i1 + 1) * F)
            row_one = dtn[i1, i, b : b + 1]
            row_two = jnp.where(even, dtn[3, i, b : b + 1], dtn[2, i, b : b + 1])
            for k, row in enumerate((row_one, row_two)):
                at, left = k * N + i, begin + 4 * b * F
                ks[at : at + 1, left : left + 4 * F] = others(even, b, row)
            at = b * N + i
            ks[at : at + 1, :F] = row_two[:, cols]
            ks[at : at + 1, F : F + 256] = two_thirds(chosen(even, (2, 3), row_two)[0], point)
            ks[at : at + 1, F + 256 : begin] = two_thirds(row_one[:, cols], point)


def pack_kernel(sc, dtn, x1, x2, dl):
    even = sc[0] == 0
    empty = jnp.zeros((4, 4 * F), F32)
    for i in range(N):
        one, two, block = [], [], []
        for b in range(2):
            i1 = 1 - b

            face = [dtn[f, i, b : b + 1] for f in range(6)]
            middle = jnp.where(even, face[2], face[3])
            outer = jnp.concatenate([face[b], middle, face[4], face[5]], axis=0)
            one.append(outer[:, i1 * F : (i1 + 1) * F])
            two.append(chosen(even, (2, 3), outer)[0])
            block.append(others(even, b, outer))
        rows = slice(8 * i, 8 * i + 8)
        x1[rows] = jnp.concatenate(one, axis=0)
        x2[rows] = jnp.concatenate(two, axis=0)
        dl[rows, : 4 * F] = jnp.concatenate([block[0], empty], axis=0)
        dl[rows, 4 * F :] = jnp.concatenate([empty, block[1]], axis=0)


def place(distance):
    return jnp.where(distance == 0, 0, jnp.where(distance == 3, 1, distance + 1))


def natural(dst, base, src, sc, offset, col=0, width=F, y_first=True):
    ys = [place((y + 4 - sc[2]) & 3) for y in range(4)]
    xs = [place((x + 4 - sc[3]) & 3) for x in range(4)]
    for z in range(2):
        for q in range(PLANE):
            at = base + (z * PLANE + q) * N
            y, x = ys[q // 4], xs[q % 4]
            first, then = (y, x) if y_first else (x, y)
            dst[at : at + N, :width] = src[first, then, (z + sc[4]) & 1, offset : offset + N, col : col + width]


def complete(ref, base):
    for a in range(3):
        b, c = (a + 1) % 3, (a + 2) % 3
        rows = slice(base + a * 128, base + (a + 1) * 128)
        own = ref[rows, :128]
        yield rows, a, own, b, ref[rows, 128:256], c, ref[base + c * 128 : base + (c + 1) * 128, 128:256].T


def symmetric(ref, base=0):
    parts = list(complete(ref, base))
    for rows, *pieces in parts:
        for at, block in zip(pieces[::2], pieces[1::2]):
            ref[rows, at * 128 : (at + 1) * 128] = block


def scaled(k_ref, n):
    eye = iota((128, 128), 0) == iota((128, 128), 1)
    row, cols = [], []
    for t in range(n // 128):
        rows = slice(t * 128, (t + 1) * 128)
        diag = jnp.where(eye, k_ref[rows, rows], 0.0)
        row.append(jnp.sum(diag, axis=0, keepdims=True))
        cols.append(lax.rsqrt(jnp.sum(diag, axis=1, keepdims=True)))
    row = lax.rsqrt(jnp.concatenate(row, axis=1))
    norm = jnp.zeros((8, n), F32)
    for t in range(n // 128):
        rows = slice(t * 128, (t + 1) * 128)
        part = k_ref[rows] * cols[t] * row
        k_ref[rows] = part
        norm = norm + jnp.sum((part * part).reshape(16, 8, n), axis=0)
    return row, cols, jnp.sum(norm)


TILE = 384
MTILE = 384


def solve_right(k_ref, v_ref, u_ref, x_ref, r_ref, xf_ref, rf_ref, kh_ref, kl_ref, n, norm):
    tile = TILE
    count = n // tile
    m = v_ref.shape[0]
    mtile = min(m, MTILE)
    alpha = n / norm

    def eye(t, width):
        return (iota((width, n), 0) + t * width == iota((width, n), 1)).astype(F32)

    for t in range(count):
        rows = slice(t * tile, (t + 1) * tile)
        e = eye(t, tile)
        part = k_ref[rows]
        kh_ref[rows], kl_ref[rows] = split(part, 2)
        first = e - alpha * part
        r_ref[0, rows] = first.astype(BF)
        x_ref[rows] = (alpha * (e + first)).astype(BF)

    def square(src, dst, with_x):
        def step(t, acc):
            rows = pl.ds(pl.multiple_of(t * tile, tile), tile)
            left = r_ref[src, rows]
            if with_x:
                old = x_ref[rows]
                both = dot(jnp.concatenate([left, old], axis=0), r_ref[src])
                new = both[:tile]
                x_ref[rows] = (old.astype(F32) + both[tile:]).astype(BF)
            else:
                new = dot(left, r_ref[src])
            r_ref[dst, rows] = new.astype(BF)
            return acc + jnp.sum(new * new)

        return lax.fori_loop(0, count, step, jnp.float32(0.0))

    def advance(src):
        def step(t, carry):
            rows = pl.ds(pl.multiple_of(t * tile, tile), tile)
            old = x_ref[rows]
            x_ref[rows] = (old.astype(F32) + dot(old, r_ref[src])).astype(BF)
            return carry

        lax.fori_loop(0, count, step, 0)

    size = square(0, 1, False)

    def more(state):
        k, size = state
        return (size > 0.003 * n) & (k < 12)

    def iterate(state):
        k, _ = state
        src = (k + 1) % 2
        return k + 1, square(src, k % 2, True)

    k, _ = lax.while_loop(more, iterate, (jnp.int32(0), size))
    advance((k + 1) % 2)

    def start(t, acc):
        rows = pl.ds(pl.multiple_of(t * mtile, mtile), mtile)
        v = v_ref[rows]
        u_ref[rows] = dot(v.astype(BF), x_ref[...])
        return acc + jnp.sum(v * v)

    scale = lax.fori_loop(0, m // mtile, start, jnp.float32(0.0))

    def refine(full):
        def step(t, acc):
            rows = pl.ds(pl.multiple_of(t * mtile, mtile), mtile)
            u = u_ref[rows]
            if full:
                left = v_ref[rows] - dot_full(u, k_ref[...])
                u_ref[rows] = u + dot_full(left, xf_ref[...])
            else:
                left = v_ref[rows] - dot_three(split(u, 2), (kh_ref[...], kl_ref[...]))
                u_ref[rows] = u + dot(left.astype(BF), x_ref[...])
            return acc + jnp.sum(left * left)

        return lax.fori_loop(0, m // mtile, step, jnp.float32(0.0))

    def unfinished(state):
        k, left = state
        return (left > 1e-7 * scale) & (left < 0.1 * scale) & (k < 12)

    done, left = lax.while_loop(
        unfinished, lambda s: (s[0] + 1, refine(False)), (jnp.int32(1), refine(False))
    )

    @pl.when(jnp.logical_not(left <= 1e-7 * scale))
    def _():
        def rows_of(t):
            return pl.ds(pl.multiple_of(t * 128, 128), 128)

        def highest(t, acc):
            return jnp.maximum(acc, jnp.max(jnp.sum(jnp.abs(k_ref[rows_of(t)]), axis=1, keepdims=True)))

        peak = lax.fori_loop(0, n // 128, highest, jnp.float32(0.0))

        def begin(t, carry):
            xf_ref[rows_of(t)] = eye(t, 128) / peak
            return carry

        lax.fori_loop(0, n // 128, begin, 0)

        def newton(state):
            k, _ = state

            def residual(t, acc):
                rows = rows_of(t)
                new = eye(t, 128) - dot_full(xf_ref[rows], k_ref[...])
                rf_ref[rows] = new
                return acc + jnp.sum(new * new)

            size = lax.fori_loop(0, n // 128, residual, jnp.float32(0.0))
            for t in range(n // 128):
                r_t = slice(t * 128, (t + 1) * 128)
                rf_ref[n + t * 128 : n + (t + 1) * 128] = xf_ref[r_t]

            def update(t, carry):
                rows = rows_of(t)
                xf_ref[rows] = xf_ref[rows] + dot_full(rf_ref[rows], rf_ref[n : 2 * n])
                return carry

            lax.fori_loop(0, n // 128, update, 0)
            return k + 1, size

        lax.while_loop(
            lambda s: (s[1] > 1e-5) & (s[0] < 80), newton, (jnp.int32(0), jnp.float32(1.0) * n)
        )

        def again(t, carry):
            rows = pl.ds(pl.multiple_of(t * mtile, mtile), mtile)
            u_ref[rows] = dot_full(v_ref[rows], xf_ref[...])
            return carry

        lax.fori_loop(0, m // mtile, again, 0)
        refine(True)
        refine(True)


def solve_scratch(n, m):
    return [
        pltpu.VMEM((n, n), F32),
        pltpu.VMEM((m, n), F32),
        pltpu.VMEM((m, n), F32),
        pltpu.VMEM((n, n), BF),
        pltpu.VMEM((2, n, n), BF),
        pltpu.VMEM((n, n), F32),
        pltpu.VMEM((2 * n, n), F32),
        pltpu.VMEM((n, n), BF),
        pltpu.VMEM((n, n), BF),
    ]


def column(row):
    eye = iota((F, F), 0) == iota((F, F), 1)
    spread = jnp.where(eye, row.astype(F32), 0.0)
    return jnp.sum(spread, axis=1, keepdims=True).astype(jnp.int32)


def permute_cols(x, perm_row):
    hot = (iota((F, F), 0) == perm_row).astype(BF)
    return sum(dot(part, hot) for part in split(x, 3))


def from_second(rows):
    return (iota((rows, 1), 0) & 7) >= 4


def level_one_kernel(sc, kg, perm_row, x1, inv, y1, f1, k, v, u, x, r, xf, rf, kh, kl):
    natural(v, 0, kg, sc, N, 0, 256)
    symmetric(v)
    hot = (column(perm_row[...]) == iota((F, F), 1)).astype(BF)
    turned = sum(dot(hot, part) for part in split(v[...], 3))
    u[...] = permute_cols(turned, perm_row[...])
    natural(k, 0, kg, sc, 0, 0, 256)
    symmetric(k)
    k[...] = k[...] + u[...]
    row, cols, norm = scaled(k, F)
    v[...] = (iota((F, F), 0) == iota((F, F), 1)).astype(F32)
    solve_right(k, v, u, x, r, xf, rf, kh, kl, F, norm)
    for t in range(F // 128):
        rows = slice(t * 128, (t + 1) * 128)
        inv[rows] = u[rows] * cols[t] * row
    inverse = split(inv[...], 2)
    points = x1[...]
    points = jnp.where(from_second(8 * N), permute_cols(points, perm_row[...]), points)
    y1[...] = dot_three(split(points, 2), inverse)
    lane = iota((16, F), 1)
    sub = iota((16, F), 0)
    pick = ((lane == sub + sc[1] * N) & (sub < N)).astype(BF)
    f1[...] = sum(dot(pick, part) for part in split(inv[...], 3))


def level_two_kernel(sc, kg, perm_row, inv, x2, y1, f1, pv, wt, sf2, st):
    for b in range(2):
        natural(st, b * F, kg, sc, b * N, 0, F, False)
        natural(wt, b * F, kg, sc, b * N, F, 256, False)
        symmetric(wt, b * F)
    st[F:] = permute_cols(st[F:], perm_row[...])
    inverse = split(inv[...], 2)
    second = split(st[...], 2)
    for t in range(2):
        rows = slice(t * F, (t + 1) * F)
        other = slice((1 - t) * F, (2 - t) * F)
        base = wt[rows]
        w = dot_three([part[rows] for part in second], inverse)
        wt[rows] = w
        part = dot_three(split(w, 2), second, dot_t)
        pv[rows, rows] = base - part[:, rows]
        pv[rows, other] = -part[:, other]
    part = dot_three(split(y1[...], 2), second, dot_t)
    late = from_second(8 * N)
    n = 2 * F
    pv[n : n + 96, :F] = jnp.where(late, 0.0, x2[...]) - part[:, :F]
    pv[n : n + 96, F:] = jnp.where(late, x2[...], 0.0) - part[:, F:]
    sf2[...] = -dot_three(split(f1[...], 2), second, dot_t)


def couple_kernel(sc, pv, other, wt, y1, f1, perm_row, target, cc, k, v, u, x, r, xf, rf, kh, kl):
    n = 2 * F
    for t in range(6):
        rows = slice(t * 128, (t + 1) * 128)
        k[rows] = pv[rows] + other[rows]
    row, _, norm = scaled(k, n)
    lane = iota((16, n), 1)
    sub = iota((16, n), 0)
    for h, source in enumerate((pv, other)):
        half = sc[0] if h == 0 else 1 - sc[0]
        pick = ((lane == half * F + sc[1] * N + sub) & (sub < N)).astype(F32)
        base = h * 128
        v[base : base + 96] = source[n : n + 96] * row
        v[base + 96 : base + 112] = pick * row
        v[base + 112 : base + 128] = jnp.zeros((16, n), F32)
    solve_right(k, v, u, x, r, xf, rf, kh, kl, n, norm)
    u2 = u[...] * row
    u[...] = -u2
    k[:256, :F] = dot_three(split(u2, 2), split(wt[...], 2))
    k[:96, :F] = k[:96, :F] - y1[...]
    k[108:120, :F] = k[108:120, :F] - f1[:N]
    lanes = target[:1] + PLANE * N * ((target[1:] + sc[4]) & 1)
    for b in range(2):
        keys = iota((n, 1), 0)
        if b == 1:
            keys = jnp.concatenate([column(perm_row[...]), keys[F:]], axis=0)
        hot = (keys == lanes).astype(BF)
        coef = jnp.concatenate([k[:256, :F], u[:, b * F : (b + 1) * F]], axis=1)
        high, low = split(coef, 2)
        cc[b] = dot(jnp.concatenate([high, low], axis=0), hot).astype(BF)


WIDE = 768


def product_kernel(cc, g, dl, own, part):
    block = g[...].reshape(2 * F, WIDE)
    high, low = split(block, 2)
    both = dot(cc[0], high)
    acc = both[:256] + (both[256:] + dot(cc[0, :256], low))
    own[:96] = acc[:96] + dl[...]
    own[96:] = acc[96:128]
    part[...] = acc[128:240]


def product(b, cc, g, dl):
    steps = 4 * F // WIDE
    return pl.pallas_call(
        product_kernel,
        grid=(steps,),
        in_specs=[
            pl.BlockSpec((1, 512, 2 * F), lambda j: (b, 0, 0)),
            pl.BlockSpec((ROWS, 2 * N, WIDE), lambda j: (0, 0, b * steps + j)),
            pl.BlockSpec((8 * N, WIDE), lambda j: (0, b * steps + j)),
        ],
        out_specs=[
            pl.BlockSpec((128, WIDE), lambda j: (0, j)),
            pl.BlockSpec((112, WIDE), lambda j: (0, j)),
        ],
        out_shape=[
            jax.ShapeDtypeStruct((128, 4 * F), F32),
            jax.ShapeDtypeStruct((112, 4 * F), F32),
        ],
        compiler_params=LIMIT,
        cost_estimate=pl.CostEstimate(flops=4 * 10**9, bytes_accessed=10**7, transcendentals=0),
    )(cc, g, dl)


def finish_kernel(sc, own_a, own_b, other_a, other_b, sf2, sf, ss, mm):
    wide = 4 * F
    for h in range(2):
        @pl.when(sc[0] == h)
        def _():
            for b, (own, other) in enumerate(((own_a, other_a), (own_b, other_b))):
                near = slice((2 * h + b) * wide, (2 * h + b + 1) * wide)
                far = slice((2 - 2 * h + b) * wide, (3 - 2 * h + b) * wide)
                for i in range(N):
                    mm[i, :, near] = own[8 * i : 8 * i + 8]
                    mm[i, :, far] = other[8 * i : 8 * i + 8]
                    ss[i, :, near] = own[96 + i : 97 + i]
                    ss[i, :, far] = other[96 + i : 97 + i]
                    row = own[108 + i : 109 + i]
                    at = 5 * b * F
                    sf[i, :, at : at + F] = row[:, :F]
                    outer, inner = (at + F, at + 2 * F) if h == 0 else (at + 2 * F, at + F)
                    sf[i, :, outer : outer + F] = row[:, F : 2 * F]
                    sf[i, :, inner : inner + F] = sf2[i : i + 1, b * F : (b + 1) * F]
                    sf[i, :, at + 3 * F : at + 5 * F] = row[:, 2 * F :]


PLANE_AXES = ("y", "x")


def swap(x, axis):
    return lax.ppermute(x, axis, [(0, 1), (1, 0)])


def around(x, axis):
    return jnp.stack(
        [x] + [lax.ppermute(x, axis, [(i, (i + k) % 4) for i in range(4)]) for k in (1, 3, 2)]
    )


def body(dtn, interface_perm):
    half = lax.axis_index("core")
    spots = [lax.axis_index(name) for name in ("z_hi", "y", "x")]
    row = (spots[0] * 4 + spots[1]) * 4 + spots[2]
    sc = jnp.stack([half, row] + spots[1:] + spots[:1]).astype(jnp.int32)
    perm_row = interface_perm
    local = dtn.transpose(1, 2, 0, 3)
    ks = pack_first(local)
    x1, x2, dl = pack(sc, local)
    across = swap(ks, "z_hi")
    begin = F + 512

    def planes(left, right):
        return jnp.stack([ks[:, left:right], across[:, left:right]])

    g = lax.all_gather(planes(begin, begin + 8 * F), PLANE_AXES).reshape(ROWS, 2 * N, 8 * F)
    k1g = around(around(planes(F + 256, begin), "x"), "y")
    k2g = around(around(planes(0, F + 256), "y"), "x")
    inv, y1, f1 = level_one(sc, k1g, perm_row, x1)
    pv, wt, sf2 = level_two(sc, k2g, perm_row, inv, x2, y1, f1)
    paired = swap(pv, "core")
    (cc,) = couple(sc, pv, paired, wt, y1, f1, perm_row)
    own_a, part_a = product(0, cc, g, dl)
    arrived_a = swap(part_a, "core")
    own_b, part_b = product(1, cc, g, dl)
    arrived_b = swap(part_b, "core")
    sf, ss, mm = finish(sc, own_a, own_b, arrived_a, arrived_b, sf2)
    return sf.transpose(1, 0, 2), ss.transpose(1, 0, 2), mm[None].transpose(0, 2, 1, 3)


def pack_first(local):
    return pl.pallas_call(
        pack_first_kernel,
        grid=(1,),
        in_specs=[pl.BlockSpec((4, N, 2, 6 * F), lambda i: (0, 0, 0, 0))],
        out_specs=pl.BlockSpec((2 * N, 9 * F + 512), lambda i: (0, 0)),
        out_shape=jax.ShapeDtypeStruct((2 * N, 9 * F + 512), F32),
        compiler_params=LIMIT,
        cost_estimate=pl.CostEstimate(flops=10**9, bytes_accessed=10**6, transcendentals=0),
    )(local)


def pack(*operands):
    return call(
        pack_kernel,
        [
            ((8 * N, F), F32),
            ((8 * N, F), F32),
            ((8 * N, 8 * F), F32),
        ],
        operands,
        smem=(0,),
    )


def level_one(*operands):
    return call(
        level_one_kernel,
        [((F, F), F32), ((8 * N, F), F32), ((16, F), F32)],
        operands,
        smem=(0,),
        scratch=solve_scratch(F, F),
        flops=10 * 10**9,
    )


def level_two(*operands):
    return call(
        level_two_kernel,
        [((864, 2 * F), F32), ((2 * F, F), F32), ((16, 2 * F), F32)],
        operands,
        smem=(0,),
        scratch=[pltpu.VMEM((2 * F, F), F32)],
        flops=5 * 10**9,
    )


def couple(*operands):
    shape = (PLANE, 2, 2, N)
    rows = np.arange(PLANE * N).reshape(PLANE, 1, 1, N) + F * np.arange(2).reshape(1, 1, 2, 1)
    turn = np.arange(2).reshape(1, 2, 1, 1)
    target = np.stack([np.broadcast_to(t, shape).reshape(-1) for t in (rows, turn)])
    return call(
        couple_kernel,
        [((2, 512, 2 * F), BF)],
        operands + (jnp.asarray(target, jnp.int32),),
        smem=(0,),
        scratch=solve_scratch(2 * F, 256),
        flops=20 * 10**9,
    )


def finish(*operands):
    return call(
        finish_kernel,
        [((N, 1, 10 * F), F32), ((N, 1, 16 * F), F32), ((N, 8, 16 * F), F32)],
        operands,
        smem=(0,),
    )


def solution(mesh):
    split_mesh = jax.sharding.Mesh(
        mesh.devices.reshape(-1, 2, 2, 4, 4), ("z_lo", "core", "z_hi", "y", "x")
    )
    pair, rows = ("z_lo", "core"), ("z_hi", "y", "x")
    return jax.shard_map(
        body,
        mesh=split_mesh,
        in_specs=(P(pair, None, rows, None), P(pair, None)),
        out_specs=(P(pair, rows, None), P(pair, rows, None), P(pair, None, rows, None)),
        check_vma=False,
    )
```
